32 devices in a mesh: tm: 16 (over z, y, core), items: 2 (over x).
Axes of the slice: x: 2, y: 2, z: 4, core: 2. Of those that a mesh axis runs over, the one named last changes fastest.
Arguments:
- frames: bfloat16 [2, 16384, 512], P('items', 'tm'), may hold values from -6 to 6
- out_grad: bfloat16 [2, 16384, 512], P('items', 'tm'), may hold values from -6 to 6
- item_lengths: int32 [2, 111], P('items'), may hold values from 0 to 1600, as said below
- domain_tags: int32 [2, 111], P('items'), may hold values from 0 to 3, as said below
- domain_weight: float32 [3], replicated, may hold values from 0.5 to 2
- query_weight: bfloat16 [512, 512], replicated, may hold values from -0.375 to 0.375
- query_bias: float32 [512], replicated, may hold values from -1.8 to 1.8
- key_weight: bfloat16 [512, 512], replicated, may hold values from -0.25 to 0.25
- value_weight: bfloat16 [512, 512], replicated, may hold values from -0.25 to 0.25
- value_bias: float32 [512], replicated, may hold values from -1.8 to 1.8
- mix_weight: bfloat16 [512, 512], replicated, may hold values from -0.5 to 0.5
- mix_bias: float32 [512], replicated, may hold values from -1.8 to 1.8
- attn_gain: float32 [512], replicated, may hold values from 0.25 to 1.75
- attn_shift: float32 [512], replicated, may hold values from -1.8 to 1.8
- feed_gain: float32 [512], replicated, may hold values from 0.25 to 1.75
- feed_shift: float32 [512], replicated, may hold values from -1.8 to 1.8
- up_weight: bfloat16 [512, 2048], replicated, may hold values from -0.25 to 0.25
- up_bias: float32 [2048], replicated, may hold values from -1.8 to 1.8
- down_weight: bfloat16 [2048, 512], replicated, may hold values from -0.125 to 0.125
- down_bias: float32 [512], replicated, may hold values from -1.8 to 1.8
Outputs:
- output: bfloat16 [2, 16384, 512], P('items', 'tm')
- input_grad: bfloat16 [2, 16384, 512], P('items', 'tm')
- grad_query_weight: float32 [512, 512], replicated
- grad_query_bias: float32 [512], replicated
- grad_key_weight: float32 [512, 512], replicated
- grad_value_weight: float32 [512, 512], replicated
- grad_value_bias: float32 [512], replicated
- grad_mix_weight: float32 [512, 512], replicated
- grad_mix_bias: float32 [512], replicated
- grad_attn_gain: float32 [512], replicated
- grad_attn_shift: float32 [512], replicated
- grad_feed_gain: float32 [512], replicated
- grad_feed_shift: float32 [512], replicated
- grad_up_weight: float32 [512, 2048], replicated
- grad_up_bias: float32 [2048], replicated
- grad_down_weight: float32 [2048, 512], replicated
- grad_down_bias: float32 [512], replicated
The draws below stay inside these ranges and needn't reach their ends.
Inputs may be any that keep to these rules, and one draw needn't show every extreme that they name: `item_lengths`: each stream's slots lie end to end from its first frame in slot order and fill it exactly. The first slot is an item of 1600 frames with tag 2 and the last slot is an item of 1600 frames with tag 2; the slot before the last is the padding slot (tag 3) of 0 to 1599 frames; the slots between hold items end to end, then slots of 0 frames. An item of tag 0 has 400 to 800 frames, of tag 1 3 * 50 to 300, and of tag 2 5 * 200 to 1600. `domain_tags`: the domain of the slot of the same index; slots of 0 frames hold tags as well.
All inputs are finite; a program needn't handle non-finite values.
Results may differ from the reference program's by a relative error of at most 0.014.
Values may be sent and summed in bfloat16 or wider, within the bound.
No kernel may reach another device: no remote copies, remote signals or barrier semaphores. Data moves between devices by JAX's collectives and lax.ppermute only.
A program may use at most 192 MiB of HBM per device.

```python
import math
import jax
import jax.numpy as jnp
from jax import lax

D = 512
HEADS = 8
FF = 2048
LEFT = 10
RIGHT = 2
ITEM_MAX = 1600
STREAMS = 2
LEN = 16384
SLOTS = 111


def items_draw(key):
    lows = jnp.array([ITEM_MAX // 4, 3 * ITEM_MAX // 32, 5 * ITEM_MAX // 8], dtype=jnp.int32)
    highs = jnp.array([ITEM_MAX // 2, 3 * ITEM_MAX // 16, ITEM_MAX], dtype=jnp.int32)
    limit = LEN - ITEM_MAX

    def one_stream(stream_key):

        def place(filled, slot):
            slot_key = jax.random.fold_in(stream_key, slot)
            kind_key, size_key = jax.random.split(slot_key)
            kind = jax.random.randint(kind_key, (), 0, 3, dtype=jnp.int32)
            kind = jnp.where(slot == 0, jnp.int32(2), kind)
            size = jax.random.randint(size_key, (), lows[kind], highs[kind] + 1, dtype=jnp.int32)
            size = jnp.where(slot == 0, jnp.int32(ITEM_MAX), size)
            fits = filled + size <= limit
            size = jnp.where(fits, size, jnp.int32(0))
            filled = jnp.where(fits, filled + size, jnp.int32(LEN + 1))
            return (filled, (size, kind))
        _, (sizes, kinds) = lax.scan(place, jnp.int32(0), jnp.arange(SLOTS - 2, dtype=jnp.int32))
        padding = limit - jnp.sum(sizes, dtype=jnp.int32)
        sizes = jnp.concatenate([sizes, jnp.stack([padding, jnp.int32(ITEM_MAX)])])
        kinds = jnp.concatenate([kinds, jnp.array([3, 2], dtype=jnp.int32)])
        return (sizes, kinds)
    return jax.vmap(one_stream)(jax.random.split(key, STREAMS))


def draw_item_lengths(key, part):
    sizes, kinds = items_draw(key)
    return sizes


def draw_domain_tags(key, part):
    sizes, kinds = items_draw(key)
    return kinds


def block_scale(key, extent, pieces, least, high):
    factor_of = 1.0
    for position, parts in pieces:
        steps = jax.random.uniform(jax.random.fold_in(jax.random.fold_in(key, 6), position), (parts,), jnp.float32, least / len(pieces), high / len(pieces))
        factor_of = factor_of * jnp.repeat(jnp.exp(steps), extent[position] // parts).reshape((-1,) + (1,) * (len(extent) - 1 - position))
    return factor_of


def normal_values(key, dims, width, reach, pieces=(), held_as=jnp.bfloat16):
    entries = jax.random.normal(key, dims, jnp.float32) * width
    if len(pieces) > 0:
        entries = block_scale(key, dims, pieces, -0.22, 0.18) * entries
    return jnp.clip(entries, min=-reach, max=reach).astype(held_as)


def setup_inputs(seed: int = 0) -> dict:
    key_of = jax.random.split(jax.random.key(seed), 21)
    return {
        "frames": normal_values(key_of[0], (STREAMS, LEN, D), 1.0, 6.0, ((0, 2), (1, 16))),
        "out_grad": normal_values(key_of[1], (STREAMS, LEN, D), 1.0, 6.0, ((0, 2), (1, 16))),
        "item_lengths": draw_item_lengths(jax.random.fold_in(key_of[20], 71), 0),
        "domain_tags": draw_domain_tags(jax.random.fold_in(key_of[20], 71), 0),
        "domain_weight": jnp.clip(jnp.exp(jax.random.uniform(key_of[4], (3,), jnp.float32, math.log(0.5), math.log(2.0))), 0.5, 2.0),
        "query_weight": normal_values(key_of[5], (D, D), (D // 2) ** -0.5, 0.375),
        "query_bias": normal_values(key_of[6], (D,), 0.3, 1.8, (), jnp.float32),
        "key_weight": normal_values(key_of[7], (D, D), D ** -0.5, 0.25),
        "value_weight": normal_values(key_of[8], (D, D), D ** -0.5, 0.25),
        "value_bias": normal_values(key_of[9], (D,), 0.3, 1.8, (), jnp.float32),
        "mix_weight": normal_values(key_of[10], (D, D), (D // 4) ** -0.5, 0.5),
        "mix_bias": normal_values(key_of[11], (D,), 0.3, 1.8, (), jnp.float32),
        "attn_gain": jnp.clip(1.0 + 0.15 * jax.random.normal(key_of[12], (D,), jnp.float32), 0.25, 1.75),
        "attn_shift": normal_values(key_of[13], (D,), 0.3, 1.8, (), jnp.float32),
        "feed_gain": jnp.clip(1.0 + 0.15 * jax.random.normal(key_of[14], (D,), jnp.float32), 0.25, 1.75),
        "feed_shift": normal_values(key_of[15], (D,), 0.3, 1.8, (), jnp.float32),
        "up_weight": normal_values(key_of[16], (D, FF), D ** -0.5, 0.25),
        "up_bias": normal_values(key_of[17], (FF,), 0.3, 1.8, (), jnp.float32),
        "down_weight": normal_values(key_of[18], (FF, D), FF ** -0.5, 0.125),
        "down_bias": normal_values(key_of[19], (D,), 0.3, 1.8, (), jnp.float32),
    }


@jax.custom_vjp
def low(v):
    return lax.optimization_barrier(v.astype(jnp.bfloat16)).astype(jnp.float32)

@jax.custom_vjp
def low_back(v):
    return v

def low_keep(v):
    return (low(v), None)

def low_pass(kept, grad):
    return (grad,)

def back_keep(v):
    return (v, None)

def back_low(kept, grad):
    return (low(grad),)
low.defvjp(low_keep, low_pass)
low_back.defvjp(back_keep, back_low)

def matmul(left, right):
    return jnp.dot(left, right, precision=lax.Precision.HIGHEST, preferred_element_type=jnp.float32)

def layer_norm(values, gain, shift):
    centered = values - lax.optimization_barrier(jnp.mean(values, axis=-1, keepdims=True))
    variance = lax.optimization_barrier(jnp.mean(centered * centered, axis=-1, keepdims=True))
    return centered * lax.rsqrt(variance + 1e-05) * gain + shift

def segment_ids(positions, lengths, stream_len):
    ends = jnp.cumsum(lengths, dtype=jnp.int32)
    below = (ends[None, :] <= positions[:, None]).astype(jnp.int32)
    segment = lax.optimization_barrier(jnp.sum(below, axis=1, dtype=jnp.int32))
    segment = jnp.where(positions < 0, jnp.int32(-1), segment)
    return jnp.where(positions >= stream_len, jnp.int32(-2), segment)

def row_weights(segment, tags, domain_weight):
    slots = jnp.arange(tags.shape[0], dtype=jnp.int32)
    kinds = jnp.arange(domain_weight.shape[0], dtype=jnp.int32)
    per_slot = lax.optimization_barrier(jnp.sum(jnp.where(tags[:, None] == kinds[None, :], domain_weight[None, :], 0.0), axis=1))
    return lax.optimization_barrier(jnp.sum(jnp.where(segment[:, None] == slots[None, :], per_slot[None, :], 0.0), axis=1))

def windows(extended, count):
    return jnp.stack([extended[offset:offset + count] for offset in range(LEFT + RIGHT + 1)], axis=1)

def attend(queries, keys_ext, values_ext, seg_rows, seg_ext):
    count = queries.shape[0]
    head_dim = D // HEADS
    query_heads = queries.reshape(count, HEADS, head_dim)
    key_win = windows(keys_ext, count).reshape(count, -1, HEADS, head_dim)
    value_win = windows(values_ext, count).reshape(count, -1, HEADS, head_dim)
    allowed = windows(seg_ext, count) == seg_rows[:, None]
    scores = jnp.einsum('rhd,rshd->rsh', query_heads, key_win, precision=lax.Precision.HIGHEST) * head_dim ** (-0.5)
    scores = jnp.where(allowed[:, :, None], scores, -1e+30)
    peak = lax.optimization_barrier(jnp.max(scores, axis=1, keepdims=True))
    weights = jnp.exp(scores - peak)
    probs = low(weights / lax.optimization_barrier(jnp.sum(weights, axis=1, keepdims=True)))
    mixed = jnp.einsum('rsh,rshd->rhd', probs, value_win, precision=lax.Precision.HIGHEST)
    return mixed.reshape(count, D)

def band_attention(queries, keys, values, segment, seg_ext):
    total = queries.shape[0]
    block = 512 if total % 512 == 0 else total
    keys_pad = jnp.pad(keys, ((LEFT, RIGHT), (0, 0)))
    values_pad = jnp.pad(values, ((LEFT, RIGHT), (0, 0)))
    span = block + LEFT + RIGHT

    def one_block(start):
        return attend(lax.dynamic_slice_in_dim(queries, start, block, 0), lax.dynamic_slice_in_dim(keys_pad, start, span, 0), lax.dynamic_slice_in_dim(values_pad, start, span, 0), lax.dynamic_slice_in_dim(segment, start, block, 0), lax.dynamic_slice_in_dim(seg_ext, start, span, 0))
    starts = jnp.arange(0, total, block, dtype=jnp.int32)
    return lax.map(jax.checkpoint(one_block), starts).reshape(total, D)

def forward(frames, params, segment, seg_ext):
    query_weight, query_bias, key_weight, value_weight, value_bias, mix_weight, mix_bias, attn_gain, attn_shift, feed_gain, feed_shift, up_weight, up_bias, down_weight, down_bias = params
    normed = low(layer_norm(frames, attn_gain, attn_shift))
    queries = low_back(low(matmul(normed, query_weight) + query_bias))
    keys = low_back(low(matmul(normed, key_weight)))
    values = low_back(low(matmul(normed, value_weight) + value_bias))
    mixed = low(band_attention(queries, keys, values, segment, seg_ext))
    resid = frames + low_back(matmul(mixed, mix_weight) + mix_bias)
    normed_ffn = low(layer_norm(resid, feed_gain, feed_shift))
    hidden = low_back(matmul(normed_ffn, up_weight) + up_bias)
    active = low(jax.nn.gelu(hidden, approximate=False))
    return resid + low_back(matmul(active, down_weight) + down_bias)

def reference(frames, out_grad, item_lengths, domain_tags, domain_weight, query_weight, query_bias, key_weight, value_weight, value_bias, mix_weight, mix_bias, attn_gain, attn_shift, feed_gain, feed_shift, up_weight, up_bias, down_weight, down_bias):
    params = tuple((value.astype(jnp.float32) for value in (query_weight, query_bias, key_weight, value_weight, value_bias, mix_weight, mix_bias, attn_gain, attn_shift, feed_gain, feed_shift, up_weight, up_bias, down_weight, down_bias)))
    stream_len = frames.shape[1]

    def one_stream(totals, inputs):
        stream, cotangent, lengths, tags = inputs
        positions = jnp.arange(stream_len, dtype=jnp.int32)
        ext_positions = jnp.arange(-LEFT, stream_len + RIGHT, dtype=jnp.int32)
        segment = segment_ids(positions, lengths, stream_len)
        seg_ext = segment_ids(ext_positions, lengths, stream_len)
        weights = row_weights(segment, tags, domain_weight)
        result, pull = jax.vjp(lambda values, weights_in: forward(values, weights_in, segment, seg_ext), stream.astype(jnp.float32), params)
        grad_input, grad_params = pull(cotangent.astype(jnp.float32) * weights[:, None])
        totals = tuple((total + grad for total, grad in zip(totals, grad_params)))
        return (totals, (result.astype(jnp.bfloat16), grad_input.astype(jnp.bfloat16)))
    zeros = tuple((jnp.zeros_like(value) for value in params))
    totals, (outputs, input_grads) = lax.scan(one_stream, zeros, (frames, out_grad, item_lengths, domain_tags))
    return (outputs, input_grads) + totals
```

```python
import functools
import math

import jax
import jax.numpy as jnp
from jax import lax
from jax.experimental import pallas as pl
from jax.experimental.pallas import tpu as pltpu
from jax.sharding import PartitionSpec as P

HEADS = 8
LEFT = 10
RIGHT = 2
EDGE = 16
TILE = 256
SUB = 64
WINDOW = SUB + 2 * EDGE
GROUP = 4
MIB = 1 << 20
F32 = jnp.float32
BF16 = jnp.bfloat16


def dot(left, right):
    return jnp.dot(left, right, preferred_element_type=F32)


def against(left, right):
    return lax.dot_general(left, right, (((1,), (1,)), ((), ())), preferred_element_type=F32)


def over_rows(left, right):
    return lax.dot_general(left, right, (((0,), (0,)), ((), ())), preferred_element_type=F32)


def norm_parts(values):
    centered = values - jnp.mean(values, axis=-1, keepdims=True)
    variance = jnp.mean(centered * centered, axis=-1, keepdims=True)
    inverse = lax.rsqrt(variance + 1e-05)
    return centered * inverse, inverse


def norm_back(upstream, unit, inverse):
    return inverse * (
        upstream
        - jnp.mean(upstream, axis=-1, keepdims=True)
        - unit * jnp.mean(upstream * unit, axis=-1, keepdims=True)
    )


def row_sum(values):
    return jnp.sum(values, axis=0, keepdims=True)


def scaled_rows(values, weight):
    return values.astype(F32) * jnp.tile(weight, (1, values.shape[1] // 128))


def halves(values, core):
    rows = values.shape[0] // 2
    low, high = values[:rows].astype(BF16), values[rows:].astype(BF16)
    return jnp.where(core == 0, low, high), jnp.where(core == 0, high, low)


def head_masks(width, dtype):
    lane = lax.broadcasted_iota(jnp.int32, (1, width), 1) // (width // GROUP)
    return [(lane == head).astype(F32).astype(dtype) for head in range(GROUP)]


def stacked(values, masks):
    return jnp.concatenate([values * mask for mask in masks], axis=0)


def unstacked(values, masks):
    rows = values.shape[0] // GROUP
    total = values[:rows] * masks[0]
    for head in range(1, GROUP):
        total = total + values[head * rows : (head + 1) * rows] * masks[head]
    return total


def shaped(shape, dtype):
    return jax.ShapeDtypeStruct(shape, dtype)


def full(shape):
    return pl.BlockSpec(shape, lambda *_: (0,) * len(shape), pipeline_mode=pl.Buffered(1))


def row_block(rows, width):
    return pl.BlockSpec((rows, width), lambda step: (step, 0))


def column_block(rows, width):
    return pl.BlockSpec((rows, width), lambda step: (0, step))


ANY = pl.BlockSpec(memory_space=pl.ANY)
SCALARS = pl.BlockSpec(memory_space=pltpu.SMEM)


def call(body, name, steps, ins, outs, scratch=(), after=(), carry=(), vmem=32, flops=0, moved=0):
    used, passed = len(ins), len(after) + len(carry)

    def run(*refs):
        body(*refs[:used], *refs[used + passed : used + passed + len(outs)], *refs[used + passed + len(outs) + len(carry) :])

    out = pl.pallas_call(
        run,
        grid=(steps,),
        in_specs=[spec for _, spec in ins] + [ANY] * passed,
        out_specs=[spec for _, spec in outs] + [ANY] * len(carry),
        out_shape=[shape for shape, _ in outs] + [shaped(a.shape, a.dtype) for a in carry],
        input_output_aliases={used + len(after) + i: len(outs) + i for i in range(len(carry))},
        scratch_shapes=list(scratch),
        name=name,
        compiler_params=pltpu.CompilerParams(vmem_limit_bytes=vmem * MIB),
        cost_estimate=pl.CostEstimate(flops=flops, bytes_accessed=moved, transcendentals=0),
    )(*[array for array, _ in ins], *after, *carry)
    return out[: len(outs)], out[len(outs) :]


def project_body(x, gain, shift, wq, wk, wv, bq, bv, q_out, k_out, v_out):
    unit, _ = norm_parts(x[...].astype(F32))
    normed = (unit * gain[...] + shift[...]).astype(BF16)
    scale = (wq.shape[1] // HEADS) ** (-0.5)
    q_out[...] = (dot(normed, wq[...]) + bq[...]).astype(BF16) * jnp.asarray(scale, BF16)
    k_out[...] = dot(normed, wk[...]).astype(BF16)
    v_out[...] = (dot(normed, wv[...]) + bv[...]).astype(BF16)


def slot_ends(lengths):
    slots = lengths.shape[1]
    low = lax.broadcasted_iota(jnp.int32, (slots, slots), 0)
    high = lax.broadcasted_iota(jnp.int32, (slots, slots), 1)
    along = jnp.sum(jnp.where(low == high, lengths, 0.0), axis=1, keepdims=True)
    ends_column = jnp.sum(jnp.where(high <= low, lengths, 0.0), axis=1, keepdims=True)
    ends_row = jnp.sum(jnp.where(low <= high, along, 0.0), axis=0, keepdims=True)
    return ends_row, ends_column


def attend_body(
    steps,
    stream_len,
    where,
    domain,
    x,
    out_grad,
    q,
    k,
    v,
    before,
    behind,
    lengths,
    tags,
    gain,
    shift,
    wk,
    wv,
    bv,
    wmix,
    bmix,
    fgain,
    fshift,
    probs_out,
    mixed_out,
    resid_out,
    nffn_out,
    branch_out,
    weight_out,
    halo_out,
    keys,
    values,
    ends_row,
    ends_column,
):
    step = pl.program_id(0)
    count = steps * TILE
    width = x.shape[1]
    half = width // 2
    first = where[0]

    @pl.when(step == 0)
    def _():
        edge = jnp.concatenate([before[...], behind[...]], axis=0).astype(F32)
        unit, _ = norm_parts(edge)
        normed = (unit * gain[...] + shift[...]).astype(BF16)
        k_edge = dot(normed, wk[...]).astype(BF16)
        v_edge = (dot(normed, wv[...]) + bv[...]).astype(BF16)
        halo_out[:, :width] = k_edge
        halo_out[:, width:] = v_edge
        keys[:EDGE] = k_edge[:EDGE]
        values[:EDGE] = v_edge[:EDGE]
        keys[EDGE + count :] = k_edge[EDGE:]
        values[EDGE + count :] = v_edge[EDGE:]
        keys[EDGE : EDGE + count] = k[...]
        values[EDGE : EDGE + count] = v[...]
        row, column = slot_ends(lengths[...].astype(F32))
        ends_row[...] = row
        ends_column[...] = column

    kinds = tags[...]
    slot_weight = jnp.where(kinds == 0, domain[0], 0.0)
    slot_weight = jnp.where(kinds == 1, domain[1], slot_weight)
    slot_weight = jnp.where(kinds == 2, domain[2], slot_weight)
    slots = kinds.shape[1]
    masks = head_masks(half, BF16)
    masks_wide = head_masks(half, F32)
    slot = lax.broadcasted_iota(jnp.int32, (SUB, slots), 1).astype(F32)
    reach = lax.broadcasted_iota(jnp.int32, (SUB, WINDOW), 1) - lax.broadcasted_iota(
        jnp.int32, (SUB, WINDOW), 0
    )
    near = (reach >= EDGE - LEFT) & (reach <= EDGE + RIGHT)
    for sub in range(TILE // SUB):
        start = step * TILE + sub * SUB
        rows = slice(sub * SUB, (sub + 1) * SUB)
        window = pl.ds(pl.multiple_of(start, SUB), WINDOW)
        at = first + start
        places = (at + lax.broadcasted_iota(jnp.int32, (SUB, 1), 0)).astype(F32)
        seg = jnp.sum((ends_row[...] <= places).astype(F32), axis=1, keepdims=True)
        weight_out[rows, :] = jnp.broadcast_to(
            jnp.sum(jnp.where(seg == slot, slot_weight, 0.0), axis=1, keepdims=True),
            (SUB, weight_out.shape[1]),
        )
        others = (at - EDGE + lax.broadcasted_iota(jnp.int32, (1, WINDOW), 1)).astype(F32)
        seg_window = jnp.sum((ends_column[...] <= others).astype(F32), axis=0, keepdims=True)
        seg_window = jnp.where(others < 0.0, -1.0, seg_window)
        seg_window = jnp.where(others >= float(stream_len), -2.0, seg_window)
        allowed = near & (seg == seg_window)
        for group in range(2):
            lanes = slice(group * half, (group + 1) * half)
            scores = against(stacked(q[rows, lanes], masks), keys[window, lanes])
            scores = scores.reshape(GROUP, SUB, WINDOW)
            scores = jnp.where(allowed[None], scores, -1e30)
            peak = jnp.max(scores, axis=2, keepdims=True)
            grown = jnp.exp(scores - peak)
            probs = grown * (1.0 / jnp.sum(grown, axis=2, keepdims=True))
            probs = probs.reshape(GROUP * SUB, WINDOW).astype(BF16)
            probs_out[sub, group * GROUP * SUB : (group + 1) * GROUP * SUB, :] = probs
            mixed = unstacked(dot(probs, values[window, lanes]), masks_wide)
            mixed_out[rows, lanes] = mixed.astype(BF16)
    resid = x[...].astype(F32) + dot(mixed_out[...], wmix[...]) + bmix[...]
    resid_out[...] = resid
    unit, _ = norm_parts(resid)
    nffn_out[...] = (unit * fgain[...] + fshift[...]).astype(BF16)
    branch_out[...] = scaled_rows(out_grad[...], weight_out[...]).astype(BF16)


def active_body(where, nffn, branch, wup, bup, active_out, slope_out, keep_out, send_out, gdb_out):
    hidden = dot(nffn[...], wup[...]) + bup[...]
    below = 0.5 + 0.5 * lax.erf(hidden * math.sqrt(0.5))
    bell = jnp.exp(hidden * hidden * -0.5) * (1.0 / math.sqrt(2.0 * math.pi))
    active = (hidden * below).astype(BF16)
    active_out[...] = active
    slope_out[...] = (below + hidden * bell).astype(BF16)
    keep_out[...], send_out[...] = halves(over_rows(active, branch[...]), where[1])

    @pl.when(pl.program_id(0) == 0)
    def _():
        gdb_out[...] = row_sum(branch[...].astype(F32))


def output_body(resid, active, wdown, bdown, out):
    out[...] = (resid[...] + dot(active[...], wdown[...]) + bdown[...]).astype(BF16)


def hidden_body(where, branch, slope, nffn, wdown, gh_out, keep_out, send_out, gub_out):
    grad = against(branch[...], wdown[...]) * slope[...].astype(F32)
    low = grad.astype(BF16)
    gh_out[...] = low
    gub_out[...] = row_sum(low.astype(F32))
    keep_out[...], send_out[...] = halves(over_rows(nffn[...], low), where[1])


def resid_body(
    gh,
    resid,
    out_grad,
    weight,
    mixed,
    wup,
    fgain,
    wmix,
    gr_out,
    gm_out,
    gmix_out,
    gmb_out,
    gfg_out,
    gfs_out,
):
    @pl.when(pl.program_id(0) == 0)
    def _():
        for ref in (gmix_out, gmb_out, gfg_out, gfs_out):
            ref[...] = jnp.zeros_like(ref)

    grad = against(gh[...], wup[...])
    unit, inverse = norm_parts(resid[...])
    gfg_out[...] += row_sum(grad * unit)
    gfs_out[...] += row_sum(grad)
    grad_resid = scaled_rows(out_grad[...], weight[...]) + norm_back(
        grad * fgain[...], unit, inverse
    )
    gr_out[...] = grad_resid
    low = grad_resid.astype(BF16)
    gmb_out[...] += row_sum(low.astype(F32))
    gmix_out[...] += over_rows(mixed[...], low)
    gm_out[...] = against(low, wmix[...]).astype(BF16)


def attend_back_body(
    steps, q, probs, gm, k, v, halo, gq_out, gk_out, gv_out, edge_out, keys, values, gk, gv
):
    step = pl.program_id(0)
    count = steps * TILE
    width = q.shape[1]
    half = width // 2

    @pl.when(step == 0)
    def _():
        keys[:EDGE] = halo[:EDGE, :width]
        values[:EDGE] = halo[:EDGE, width:]
        keys[EDGE + count :] = halo[EDGE:, :width]
        values[EDGE + count :] = halo[EDGE:, width:]
        keys[EDGE : EDGE + count] = k[...]
        values[EDGE : EDGE + count] = v[...]
        gk[...] = jnp.zeros_like(gk)
        gv[...] = jnp.zeros_like(gv)

    scale = (width // HEADS) ** (-0.5)
    masks = head_masks(half, BF16)
    masks_wide = head_masks(half, F32)
    for sub in range(TILE // SUB):
        start = step * TILE + sub * SUB
        rows = slice(sub * SUB, (sub + 1) * SUB)
        window = pl.ds(pl.multiple_of(start, SUB), WINDOW)
        for group in range(2):
            lanes = slice(group * half, (group + 1) * half)
            queries = stacked(q[rows, lanes], masks)
            pulled = stacked(gm[rows, lanes], masks)
            low = probs[sub, group * GROUP * SUB : (group + 1) * GROUP * SUB, :]
            wide = low.astype(F32)
            grad = against(pulled, values[window, lanes])
            grad = wide * (grad - jnp.sum(wide * grad, axis=1, keepdims=True))
            grad = grad.astype(BF16)
            gq = unstacked(dot(grad, keys[window, lanes]), masks_wide) * scale
            gq_out[rows, lanes] = gq.astype(BF16)
            gk[window, lanes] += over_rows(grad, queries)
            gv[window, lanes] += over_rows(low, pulled)

    @pl.when(step == steps - 1)
    def _():
        gk_out[...] = gk[EDGE : EDGE + count].astype(BF16)
        gv_out[...] = gv[EDGE : EDGE + count].astype(BF16)
        edge_out[:EDGE, :width] = gk[:EDGE].astype(BF16)
        edge_out[:EDGE, width:] = gv[:EDGE].astype(BF16)
        edge_out[EDGE:, :width] = gk[EDGE + count :].astype(BF16)
        edge_out[EDGE:, width:] = gv[EDGE + count :].astype(BF16)


def weights_body(
    where,
    x,
    gq,
    gk,
    gv,
    before,
    behind,
    edge,
    gain,
    shift,
    wq,
    wk,
    wv,
    gmix,
    gdb,
    gub,
    gmb,
    gfg,
    gfs,
    keep_out,
    send_out,
    sums,
    vec,
):
    width = x.shape[1]
    core = where[1]
    unit = norm_parts(x[...].astype(F32))[0].astype(BF16)
    far = norm_parts(jnp.concatenate([before[...], behind[...]], axis=0).astype(F32))[0].astype(BF16)
    gain_column = jnp.transpose(jnp.broadcast_to(gain[...], (128, width)))[:, :1]
    shift_column = jnp.transpose(jnp.broadcast_to(shift[...], (128, width)))[:, :1]
    by_gain = jnp.zeros((width, 1), F32)
    by_shift = jnp.zeros((width, 1), F32)
    for place, (grad, weight) in enumerate(((gq, wq), (gk, wk), (gv, wv))):
        product = over_rows(unit, grad[...])
        column = row_sum(grad[...].astype(F32))
        if place > 0:
            lanes = slice((place - 1) * width, place * width)
            product = product + over_rows(far, edge[:, lanes])
            column = column + row_sum(edge[:, lanes].astype(F32))
        lanes = slice(place * width, (place + 1) * width)
        keep_out[:, lanes], send_out[:, lanes] = halves(
            product * gain_column + shift_column * column, core
        )
        wide = weight[...].astype(F32)
        by_gain = by_gain + jnp.sum(wide * product, axis=1, keepdims=True)
        by_shift = by_shift + jnp.sum(wide * column, axis=1, keepdims=True)
        if place != 1:
            sums[place // 2 : place // 2 + 1] = column
    sums[2:3] = jnp.transpose(jnp.broadcast_to(by_gain, (width, 128)))[:1]
    sums[3:4] = jnp.transpose(jnp.broadcast_to(by_shift, (width, 128)))[:1]
    keep_out[:, 3 * width : 4 * width], send_out[:, 3 * width : 4 * width] = halves(
        gmix[...], core
    )
    vec[...] = jnp.zeros_like(vec)
    row = 0
    for ref in [sums.at[i : i + 1] for i in range(4)] + [gmb, gfg, gfs, gdb, gub]:
        for part in range(0, ref.shape[1], 128):
            vec[row : row + 1] = ref[:, part : part + 128]
            row += 1
    keep_out[:, 4 * width :], send_out[:, 4 * width :] = halves(vec[...], core)


def input_body(
    steps,
    x,
    gq,
    gk,
    gv,
    gr,
    before,
    behind,
    edge,
    gain,
    wq,
    wk,
    wv,
    ig_out,
    own_edge_out,
    far_edge_out,
):
    step = pl.program_id(0)
    width = x.shape[1]

    @pl.when(step == 0)
    def _():
        unit, inverse = norm_parts(
            jnp.concatenate([before[...], behind[...]], axis=0).astype(F32)
        )
        grad = against(edge[:, :width], wk[...]) + against(edge[:, width:], wv[...])
        far_edge_out[...] = norm_back(grad * gain[...], unit, inverse)

    unit, inverse = norm_parts(x[...].astype(F32))
    grad = against(gq[...], wq[...]) + against(gk[...], wk[...]) + against(gv[...], wv[...])
    result = gr[...] + norm_back(grad * gain[...], unit, inverse)
    ig_out[...] = result.astype(BF16)

    @pl.when(step == 0)
    def _():
        own_edge_out[:EDGE] = result[:EDGE]

    @pl.when(step == steps - 1)
    def _():
        own_edge_out[EDGE:] = result[-EDGE:]


def swapped(value, axis, mask):
    count = lax.axis_size(axis)
    return lax.ppermute(value, axis, [(i, i ^ mask) for i in range(count)])


def across(value, first):
    tm, items = lax.axis_size("tm"), lax.axis_size("items")
    pairs = []
    for i in range(tm):
        for j in range(items):
            along_x = (i % 2 == 0) == first
            pairs.append((i * items + j, i * items + (j ^ 1) if along_x else (i ^ 2) * items + j))
    return lax.ppermute(value, ("tm", "items"), pairs)


def line(values):
    return [swapped(values[i], "tm", 4 * i) for i in (1, 2, 3)]


def cut(value, place, rows):
    return lax.dynamic_slice_in_dim(value, place * rows, rows, 0)


def total_of(parts):
    total = parts[0].astype(F32)
    for part in parts[1:]:
        total = total + part.astype(F32)
    return total.astype(BF16)


def paired(own, got, bit):
    return jnp.where(bit == 0, jnp.concatenate([own, got]), jnp.concatenate([got, own]))


class Place:
    def __init__(self):
        tm = lax.axis_index("tm").astype(jnp.int32)
        x_bit = lax.axis_index("items").astype(jnp.int32) % 2
        y_bit = (tm // 2) % 2
        self.core = tm % 2
        self.first = jnp.where(self.core == 0, x_bit, y_bit)
        self.second = jnp.where(self.core == 0, y_bit, x_bit)
        self.line = tm // 4


class Sum:
    def __init__(self, place, keep, send):
        self.place = place
        self.parts = [keep, swapped(send, "tm", 1)]

    def held(self):
        return self.parts[0]

    def hold(self, value):
        self.parts[0] = value

    def fold_half(self, bit, first):
        rows = self.parts[0].shape[0] // 2
        mine, other = (
            total_of([cut(part, place, rows) for part in self.parts]) for place in (bit, 1 - bit)
        )
        self.parts = [mine, across(other, first)]

    def fold_core(self):
        self.fold_half(self.place.first, True)

    def fold_plane(self):
        self.fold_half(self.place.second, False)

    def fold_pair(self):
        rows = self.parts[0].shape[0] // 4
        cuts = [
            total_of([cut(part, self.place.line ^ i, rows) for part in self.parts])
            for i in range(4)
        ]
        self.parts = [cuts[0]] + line(cuts)

    def fold_line(self):
        own = total_of(self.parts)
        self.parts = [own] + line([own] * 4)

    def spread_line(self):
        rows = self.parts[0].shape[0]
        own = jnp.zeros((4 * rows, self.parts[0].shape[1]), BF16)
        for i, part in enumerate(self.parts):
            own = lax.dynamic_update_slice_in_dim(own, part, (self.place.line ^ i) * rows, 0)
        self.parts = [own, across(own, False)]

    def spread_pair(self):
        own = paired(*self.parts, self.place.second)
        self.parts = [own, across(own, True)]

    def spread_plane(self):
        own = paired(*self.parts, self.place.first)
        self.parts = [own, swapped(own, "tm", 1)]

    def whole(self):
        own, got = self.parts
        low = self.place.core == 0
        return jnp.where(low, own, got), jnp.where(low, got, own)


class PlainSum:
    def __init__(self, place, keep, send):
        self.place = place
        self.parts = [keep, send]

    def held(self):
        return self.parts[0]

    def hold(self, value):
        self.parts[0] = value

    def fold_core(self):
        pass

    fold_plane = fold_pair = fold_line = spread_line = spread_pair = spread_plane = fold_core

    def whole(self):
        return lax.psum(Sum.whole(self), ("tm", "items"))


def passed_along(x, by):
    count = lax.axis_size("tm")
    return lax.ppermute(x, "tm", [(i, i + by) for i in range(count) if 0 <= i + by < count])


def local(
    fast,
    frames,
    out_grad,
    item_lengths,
    domain_tags,
    domain_weight,
    wq,
    bq,
    wk,
    wv,
    bv,
    wmix,
    bmix,
    again,
    ashift,
    fgain,
    fshift,
    wup,
    bup,
    wdown,
    bdown,
):
    frames = frames[0]
    out_grad = out_grad[0]
    count, width = frames.shape
    ffw = wup.shape[1]
    steps = count // TILE
    parts = ffw // width
    subs = TILE // SUB
    slots = item_lengths.shape[1]
    stream_len = count * lax.axis_size("tm")
    unit_flops = 2 * count * width * width
    bq, bv, bmix, again, ashift, fgain, fshift, bup, bdown = (
        vector[None] for vector in (bq, bv, bmix, again, ashift, fgain, fshift, bup, bdown)
    )
    place = Place()
    where = jnp.stack([lax.axis_index("tm") * count, place.core]).astype(jnp.int32)
    scalars = (where, SCALARS)
    before = passed_along(frames[count - EDGE :], 1)
    behind = passed_along(frames[:EDGE], -1)

    def stays(array):
        return pltpu.with_memory_space_constraint(array, pltpu.HBM)

    def rows(array, size=TILE):
        return (stays(array), row_block(size, array.shape[1]))

    def columns(array):
        return (stays(array), column_block(array.shape[0], width))

    def held(array):
        return (array, full(array.shape))

    def held_there(array):
        return (stays(array), full(array.shape))

    def row_out(wide, dtype, size=TILE):
        return (pltpu.HBM((count, wide), dtype), row_block(size, wide))

    def column_out(high, dtype):
        return (pltpu.HBM((high, ffw), dtype), column_block(high, width))

    def held_out(shape, dtype):
        return (shaped(shape, dtype), full(shape))

    vec_out = held_out((1, width), F32)

    (q, k, v), _ = call(
        project_body,
        "project",
        2,
        [rows(frames, count // 2)] + [held(a) for a in (again, ashift, wq, wk, wv, bq, bv)],
        [row_out(width, BF16, count // 2)] * 3,
        flops=3 * unit_flops,
        moved=6 * MIB,
    )
    probs_spec = pl.BlockSpec((subs, HEADS * SUB, WINDOW), lambda step: (step, 0, 0))
    (probs, mixed, resid, nffn, branch, weight, halo), _ = call(
        functools.partial(attend_body, steps, stream_len),
        "attend",
        steps,
        [scalars, (domain_weight, SCALARS)]
        + [rows(a) for a in (frames, out_grad, q)]
        + [held_there(k), held_there(v)]
        + [
            held(a)
            for a in (
                before,
                behind,
                item_lengths,
                domain_tags,
                again,
                ashift,
                wk,
                wv,
                bv,
                wmix,
                bmix,
                fgain,
                fshift,
            )
        ],
        [
            (pltpu.HBM((count // SUB, HEADS * SUB, WINDOW), BF16), probs_spec),
            row_out(width, BF16),
            row_out(width, F32),
            row_out(width, BF16),
            row_out(width, BF16),
            row_out(128, F32),
            held_out((2 * EDGE, 2 * width), BF16),
        ],
        scratch=[
            pltpu.VMEM((count + 2 * EDGE, width), BF16),
            pltpu.VMEM((count + 2 * EDGE, width), BF16),
            pltpu.VMEM((1, slots), F32),
            pltpu.VMEM((slots, 1), F32),
        ],
        flops=4 * unit_flops,
        moved=12 * MIB,
    )
    half_block = (shaped((ffw // 2, width), BF16), row_block(width // 2, width))
    (active, slope, keep_d, send_d, gdb), _ = call(
        active_body,
        "active",
        parts,
        [scalars, held_there(nffn), held_there(branch)]
        + [(wup, column_block(width, width)), (bup, column_block(1, width))],
        [column_out(count, BF16), column_out(count, BF16), half_block, half_block, vec_out],
        flops=4 * parts * unit_flops,
        moved=14 * MIB,
    )
    kind = Sum if fast else PlainSum
    down = kind(place, keep_d, send_d)

    half_block = (shaped((width // 2, ffw), BF16), column_block(width // 2, width))
    (gh, keep_u, send_u, gub), held_on = call(
        hidden_body,
        "hidden",
        parts,
        [scalars, held_there(branch), columns(slope), held_there(nffn)]
        + [(wdown, row_block(width, width))],
        [
            column_out(count, BF16),
            half_block,
            half_block,
            (shaped((1, ffw), F32), column_block(1, width)),
        ],
        carry=[down.held()],
        flops=2 * parts * unit_flops,
        moved=14 * MIB,
    )
    down.hold(held_on[0])
    up = kind(place, keep_u, send_u)
    down.fold_core()

    (gr, gm, gmix, gmb, gfg, gfs), held_on = call(
        resid_body,
        "resid",
        steps,
        [rows(a) for a in (gh, resid, out_grad, weight, mixed)]
        + [held(a) for a in (wup, fgain, wmix)],
        [
            row_out(width, F32),
            row_out(width, BF16),
            held_out((width, width), F32),
            vec_out,
            vec_out,
            vec_out,
        ],
        carry=[down.held(), up.held()],
        flops=(parts + 2) * unit_flops,
        moved=14 * MIB,
    )
    down.hold(held_on[0])
    up.hold(held_on[1])
    down.fold_plane()
    up.fold_core()

    (gq, gk, gv, edge), held_on = call(
        functools.partial(attend_back_body, steps),
        "attend_back",
        steps,
        [rows(q), (stays(probs), probs_spec), rows(gm)]
        + [held_there(k), held_there(v), held_there(halo)],
        [
            row_out(width, BF16),
            (pltpu.HBM((count, width), BF16), full((count, width))),
            (pltpu.HBM((count, width), BF16), full((count, width))),
            held_out((2 * EDGE, 2 * width), BF16),
        ],
        scratch=[pltpu.VMEM((count + 2 * EDGE, width), BF16)] * 2
        + [pltpu.VMEM((count + 2 * EDGE, width), F32)] * 2,
        carry=[down.held(), up.held()],
        flops=8 * unit_flops,
        moved=10 * MIB,
    )
    down.hold(held_on[0])
    up.hold(held_on[1])
    down.fold_pair()
    up.fold_plane()

    rest_out = held_out((width // 2, 4 * width + 128), BF16)
    (keep_q, send_q), held_on = call(
        weights_body,
        "weights",
        1,
        [scalars]
        + [held_there(a) for a in (frames, gq, gk, gv)]
        + [
            held(a)
            for a in (
                before,
                behind,
                edge,
                again,
                ashift,
                wq,
                wk,
                wv,
                gmix,
                gdb,
                gub,
                gmb,
                gfg,
                gfs,
            )
        ],
        [rest_out, rest_out],
        scratch=[pltpu.VMEM((8, width), F32), pltpu.VMEM((width, 128), F32)],
        carry=[down.held(), up.held()],
        flops=3 * unit_flops,
        moved=8 * MIB,
    )
    down.hold(held_on[0])
    up.hold(held_on[1])
    rest = kind(place, keep_q, send_q)
    down.fold_line()
    up.fold_pair()

    (output,), held_on = call(
        output_body,
        "output",
        steps,
        [rows(resid), rows(active), held(wdown), held(bdown)],
        [row_out(width, BF16)],
        carry=[rest.held(), up.held()],
        flops=parts * unit_flops,
        moved=9 * MIB,
    )
    rest.hold(held_on[0])
    up.hold(held_on[1])
    rest.fold_core()
    down.spread_line()
    up.fold_line()

    (ig, own_edge, far_edge), held_on = call(
        functools.partial(input_body, steps),
        "input",
        steps,
        [rows(a) for a in (frames, gq, gk, gv, gr)]
        + [held(a) for a in (before, behind, edge, again, wq, wk, wv)],
        [
            row_out(width, BF16),
            held_out((2 * EDGE, width), F32),
            held_out((2 * EDGE, width), F32),
        ],
        carry=[rest.held()],
        flops=3 * unit_flops,
        moved=8 * MIB,
    )
    rest.hold(held_on[0])
    rest.fold_plane()
    down.spread_pair()
    up.spread_line()
    rest.fold_pair()
    down.spread_plane()
    up.spread_pair()
    rest.fold_line()
    up.spread_plane()
    from_behind = passed_along(far_edge[:EDGE], -1)
    from_before = passed_along(far_edge[EDGE:], 1)
    ig = ig.at[:EDGE].set((own_edge[:EDGE] + from_before).astype(BF16))
    ig = ig.at[count - EDGE :].set((own_edge[EDGE:] + from_behind).astype(BF16))
    low, high = (half.reshape(parts, width // 2, width) for half in down.whole())
    grad_down = jnp.stack([low, high], axis=1).reshape(ffw, width).astype(F32)
    rest.spread_line()
    grad_up = jnp.concatenate(up.whole(), axis=0).astype(F32)
    rest.spread_pair()
    rest.spread_plane()
    rest = jnp.concatenate(rest.whole(), axis=0).astype(F32)
    grad_q, grad_k, grad_v, grad_mix = (rest[:, i * width : (i + 1) * width] for i in range(4))
    vectors = rest[: 12 * width // 128, 4 * width :].reshape(-1)
    gqb, gvb, gag, gas, gmb, gfg, gfs, gdb = (
        vectors[i * width : (i + 1) * width] for i in range(8)
    )
    gub = vectors[8 * width :]
    return (
        output[None],
        ig[None],
        grad_q,
        gqb,
        grad_k,
        grad_v,
        gvb,
        grad_mix,
        gmb,
        gag,
        gas,
        gfg,
        gfs,
        grad_up,
        gub,
        grad_down,
        gdb,
    )


def solution(mesh):
    rows = P("items", "tm", None)
    in_specs = (rows, rows, P("items", None), P("items", None)) + (P(),) * 16
    out_specs = (rows, rows) + (P(),) * 15
    fast = mesh.shape["tm"] == 16 and mesh.shape["items"] == 2
    return jax.shard_map(
        functools.partial(local, fast),
        mesh=mesh,
        in_specs=in_specs,
        out_specs=out_specs,
        check_vma=False,
    )
```

```python
import functools
import math

import jax
import jax.numpy as jnp
from jax import lax
from jax.experimental import pallas as pl
from jax.experimental.pallas import tpu as pltpu
from jax.sharding import PartitionSpec as P

HEADS = 8
LEFT = 10
RIGHT = 2
EDGE = 16
TILE = 256
SUB = 32
WINDOW = 48
GROUP = 4
MIB = 1 << 20
LOG2E = 1.0 / math.log(2.0)
F32 = jnp.float32
BF16 = jnp.bfloat16


def dot(left, right):
    return jnp.dot(left, right, preferred_element_type=F32)


def against(left, right):
    return lax.dot_general(left, right, (((1,), (1,)), ((), ())), preferred_element_type=F32)


def over_rows(left, right):
    return lax.dot_general(left, right, (((0,), (0,)), ((), ())), preferred_element_type=F32)


def norm_parts(values):
    centered = values - jnp.mean(values, axis=-1, keepdims=True)
    variance = jnp.mean(centered * centered, axis=-1, keepdims=True)
    inverse = lax.rsqrt(variance + 1e-05)
    return centered * inverse, inverse


def norm_back(upstream, unit, inverse):
    return inverse * (
        upstream
        - jnp.mean(upstream, axis=-1, keepdims=True)
        - unit * jnp.mean(upstream * unit, axis=-1, keepdims=True)
    )


def row_sum(values):
    return jnp.sum(values, axis=0, keepdims=True)


def scaled_rows(values, weight):
    return values.astype(F32) * jnp.tile(weight, (1, values.shape[1] // 128))


def halves(values, core):
    rows = values.shape[0] // 2
    low, high = values[:rows].astype(BF16), values[rows:].astype(BF16)
    return jnp.where(core == 0, low, high), jnp.where(core == 0, high, low)


def tiles(count, rows=TILE):
    return [slice(start, start + rows) for start in range(0, count, rows)]


def shaped(shape, dtype):
    return jax.ShapeDtypeStruct(shape, dtype)


ANY = pl.BlockSpec(memory_space=pl.ANY)
SCALARS = pl.BlockSpec(memory_space=pltpu.SMEM)
WHOLE = pl.BlockSpec(memory_space=pltpu.VMEM)


def call(body, name, ins, outs, scratch=(), scalars=(), far_ins=(), vmem=10, flops=0, moved=0):
    return pl.pallas_call(
        body,
        in_specs=[SCALARS] * len(scalars) + [WHOLE] * len(ins) + [ANY] * len(far_ins),
        out_specs=[ANY if own_copies else WHOLE for _, own_copies in outs],
        out_shape=[out for out, _ in outs],
        scratch_shapes=list(scratch),
        name=name,
        compiler_params=pltpu.CompilerParams(vmem_limit_bytes=vmem * MIB),
        cost_estimate=pl.CostEstimate(flops=flops, bytes_accessed=moved, transcendentals=0),
    )(*scalars, *ins, *far_ins)


def near(*shape):
    return pltpu.VMEM(shape[:-1], shape[-1]), False


def far(*shape):
    return pltpu.HBM(shape[:-1], shape[-1]), False


def copied(*shape):
    return pltpu.HBM(shape[:-1], shape[-1]), True


def free(*shape):
    return shaped(shape[:-1], shape[-1]), False


def project_body(x, gain, shift, wq, wk, wv, bq, bv, q_out, k_out, v_out):
    scale = (wq.shape[1] // HEADS) ** (-0.5)
    for rows in tiles(x.shape[0]):
        unit, _ = norm_parts(x[rows, :].astype(F32))
        normed = (unit * gain[...] + shift[...]).astype(BF16)
        q_out[rows, :] = (dot(normed, wq[...]) + bq[...]).astype(BF16) * jnp.asarray(scale, BF16)
        k_out[rows, :] = dot(normed, wk[...]).astype(BF16)
        v_out[rows, :] = (dot(normed, wv[...]) + bv[...]).astype(BF16)


def slot_ends(lengths):
    slots = lengths.shape[1]
    low = lax.broadcasted_iota(jnp.int32, (slots, slots), 0)
    high = lax.broadcasted_iota(jnp.int32, (slots, slots), 1)
    along = jnp.sum(jnp.where(low == high, lengths, 0.0), axis=1, keepdims=True)
    ends_column = jnp.sum(jnp.where(high <= low, lengths, 0.0), axis=1, keepdims=True)
    ends_row = jnp.sum(jnp.where(low <= high, along, 0.0), axis=0, keepdims=True)
    return ends_row, ends_column


def head_lanes(dtype):
    lane = lax.broadcasted_iota(jnp.int32, (1, 128), 1)
    return [(lane < 64).astype(F32).astype(dtype), (lane >= 64).astype(F32).astype(dtype)]


def stacked(values, masks):
    low, high = values[:, :128], values[:, 128:]
    none = jnp.zeros_like(low)
    return jnp.concatenate(
        [
            jnp.concatenate([low * masks[0], none], axis=1),
            jnp.concatenate([low * masks[1], none], axis=1),
            jnp.concatenate([none, high * masks[0]], axis=1),
            jnp.concatenate([none, high * masks[1]], axis=1),
        ],
        axis=0,
    )


def unstacked(values):
    rows = values.shape[0] // GROUP
    first = lax.broadcasted_iota(jnp.int32, (rows, 128), 1) < 64
    low = jnp.where(first, values[:rows, :128], values[rows : 2 * rows, :128])
    high = jnp.where(first, values[2 * rows : 3 * rows, 128:], values[3 * rows :, 128:])
    return jnp.concatenate([low, high], axis=1)


def fill_window(store, edge, own, count):
    store[:LEFT] = edge[EDGE - LEFT : EDGE]
    store[LEFT : LEFT + count] = own
    store[LEFT + count :] = edge[EDGE : EDGE + store.shape[0] - LEFT - count]


def forward_body(
    stream_len,
    where,
    domain,
    x,
    out_grad,
    q,
    k,
    v,
    before,
    behind,
    lengths,
    tags,
    gain,
    shift,
    wk,
    wv,
    bv,
    wmix,
    bmix,
    fgain,
    fshift,
    wup,
    bup,
    wdown,
    probs_out,
    q_out,
    keys_out,
    values_out,
    active_out,
    resid_out,
    gr_out,
    gm_out,
    keep_d_out,
    send_d_out,
    keep_u_out,
    send_u_out,
    gdb_out,
    gub_out,
    gmb_out,
    gfg_out,
    gfs_out,
    keys,
    values,
    ends_row,
    ends_column,
    probs,
    mixed,
    resid,
    weight,
    nffn,
    branch,
    active,
    slope,
    gh,
    gr,
    gm,
    sems,
    block_sems,
):
    count, width = x.shape
    ffw = wup.shape[1]
    half = width // 2
    first = where[0]
    core = where[1]
    copies = []

    def carry_out(source, target):
        copies.append(pltpu.make_async_copy(source, target, sems.at[len(copies)]))
        copies[-1].start()

    carry_out(q, q_out)
    edge = jnp.concatenate([before[...], behind[...]], axis=0).astype(F32)
    unit, _ = norm_parts(edge)
    normed = (unit * gain[...] + shift[...]).astype(BF16)
    fill_window(keys, dot(normed, wk[...]).astype(BF16), k[...], count)
    fill_window(values, (dot(normed, wv[...]) + bv[...]).astype(BF16), v[...], count)
    carry_out(keys, keys_out)
    carry_out(values, values_out)
    row, column = slot_ends(lengths[...].astype(F32))
    ends_row[...] = row
    ends_column[...] = column

    kinds = tags[...]
    slot_weight = jnp.where(kinds == 0, domain[0], 0.0)
    slot_weight = jnp.where(kinds == 1, domain[1], slot_weight)
    slot_weight = jnp.where(kinds == 2, domain[2], slot_weight)
    slots = kinds.shape[1]
    slot = lax.broadcasted_iota(jnp.int32, (TILE, slots), 1).astype(F32)
    masks = head_lanes(BF16)
    lanes_all = GROUP * SUB
    key_at = lax.broadcasted_iota(jnp.int32, (WINDOW, lanes_all), 0)
    query_at = lax.broadcasted_iota(jnp.int32, (WINDOW, lanes_all), 1) % SUB
    near = (key_at >= query_at) & (key_at <= query_at + LEFT + RIGHT)

    def one_tile(step, carried):
        tile_at = pl.multiple_of(step * TILE, TILE)
        places = (first + tile_at + lax.broadcasted_iota(jnp.int32, (TILE, 1), 0)).astype(F32)
        seg = jnp.sum((ends_row[...] <= places).astype(F32), axis=1, keepdims=True)
        weight[pl.ds(tile_at, TILE), :] = jnp.broadcast_to(
            jnp.sum(jnp.where(seg == slot, slot_weight, 0.0), axis=1, keepdims=True),
            (TILE, weight.shape[1]),
        )
        allowed, scores, pieces = [], [], []
        for sub in range(TILE // SUB):
            at = first + tile_at + sub * SUB
            ours = (at + lax.broadcasted_iota(jnp.int32, (1, lanes_all), 1) % SUB).astype(F32)
            others = (at - LEFT + lax.broadcasted_iota(jnp.int32, (WINDOW, 1), 0)).astype(F32)
            seg_ours = jnp.sum((ends_column[...] <= ours).astype(F32), axis=0, keepdims=True)
            seg_others = jnp.sum((ends_row[...] <= others).astype(F32), axis=1, keepdims=True)
            seg_others = jnp.where(others < 0.0, -1.0, seg_others)
            seg_others = jnp.where(others >= float(stream_len), -2.0, seg_others)
            allowed.append(near & (seg_ours == seg_others))
            for group in range(2):
                pieces.append((sub, group))
        for sub, group in pieces:
            start = pl.multiple_of(tile_at + sub * SUB, SUB)
            lanes = slice(group * half, (group + 1) * half)
            queries = stacked(q[pl.ds(start, SUB), lanes], masks)
            scores.append(against(keys[pl.ds(start, WINDOW), lanes], queries))
        lows = []
        for (sub, group), score in zip(pieces, scores):
            score = jnp.where(allowed[sub], score, -1e30)
            grown = jnp.exp(score - jnp.max(score, axis=0, keepdims=True))
            low = (grown * (1.0 / jnp.sum(grown, axis=0, keepdims=True))).astype(BF16)
            probs[2 * (step * (TILE // SUB) + sub) + group] = low
            lows.append(low)
        for (sub, group), low in zip(pieces, lows):
            start = pl.multiple_of(tile_at + sub * SUB, SUB)
            lanes = slice(group * half, (group + 1) * half)
            heads = unstacked(over_rows(low, values[pl.ds(start, WINDOW), lanes]))
            mixed[pl.ds(start, SUB), lanes] = heads.astype(BF16)
        return carried

    lax.fori_loop(0, count // TILE, one_tile, 0)
    carry_out(probs, probs_out)
    bias = jnp.zeros((1, width), F32)
    for rows in tiles(count):
        summed = x[rows, :].astype(F32) + dot(mixed[rows, :], wmix[...]) + bmix[...]
        resid[rows, :] = summed
        unit, _ = norm_parts(summed)
        nffn[rows, :] = (unit * fgain[...] + fshift[...]).astype(BF16)
        scaled = scaled_rows(out_grad[rows, :], weight[rows, :]).astype(BF16)
        branch[rows, :] = scaled
        bias = bias + row_sum(scaled.astype(F32))
    gdb_out[...] = bias
    carry_out(resid, resid_out)

    def one_block(block, carried):
        at = pl.multiple_of(block * width, width)
        lanes = pl.ds(at, width)
        for rows in tiles(count):
            hidden = dot(nffn[rows, :], wup[:, lanes]) + bup[:, lanes]
            below = 1.0 + lax.erf(hidden * math.sqrt(0.5))
            bell = jnp.exp2(
                hidden * hidden * (-0.5 * LOG2E) + math.log2(2.0 / math.sqrt(2.0 * math.pi))
            )
            active[rows, lanes] = ((hidden * 0.5) * below).astype(BF16)
            slope[rows, :] = (below + hidden * bell).astype(BF16)
        pltpu.make_async_copy(
            active.at[:, lanes], active_out.at[:, lanes], block_sems.at[block]
        ).start()
        keep_d_out[:, lanes], send_d_out[:, lanes] = halves(
            over_rows(active[:, lanes], branch[...]), core
        )
        bias = jnp.zeros((1, width), F32)
        for rows in tiles(count):
            half_branch = branch[rows, :] * jnp.asarray(0.5, BF16)
            grad = against(half_branch, wdown[lanes, :]) * slope[rows, :].astype(F32)
            low = grad.astype(BF16)
            gh[rows, lanes] = low
            bias = bias + row_sum(low.astype(F32))
        gub_out[:, lanes] = bias
        keep_u_out[:, lanes], send_u_out[:, lanes] = halves(
            over_rows(nffn[...], gh[:, lanes]), core
        )
        return carried

    lax.fori_loop(0, ffw // width, one_block, 0)
    by_bias, by_gain, by_shift = (jnp.zeros((1, width), F32) for _ in range(3))
    for rows in tiles(count):
        grad = against(gh[rows, :], wup[...])
        unit, inverse = norm_parts(resid[rows, :])
        by_gain = by_gain + row_sum(grad * unit)
        by_shift = by_shift + row_sum(grad)
        grad_resid = scaled_rows(out_grad[rows, :], weight[rows, :]) + norm_back(
            grad * fgain[...], unit, inverse
        )
        gr[rows, :] = grad_resid
        low = grad_resid.astype(BF16)
        branch[rows, :] = low
        by_bias = by_bias + row_sum(low.astype(F32))
        gm[rows, :] = against(low, wmix[...]).astype(BF16)
    carry_out(gr, gr_out)
    carry_out(gm, gm_out)
    there = slice(ffw, ffw + width)
    keep_u_out[:, there], send_u_out[:, there] = halves(over_rows(mixed[...], branch[...]), core)
    gmb_out[...] = by_bias
    gfg_out[...] = by_gain
    gfs_out[...] = by_shift
    for block in range(ffw // width):
        lanes = slice(block * width, (block + 1) * width)
        copies.append(
            pltpu.make_async_copy(
                active.at[:, lanes], active_out.at[:, lanes], block_sems.at[block]
            )
        )
    for copy in copies:
        copy.wait()


def output_body(resid, active, wdown, bdown, out):
    for rows in tiles(resid.shape[0]):
        out[rows, :] = (resid[rows, :] + dot(active[rows, :], wdown[...]) + bdown[...]).astype(BF16)


def backward_body(
    where,
    q,
    probs,
    gm,
    keys,
    values,
    before,
    behind,
    gain,
    shift,
    gdb,
    gub,
    gmb,
    gfg,
    gfs,
    x_in,
    gr_in,
    wq_in,
    wk_in,
    wv_in,
    keep_out,
    send_out,
    own_edge_out,
    far_edge_out,
    ig_out,
    x,
    gr,
    wq,
    wk,
    wv,
    gk_window,
    gv_window,
    gq,
    gk,
    gv,
    ig,
    sums,
    vec,
    sems,
    tile_sems,
):
    count, width = q.shape
    half = width // 2
    core = where[1]
    loads = []
    for source, target in ((x_in, x), (wq_in, wq), (wk_in, wk), (wv_in, wv), (gr_in, gr)):
        loads.append(pltpu.make_async_copy(source, target, sems.at[len(loads)]))
        loads[-1].start()
    gk_window[...] = jnp.zeros_like(gk_window)
    gv_window[...] = jnp.zeros_like(gv_window)
    scale = (width // HEADS) ** (-0.5)
    masks = head_lanes(BF16)
    pieces = [(sub, group) for sub in range(TILE // SUB) for group in range(2)]

    def one_tile(step, carried):
        tile_at = pl.multiple_of(step * TILE, TILE)

        def spot(sub, group):
            start = pl.multiple_of(tile_at + sub * SUB, SUB)
            return pl.ds(start, SUB), pl.ds(start, WINDOW), slice(group * half, (group + 1) * half)

        pulls, grads = [], []
        for sub, group in pieces:
            rows, window, lanes = spot(sub, group)
            pulled = stacked(gm[rows, lanes], masks)
            pulls.append(pulled)
            grads.append(against(values[window, lanes], pulled))
        lows = []
        for (sub, group), grad in zip(pieces, grads):
            wide = probs[2 * (step * (TILE // SUB) + sub) + group].astype(F32)
            product = wide * grad
            lows.append((product - wide * jnp.sum(product, axis=0, keepdims=True)).astype(BF16))
        for (sub, group), pulled, low in zip(pieces, pulls, lows):
            rows, window, lanes = spot(sub, group)
            queries = stacked(q[rows, lanes], masks)
            gq[rows, lanes] = (unstacked(over_rows(low, keys[window, lanes])) * scale).astype(BF16)
            gk_window[window, lanes] += dot(low, queries)
            gv_window[window, lanes] += dot(
                probs[2 * (step * (TILE // SUB) + sub) + group], pulled
            )
        return carried

    lax.fori_loop(0, count // TILE, one_tile, 0)
    edges = []
    for window, grad in ((gk_window, gk), (gv_window, gv)):
        grad[...] = window[LEFT : LEFT + count].astype(BF16)
        edges.append(
            jnp.concatenate(
                [window[:LEFT], window[LEFT + count : LEFT + count + RIGHT]], axis=0
            ).astype(BF16)
        )

    far_frames = jnp.concatenate([before[EDGE - LEFT :], behind[:RIGHT]], axis=0).astype(F32)
    far_unit, far_inverse = norm_parts(far_frames)
    far_low = far_unit.astype(BF16)
    for load in loads:
        load.wait()
    unit = norm_parts(x[...].astype(F32))[0].astype(BF16)
    gain_column = jnp.transpose(jnp.broadcast_to(gain[...], (128, width)))[:, :1]
    shift_column = jnp.transpose(jnp.broadcast_to(shift[...], (128, width)))[:, :1]
    by_gain = jnp.zeros((width, 1), F32)
    by_shift = jnp.zeros((width, 1), F32)
    for place, (grad, weight) in enumerate(((gq, wq), (gk, wk), (gv, wv))):
        product = over_rows(unit, grad[...])
        column = row_sum(grad[...].astype(F32))
        if place > 0:
            product = product + over_rows(far_low, edges[place - 1])
            column = column + row_sum(edges[place - 1].astype(F32))
        lanes = slice(place * width, (place + 1) * width)
        keep_out[:, lanes], send_out[:, lanes] = halves(
            product * gain_column + shift_column * column, core
        )
        wide = weight[...].astype(F32)
        by_gain = by_gain + jnp.sum(wide * product, axis=1, keepdims=True)
        by_shift = by_shift + jnp.sum(wide * column, axis=1, keepdims=True)
        if place != 1:
            sums[place // 2 : place // 2 + 1] = column
    sums[2:3] = jnp.transpose(jnp.broadcast_to(by_gain, (width, 128)))[:1]
    sums[3:4] = jnp.transpose(jnp.broadcast_to(by_shift, (width, 128)))[:1]
    vec[...] = jnp.zeros_like(vec)
    row = 0
    for ref in [sums.at[i : i + 1] for i in range(4)] + [gmb, gfg, gfs, gdb, gub]:
        for part in range(0, ref.shape[1], 128):
            vec[row : row + 1] = ref[:, part : part + 128]
            row += 1
    keep_out[:, 3 * width :], send_out[:, 3 * width :] = halves(vec[...], core)

    grad = against(edges[0], wk[...]) + against(edges[1], wv[...])
    far_edge = norm_back(grad * gain[...], far_unit, far_inverse)
    far_edge_out[...] = jnp.zeros_like(far_edge_out)
    far_edge_out[EDGE - LEFT : EDGE] = far_edge[:LEFT]
    far_edge_out[EDGE : EDGE + RIGHT] = far_edge[LEFT:]
    stores = []
    for rows in tiles(count):
        unit, inverse = norm_parts(x[rows, :].astype(F32))
        grad = (
            against(gq[rows, :], wq[...])
            + against(gk[rows, :], wk[...])
            + against(gv[rows, :], wv[...])
        )
        result = gr[rows, :] + norm_back(grad * gain[...], unit, inverse)
        ig[rows, :] = result.astype(BF16)
        stores.append(
            pltpu.make_async_copy(
                ig.at[rows, :], ig_out.at[rows, :], tile_sems.at[len(stores)]
            )
        )
        stores[-1].start()
        if rows.start == 0:
            own_edge_out[:EDGE] = result[:EDGE]
        if rows.stop == count:
            own_edge_out[EDGE:] = result[-EDGE:]
    for store in stores:
        store.wait()


def swapped(value, axis, mask):
    count = lax.axis_size(axis)
    return lax.ppermute(value, axis, [(i, i ^ mask) for i in range(count)])


def across(value, first):
    tm, items = lax.axis_size("tm"), lax.axis_size("items")
    pairs = []
    for i in range(tm):
        for j in range(items):
            along_x = (i % 2 == 0) == first
            pairs.append((i * items + j, i * items + (j ^ 1) if along_x else (i ^ 2) * items + j))
    return lax.ppermute(value, ("tm", "items"), pairs)


def cut(value, place, rows):
    return lax.dynamic_slice_in_dim(value, place * rows, rows, 0)


def total_of(parts):
    total = parts[0].astype(F32)
    for part in parts[1:]:
        total = total + part.astype(F32)
    return total.astype(BF16)


def paired(own, got, bit):
    return jnp.where(bit == 0, jnp.concatenate([own, got]), jnp.concatenate([got, own]))


class Place:
    def __init__(self):
        tm = lax.axis_index("tm").astype(jnp.int32)
        x_bit = lax.axis_index("items").astype(jnp.int32) % 2
        y_bit = (tm // 2) % 2
        self.core = tm % 2
        self.steps = [
            (jnp.where(self.core == 0, x_bit, y_bit), lambda value: across(value, True)),
            (jnp.where(self.core == 0, y_bit, x_bit), lambda value: across(value, False)),
            ((tm // 4) % 2, lambda value: swapped(value, "tm", 4)),
            ((tm // 8) % 2, lambda value: swapped(value, "tm", 8)),
        ]


class Sum:
    def __init__(self, place, halved, keep, send):
        self.place = place
        self.parts = [keep, swapped(send, "tm", 1)]
        self.todo = [functools.partial(self.exchange, step, step < halved) for step in range(4)]
        self.todo += [functools.partial(self.spread, step) for step in range(halved - 1, -1, -1)]
        self.todo += [functools.partial(self.spread, -1)]
        self.bit = None

    def held(self):
        return self.parts[0]

    def hold(self, value):
        self.parts[0] = value

    def advance(self):
        self.todo.pop(0)()

    def exchange(self, step, halve):
        bit, exchange = self.place.steps[step]
        if halve:
            rows = self.parts[0].shape[0] // 2
            mine, other = (
                total_of([cut(part, at, rows) for part in self.parts]) for at in (bit, 1 - bit)
            )
        else:
            mine = other = total_of(self.parts)
        self.parts = [mine, exchange(other)]

    def spread(self, step):
        own = total_of(self.parts) if self.bit is None else paired(*self.parts, self.bit)
        if step >= 0:
            self.bit, exchange = self.place.steps[step]
            self.parts = [own, exchange(own)]
        else:
            self.parts = [own, swapped(own, "tm", 1)]

    def whole(self):
        own, got = self.parts
        low = self.place.core == 0
        return jnp.where(low, own, got), jnp.where(low, got, own)


class PlainSum:
    def __init__(self, place, halved, keep, send):
        self.place = place
        self.parts = [keep, send]

    def held(self):
        return self.parts[0]

    def hold(self, value):
        self.parts[0] = value

    def advance(self):
        pass

    def whole(self):
        return lax.psum(Sum.whole(self), ("tm", "items"))


def stays(array):
    return pltpu.with_memory_space_constraint(array, pltpu.HBM)


def here(array):
    return pltpu.with_memory_space_constraint(array, pltpu.VMEM)


def ordered(first, second):
    return lax.optimization_barrier((first, second))[1]


def follow(first, second):
    second.hold(ordered(first.held(), second.held()))


def passed_along(x, by):
    count = lax.axis_size("tm")
    return lax.ppermute(x, "tm", [(i, i + by) for i in range(count) if 0 <= i + by < count])


def local(
    fast,
    frames,
    out_grad,
    item_lengths,
    domain_tags,
    domain_weight,
    wq,
    bq,
    wk,
    wv,
    bv,
    wmix,
    bmix,
    again,
    ashift,
    fgain,
    fshift,
    wup,
    bup,
    wdown,
    bdown,
):
    frames = frames[0]
    out_grad = out_grad[0]
    count, width = frames.shape
    ffw = wup.shape[1]
    slots = item_lengths.shape[1]
    stream_len = count * lax.axis_size("tm")
    reach = count + WINDOW - SUB
    unit_flops = 2 * count * width * width
    parts = ffw // width
    bq, bv, bmix, again, ashift, fgain, fshift, bup, bdown = (
        vector[None] for vector in (bq, bv, bmix, again, ashift, fgain, fshift, bup, bdown)
    )
    place = Place()
    where = jnp.stack([lax.axis_index("tm") * count, place.core]).astype(jnp.int32)
    before = passed_along(frames[count - EDGE :], 1)
    behind = passed_along(frames[:EDGE], -1)
    kind = Sum if fast else PlainSum
    vector = free(1, width, F32)
    edge_wide = free(2 * EDGE, width, F32)
    model_low = (count, width, BF16)
    model_wide = (count, width, F32)
    hidden_low = (count, ffw, BF16)
    blocks = (2 * count // SUB, WINDOW, GROUP * SUB, BF16)
    windowed = (reach, width)

    q, k, v = call(
        project_body,
        "project",
        [stays(a) for a in (frames, again, ashift, wq, wk, wv, bq, bv)],
        [near(*model_low)] * 3,
        flops=3 * unit_flops,
        moved=6 * MIB,
    )
    (
        probs,
        q,
        keys,
        values,
        active,
        resid,
        gr,
        gm,
        keep_d,
        send_d,
        keep_u,
        send_u,
        gdb,
        gub,
        gmb,
        gfg,
        gfs,
    ) = call(
        functools.partial(forward_body, stream_len),
        "forward",
        [frames, out_grad, q, k, v, before, behind, item_lengths, domain_tags]
        + [again, ashift, wk, wv, bv, wmix, bmix, fgain, fshift, wup, bup, wdown],
        [copied(*blocks), copied(*model_low), copied(*windowed, BF16), copied(*windowed, BF16)]
        + [copied(*hidden_low), copied(*model_wide), copied(*model_wide), copied(*model_low)]
        + [near(width // 2, ffw, BF16)] * 2
        + [near(width // 2, ffw + width, BF16)] * 2
        + [vector, free(1, ffw, F32), vector, vector, vector],
        scratch=[
            pltpu.VMEM(windowed, BF16),
            pltpu.VMEM(windowed, BF16),
            pltpu.VMEM((1, slots), F32),
            pltpu.VMEM((slots, 1), F32),
            pltpu.VMEM(blocks[:-1], BF16),
            pltpu.VMEM((count, width), BF16),
            pltpu.VMEM((count, width), F32),
            pltpu.VMEM((count, 128), F32),
            pltpu.VMEM((count, width), BF16),
            pltpu.VMEM((count, width), BF16),
            pltpu.VMEM((count, ffw), BF16),
            pltpu.VMEM((count, width), BF16),
            pltpu.VMEM((count, ffw), BF16),
            pltpu.VMEM((count, width), F32),
            pltpu.VMEM((count, width), BF16),
            pltpu.SemaphoreType.DMA((7,)),
            pltpu.SemaphoreType.DMA((parts,)),
        ],
        scalars=[where, domain_weight],
        vmem=36,
        flops=(6 + 5 * parts) * unit_flops,
        moved=24 * MIB,
    )
    down = kind(place, 3, keep_d, send_d)
    up = kind(place, 3, keep_u, send_u)

    (output,) = call(
        output_body,
        "output",
        [stays(a) for a in (resid, active, wdown, bdown)],
        [far(*model_low)],
        vmem=20,
        flops=parts * unit_flops,
        moved=9 * MIB,
    )
    down.hold(ordered(output, down.held()))
    down.advance()
    follow(down, up)
    up.advance()
    gm = ordered(up.held(), gm)
    rest_half = near(width // 2, 3 * width + 128, BF16)
    low_scratch = pltpu.VMEM((count, width), BF16)
    keep_r, send_r, own_edge, far_edge, ig = call(
        backward_body,
        "backward",
        [stays(a) for a in (q, probs, gm, keys, values)]
        + [before, behind, again, ashift, gdb, gub, gmb, gfg, gfs],
        [rest_half, rest_half, edge_wide, edge_wide, copied(*model_low)],
        scratch=[low_scratch, pltpu.VMEM((count, width), F32)]
        + [pltpu.VMEM((width, width), BF16)] * 3
        + [pltpu.VMEM(windowed, F32)] * 2
        + [low_scratch] * 4
        + [pltpu.VMEM((8, width), F32), pltpu.VMEM((width, 128), F32)]
        + [pltpu.SemaphoreType.DMA((5,)), pltpu.SemaphoreType.DMA((count // TILE,))],
        scalars=[where],
        far_ins=[stays(a) for a in (frames, gr, wq, wk, wv)],
        vmem=36,
        flops=14 * unit_flops,
        moved=12 * MIB,
    )
    rest = kind(place, 2, keep_r, send_r)
    down.hold(ordered(keep_r, down.held()))
    order = [down, up, rest] * 5
    for turn, one in enumerate(order):
        if turn > 0:
            follow(order[turn - 1], one)
        one.advance()
        if turn == 8:
            far_edge = ordered(one.held(), far_edge)
            from_behind = passed_along(far_edge[:EDGE], -1)
            from_before = passed_along(far_edge[EDGE:], 1)
    ig = ig.at[:EDGE].set((own_edge[:EDGE] + from_before).astype(BF16))
    ig = ig.at[count - EDGE :].set((own_edge[EDGE:] + from_behind).astype(BF16))
    follow(rest, down)
    down.advance()
    follow(down, up)
    up.advance()
    follow(up, rest)
    rest.advance()
    follow(rest, down)
    down.advance()
    follow(down, up)
    up.advance()
    low, high = down.whole()
    grad_down = jnp.concatenate(
        [rows[:, part : part + width] for part in range(0, ffw, width) for rows in (low, high)],
        axis=0,
    ).astype(F32)
    rest.hold(ordered(grad_down, rest.held()))
    rest.advance()
    upper = jnp.concatenate(up.whole(), axis=0).astype(F32)
    grad_up, grad_mix = upper[:, :ffw], upper[:, ffw:]
    rest = jnp.concatenate(rest.whole(), axis=0).astype(F32)
    grad_q, grad_k, grad_v = (rest[:, i * width : (i + 1) * width] for i in range(3))
    vectors = rest[: 12 * width // 128, 3 * width :].reshape(-1)
    gqb, gvb, gag, gas, gmb, gfg, gfs, gdb = (
        vectors[i * width : (i + 1) * width] for i in range(8)
    )
    gub = vectors[8 * width :]
    return (
        output[None],
        ig[None],
        grad_q,
        gqb,
        grad_k,
        grad_v,
        gvb,
        grad_mix,
        gmb,
        gag,
        gas,
        gfg,
        gfs,
        grad_up,
        gub,
        grad_down,
        gdb,
    )


def solution(mesh):
    rows = P("items", "tm", None)
    in_specs = (rows, rows, P("items", None), P("items", None)) + (P(),) * 16
    out_specs = (rows, rows) + (P(),) * 15
    fast = mesh.shape["tm"] == 16 and mesh.shape["items"] == 2
    return jax.shard_map(
        functools.partial(local, fast),
        mesh=mesh,
        in_specs=in_specs,
        out_specs=out_specs,
        check_vma=False,
    )
```

```python
import functools
import math

import jax
import jax.numpy as jnp
from jax import lax
from jax.experimental import pallas as pl
from jax.experimental.pallas import tpu as pltpu
from jax.sharding import PartitionSpec as P

HEADS = 8
LEFT = 10
RIGHT = 2
EDGE = 16
TILE = 256
SUB = 32
WINDOW = 48
GROUP = 4
MIB = 1 << 20
ORDER = "durdudrunrdurdeurdruoirdudru"
LOG2E = 1.0 / math.log(2.0)
F32 = jnp.float32
BF16 = jnp.bfloat16


def dot(left, right):
    return jnp.dot(left, right, preferred_element_type=F32)


def against(left, right):
    return lax.dot_general(left, right, (((1,), (1,)), ((), ())), preferred_element_type=F32)


def over_rows(left, right):
    return lax.dot_general(left, right, (((0,), (0,)), ((), ())), preferred_element_type=F32)


def norm_parts(values):
    centered = values - jnp.mean(values, axis=-1, keepdims=True)
    variance = jnp.mean(centered * centered, axis=-1, keepdims=True)
    inverse = lax.rsqrt(variance + 1e-05)
    return centered * inverse, inverse


def norm_back(upstream, unit, inverse):
    return inverse * (
        upstream
        - jnp.mean(upstream, axis=-1, keepdims=True)
        - unit * jnp.mean(upstream * unit, axis=-1, keepdims=True)
    )


def row_sum(values):
    return jnp.sum(values, axis=0, keepdims=True)


def scaled_rows(values, weight):
    return values.astype(F32) * jnp.tile(weight, (1, values.shape[1] // 128))


def halves(values, core):
    rows = values.shape[0] // 2
    low, high = values[:rows].astype(BF16), values[rows:].astype(BF16)
    return jnp.where(core == 0, low, high), jnp.where(core == 0, high, low)


def tiles(count, rows=TILE):
    return [slice(start, start + rows) for start in range(0, count, rows)]


def shaped(shape, dtype):
    return jax.ShapeDtypeStruct(shape, dtype)


ANY = pl.BlockSpec(memory_space=pl.ANY)
SCALARS = pl.BlockSpec(memory_space=pltpu.SMEM)
WHOLE = pl.BlockSpec(memory_space=pltpu.VMEM)


def call(body, name, ins, outs, scratch=(), scalars=(), far_ins=(), vmem=10, flops=0, moved=0):
    return pl.pallas_call(
        body,
        in_specs=[SCALARS] * len(scalars) + [WHOLE] * len(ins) + [ANY] * len(far_ins),
        out_specs=[ANY if own_copies else WHOLE for _, own_copies in outs],
        out_shape=[out for out, _ in outs],
        scratch_shapes=list(scratch),
        name=name,
        compiler_params=pltpu.CompilerParams(vmem_limit_bytes=vmem * MIB),
        cost_estimate=pl.CostEstimate(flops=flops, bytes_accessed=moved, transcendentals=0),
    )(*scalars, *ins, *far_ins)


def near(*shape):
    return pltpu.VMEM(shape[:-1], shape[-1]), False


def copied(*shape):
    return pltpu.HBM(shape[:-1], shape[-1]), True


def free(*shape):
    return shaped(shape[:-1], shape[-1]), False


def project_body(x, gain, shift, wq, wk, wv, bq, bv, q_out, k_out, v_out):
    scale = (wq.shape[1] // HEADS) ** (-0.5)
    for rows in tiles(x.shape[0]):
        unit, _ = norm_parts(x[rows, :].astype(F32))
        normed = (unit * gain[...] + shift[...]).astype(BF16)
        q_out[rows, :] = (dot(normed, wq[...]) + bq[...]).astype(BF16) * jnp.asarray(scale, BF16)
        k_out[rows, :] = dot(normed, wk[...]).astype(BF16)
        v_out[rows, :] = (dot(normed, wv[...]) + bv[...]).astype(BF16)


def slot_ends(lengths):
    slots = lengths.shape[1]
    low = lax.broadcasted_iota(jnp.int32, (slots, slots), 0)
    high = lax.broadcasted_iota(jnp.int32, (slots, slots), 1)
    along = jnp.sum(jnp.where(low == high, lengths, 0.0), axis=1, keepdims=True)
    ends_column = jnp.sum(jnp.where(high <= low, lengths, 0.0), axis=1, keepdims=True)
    ends_row = jnp.sum(jnp.where(low <= high, along, 0.0), axis=0, keepdims=True)
    return ends_row, ends_column


def head_lanes(dtype):
    lane = lax.broadcasted_iota(jnp.int32, (1, 128), 1)
    return [(lane < 64).astype(F32).astype(dtype), (lane >= 64).astype(F32).astype(dtype)]


def stacked(values, masks):
    low, high = values[:, :128], values[:, 128:]
    none = jnp.zeros_like(low)
    return jnp.concatenate(
        [
            jnp.concatenate([low * masks[0], none], axis=1),
            jnp.concatenate([low * masks[1], none], axis=1),
            jnp.concatenate([none, high * masks[0]], axis=1),
            jnp.concatenate([none, high * masks[1]], axis=1),
        ],
        axis=0,
    )


def unstacked(values):
    rows = values.shape[0] // GROUP
    first = lax.broadcasted_iota(jnp.int32, (rows, 128), 1) < 64
    low = jnp.where(first, values[:rows, :128], values[rows : 2 * rows, :128])
    high = jnp.where(first, values[2 * rows : 3 * rows, 128:], values[3 * rows :, 128:])
    return jnp.concatenate([low, high], axis=1)


def neighbours(core, near_rows, far_rows):
    one, other = near_rows[...], far_rows[...]
    return jnp.where(core == 0, other, one), jnp.where(core == 0, one, other)


def fill_window(store, edge, own, count):
    store[:LEFT] = edge[EDGE - LEFT : EDGE]
    store[LEFT : LEFT + count] = own
    store[LEFT + count :] = edge[EDGE : EDGE + store.shape[0] - LEFT - count]


def forward_body(
    stream_len,
    where,
    domain,
    q,
    k,
    v,
    near_rows,
    far_rows,
    lengths,
    tags,
    gain,
    shift,
    wk,
    wv,
    bv,
    bmix,
    fgain,
    fshift,
    bup,
    x_in,
    wmix_in,
    out_grad_in,
    wup_in,
    wdown_in,
    probs_out,
    q_out,
    keys_out,
    values_out,
    active_out,
    resid_out,
    gr_out,
    gm_out,
    keep_d_out,
    send_d_out,
    keep_u_out,
    send_u_out,
    gdb_out,
    gub_out,
    gmb_out,
    gfg_out,
    gfs_out,
    keys,
    values,
    ends_row,
    ends_column,
    probs,
    mixed,
    resid,
    weight,
    nffn,
    branch,
    active,
    slope,
    gh,
    gr,
    gm,
    x,
    wmix,
    out_grad,
    wup,
    wdown,
    sems,
    block_sems,
    load_sems,
):
    count, width = q.shape
    ffw = wup.shape[1]
    half = width // 2
    first = where[0]
    core = where[1]
    copies = []
    loads = []
    for source, target in (
        (x_in, x),
        (wmix_in, wmix),
        (out_grad_in, out_grad),
        (wup_in, wup),
        (wdown_in, wdown),
    ):
        loads.append(pltpu.make_async_copy(source, target, load_sems.at[len(loads)]))
        loads[-1].start()

    def carry_out(source, target):
        copies.append(pltpu.make_async_copy(source, target, sems.at[len(copies)]))
        copies[-1].start()

    carry_out(q, q_out)
    edge = jnp.concatenate(neighbours(core, near_rows, far_rows), axis=0).astype(F32)
    unit, _ = norm_parts(edge)
    normed = (unit * gain[...] + shift[...]).astype(BF16)
    fill_window(keys, dot(normed, wk[...]).astype(BF16), k[...], count)
    fill_window(values, (dot(normed, wv[...]) + bv[...]).astype(BF16), v[...], count)
    carry_out(keys, keys_out)
    carry_out(values, values_out)
    row, column = slot_ends(lengths[...].astype(F32))
    ends_row[...] = row
    ends_column[...] = column

    kinds = tags[...]
    slot_weight = jnp.where(kinds == 0, domain[0], 0.0)
    slot_weight = jnp.where(kinds == 1, domain[1], slot_weight)
    slot_weight = jnp.where(kinds == 2, domain[2], slot_weight)
    slots = kinds.shape[1]
    slot = lax.broadcasted_iota(jnp.int32, (TILE, slots), 1).astype(F32)
    masks = head_lanes(BF16)
    lanes_all = GROUP * SUB
    key_at = lax.broadcasted_iota(jnp.int32, (WINDOW, lanes_all), 0)
    query_at = lax.broadcasted_iota(jnp.int32, (WINDOW, lanes_all), 1) % SUB
    near = (key_at >= query_at) & (key_at <= query_at + LEFT + RIGHT)

    def one_tile(step, carried):
        tile_at = pl.multiple_of(step * TILE, TILE)
        places = (first + tile_at + lax.broadcasted_iota(jnp.int32, (TILE, 1), 0)).astype(F32)
        seg = jnp.sum((ends_row[...] <= places).astype(F32), axis=1, keepdims=True)
        weight[pl.ds(tile_at, TILE), :] = jnp.broadcast_to(
            jnp.sum(jnp.where(seg == slot, slot_weight, 0.0), axis=1, keepdims=True),
            (TILE, weight.shape[1]),
        )
        allowed, scores, pieces = [], [], []
        for sub in range(TILE // SUB):
            at = first + tile_at + sub * SUB
            ours = (at + lax.broadcasted_iota(jnp.int32, (1, lanes_all), 1) % SUB).astype(F32)
            others = (at - LEFT + lax.broadcasted_iota(jnp.int32, (WINDOW, 1), 0)).astype(F32)
            seg_ours = jnp.sum((ends_column[...] <= ours).astype(F32), axis=0, keepdims=True)
            seg_others = jnp.sum((ends_row[...] <= others).astype(F32), axis=1, keepdims=True)
            seg_others = jnp.where(others < 0.0, -1.0, seg_others)
            seg_others = jnp.where(others >= float(stream_len), -2.0, seg_others)
            allowed.append(near & (seg_ours == seg_others))
            for group in range(2):
                pieces.append((sub, group))
        for sub, group in pieces:
            start = pl.multiple_of(tile_at + sub * SUB, SUB)
            lanes = slice(group * half, (group + 1) * half)
            queries = stacked(q[pl.ds(start, SUB), lanes], masks)
            scores.append(against(keys[pl.ds(start, WINDOW), lanes], queries))
        lows = []
        for (sub, group), score in zip(pieces, scores):
            score = jnp.where(allowed[sub], score, -1e30)
            grown = jnp.exp(score - jnp.max(score, axis=0, keepdims=True))
            low = (grown * (1.0 / jnp.sum(grown, axis=0, keepdims=True))).astype(BF16)
            probs[2 * (step * (TILE // SUB) + sub) + group] = low
            lows.append(low)
        for (sub, group), low in zip(pieces, lows):
            start = pl.multiple_of(tile_at + sub * SUB, SUB)
            lanes = slice(group * half, (group + 1) * half)
            heads = unstacked(over_rows(low, values[pl.ds(start, WINDOW), lanes]))
            mixed[pl.ds(start, SUB), lanes] = heads.astype(BF16)
        return carried

    lax.fori_loop(0, count // TILE, one_tile, 0)
    carry_out(probs, probs_out)
    for load in loads:
        load.wait()
    bias = jnp.zeros((1, width), F32)
    for rows in tiles(count):
        summed = x[rows, :].astype(F32) + dot(mixed[rows, :], wmix[...]) + bmix[...]
        resid[rows, :] = summed
        unit, _ = norm_parts(summed)
        nffn[rows, :] = (unit * fgain[...] + fshift[...]).astype(BF16)
        scaled = scaled_rows(out_grad[rows, :], weight[rows, :]).astype(BF16)
        branch[rows, :] = scaled
        bias = bias + row_sum(scaled.astype(F32))
    gdb_out[...] = bias
    carry_out(resid, resid_out)

    def one_block(block, carried):
        at = pl.multiple_of(block * width, width)
        lanes = pl.ds(at, width)
        for rows in tiles(count):
            hidden = dot(nffn[rows, :], wup[:, lanes]) + bup[:, lanes]
            below = 1.0 + lax.erf(hidden * math.sqrt(0.5))
            bell = jnp.exp2(
                hidden * hidden * (-0.5 * LOG2E) + math.log2(2.0 / math.sqrt(2.0 * math.pi))
            )
            active[rows, lanes] = ((hidden * 0.5) * below).astype(BF16)
            slope[rows, :] = (below + hidden * bell).astype(BF16)
        pltpu.make_async_copy(
            active.at[:, lanes], active_out.at[:, lanes], block_sems.at[block]
        ).start()
        keep_d_out[:, lanes], send_d_out[:, lanes] = halves(
            over_rows(active[:, lanes], branch[...]), core
        )
        bias = jnp.zeros((1, width), F32)
        for rows in tiles(count):
            half_branch = branch[rows, :] * jnp.asarray(0.5, BF16)
            grad = against(half_branch, wdown[lanes, :]) * slope[rows, :].astype(F32)
            low = grad.astype(BF16)
            gh[rows, lanes] = low
            bias = bias + row_sum(low.astype(F32))
        gub_out[:, lanes] = bias
        keep_u_out[:, lanes], send_u_out[:, lanes] = halves(
            over_rows(nffn[...], gh[:, lanes]), core
        )
        return carried

    lax.fori_loop(0, ffw // width, one_block, 0)
    by_bias, by_gain, by_shift = (jnp.zeros((1, width), F32) for _ in range(3))
    for rows in tiles(count):
        grad = against(gh[rows, :], wup[...])
        unit, inverse = norm_parts(resid[rows, :])
        by_gain = by_gain + row_sum(grad * unit)
        by_shift = by_shift + row_sum(grad)
        grad_resid = scaled_rows(out_grad[rows, :], weight[rows, :]) + norm_back(
            grad * fgain[...], unit, inverse
        )
        gr[rows, :] = grad_resid
        low = grad_resid.astype(BF16)
        branch[rows, :] = low
        by_bias = by_bias + row_sum(low.astype(F32))
        gm[rows, :] = against(low, wmix[...]).astype(BF16)
    carry_out(gr, gr_out)
    carry_out(gm, gm_out)
    there = slice(ffw, ffw + width)
    keep_u_out[:, there], send_u_out[:, there] = halves(over_rows(mixed[...], branch[...]), core)
    gmb_out[...] = by_bias
    gfg_out[...] = by_gain
    gfs_out[...] = by_shift
    for block in range(ffw // width):
        lanes = slice(block * width, (block + 1) * width)
        copies.append(
            pltpu.make_async_copy(
                active.at[:, lanes], active_out.at[:, lanes], block_sems.at[block]
            )
        )
    for copy in copies:
        copy.wait()


def output_body(bdown, wdown_in, resid_in, active_in, out, wdown, resid, active, low, sems):
    steps = tiles(resid.shape[0])

    def moved(source, target, place):
        return pltpu.make_async_copy(source, target, sems.at[place])

    loads = [moved(wdown_in, wdown, 0)]
    for i, rows in enumerate(steps):
        loads.append(moved(active_in.at[rows, :], active.at[rows, :], 1 + 2 * i))
        loads.append(moved(resid_in.at[rows, :], resid.at[rows, :], 2 + 2 * i))
    for load in loads:
        load.start()
    loads[0].wait()
    stores = []
    for i, rows in enumerate(steps):
        loads[1 + 2 * i].wait()
        loads[2 + 2 * i].wait()
        low[rows, :] = (
            resid[rows, :] + dot(active[rows, :], wdown[...]) + bdown[...]
        ).astype(BF16)
        stores.append(moved(low.at[rows, :], out.at[rows, :], 1 + 2 * len(steps) + i))
        stores[-1].start()
    for store in stores:
        store.wait()


def attend_back_body(
    q,
    probs,
    gm,
    keys,
    values,
    gq,
    gk,
    gv,
    edge,
    gq_out,
    gk_out,
    gv_out,
    gk_window,
    gv_window,
    sems,
):
    count, width = q.shape
    half = width // 2
    gk_window[...] = jnp.zeros_like(gk_window)
    gv_window[...] = jnp.zeros_like(gv_window)
    scale = (width // HEADS) ** (-0.5)
    masks = head_lanes(BF16)
    pieces = [(sub, group) for sub in range(TILE // SUB) for group in range(2)]

    def one_tile(step, carried):
        tile_at = pl.multiple_of(step * TILE, TILE)

        def spot(sub, group):
            start = pl.multiple_of(tile_at + sub * SUB, SUB)
            return pl.ds(start, SUB), pl.ds(start, WINDOW), slice(group * half, (group + 1) * half)

        pulls, grads = [], []
        for sub, group in pieces:
            rows, window, lanes = spot(sub, group)
            pulled = stacked(gm[rows, lanes], masks)
            pulls.append(pulled)
            grads.append(against(values[window, lanes], pulled))
        lows = []
        for (sub, group), grad in zip(pieces, grads):
            wide = probs[2 * (step * (TILE // SUB) + sub) + group].astype(F32)
            product = wide * grad
            lows.append((product - wide * jnp.sum(product, axis=0, keepdims=True)).astype(BF16))
        for (sub, group), pulled, low in zip(pieces, pulls, lows):
            rows, window, lanes = spot(sub, group)
            queries = stacked(q[rows, lanes], masks)
            gq[rows, lanes] = (unstacked(over_rows(low, keys[window, lanes])) * scale).astype(BF16)
            gk_window[window, lanes] += dot(low, queries)
            gv_window[window, lanes] += dot(
                probs[2 * (step * (TILE // SUB) + sub) + group], pulled
            )
        return carried

    lax.fori_loop(0, count // TILE, one_tile, 0)
    stores = []

    def store(source, target):
        stores.append(pltpu.make_async_copy(source, target, sems.at[len(stores)]))
        stores[-1].start()

    store(gq, gq_out)
    for place, (window, grad, out) in enumerate(
        ((gk_window, gk, gk_out), (gv_window, gv, gv_out))
    ):
        lanes = slice(place * width, (place + 1) * width)
        grad[...] = window[LEFT : LEFT + count].astype(BF16)
        store(grad, out)
        edge[:LEFT, lanes] = window[:LEFT].astype(BF16)
        edge[LEFT : LEFT + RIGHT, lanes] = window[LEFT + count : LEFT + count + RIGHT].astype(BF16)
    for one in stores:
        one.wait()


def edge_frames(core, near_rows, far_rows):
    before, behind = neighbours(core, near_rows, far_rows)
    return jnp.concatenate([before[EDGE - LEFT :], behind[:RIGHT]], axis=0).astype(F32)


def weights_body(
    where,
    gq,
    gk,
    gv,
    edge,
    near_rows,
    far_rows,
    gain,
    shift,
    gdb,
    gub,
    gmb,
    gfg,
    gfs,
    x_in,
    wq_in,
    wk_in,
    wv_in,
    keep_out,
    send_out,
    x,
    wq,
    wk,
    wv,
    sums,
    vec,
    sems,
):
    width = x.shape[1]
    core = where[1]
    loads = []
    for source, target in ((x_in, x), (wq_in, wq), (wk_in, wk), (wv_in, wv)):
        loads.append(pltpu.make_async_copy(source, target, sems.at[len(loads)]))
        loads[-1].start()
    far_low = norm_parts(edge_frames(core, near_rows, far_rows))[0].astype(BF16)
    gain_column = jnp.transpose(jnp.broadcast_to(gain[...], (128, width)))[:, :1]
    shift_column = jnp.transpose(jnp.broadcast_to(shift[...], (128, width)))[:, :1]
    for load in loads:
        load.wait()
    unit = norm_parts(x[...].astype(F32))[0].astype(BF16)
    by_gain = jnp.zeros((width, 1), F32)
    by_shift = jnp.zeros((width, 1), F32)
    for place, (grad, weight) in enumerate(((gq, wq), (gk, wk), (gv, wv))):
        product = over_rows(unit, grad[...])
        column = row_sum(grad[...].astype(F32))
        if place > 0:
            there = slice((place - 1) * width, place * width)
            product = product + over_rows(far_low, edge[: LEFT + RIGHT, there])
            column = column + row_sum(edge[: LEFT + RIGHT, there].astype(F32))
        lanes = slice(place * width, (place + 1) * width)
        keep_out[:, lanes], send_out[:, lanes] = halves(
            product * gain_column + shift_column * column, core
        )
        wide = weight[...].astype(F32)
        by_gain = by_gain + jnp.sum(wide * product, axis=1, keepdims=True)
        by_shift = by_shift + jnp.sum(wide * column, axis=1, keepdims=True)
        if place != 1:
            sums[place // 2 : place // 2 + 1] = column
    sums[2:3] = jnp.transpose(jnp.broadcast_to(by_gain, (width, 128)))[:1]
    sums[3:4] = jnp.transpose(jnp.broadcast_to(by_shift, (width, 128)))[:1]
    vec[...] = jnp.zeros_like(vec)
    row = 0
    for ref in [sums.at[i : i + 1] for i in range(4)] + [gmb, gfg, gfs, gdb, gub]:
        for part in range(0, ref.shape[1], 128):
            vec[row : row + 1] = ref[:, part : part + 128]
            row += 1
    keep_out[:, 3 * width :], send_out[:, 3 * width :] = halves(vec[...], core)


def input_body(
    where,
    x,
    gq,
    gk,
    gv,
    gr,
    edge,
    near_rows,
    far_rows,
    gain,
    wq,
    wk,
    wv,
    own_edge_out,
    near_edge_out,
    far_edge_out,
    ig_out,
    ig,
    sems,
):
    count, width = x.shape
    core = where[1]
    unit, inverse = norm_parts(edge_frames(core, near_rows, far_rows))
    cut = slice(0, LEFT + RIGHT)
    grad = against(edge[cut, :width], wk[...]) + against(edge[cut, width:], wv[...])
    grad = norm_back(grad * gain[...], unit, inverse)
    before = jnp.concatenate([jnp.zeros((EDGE - LEFT, width), F32), grad[:LEFT]], axis=0)
    behind = jnp.concatenate([grad[LEFT:], jnp.zeros((EDGE - RIGHT, width), F32)], axis=0)
    near_edge_out[...] = jnp.where(core == 0, behind, before)
    far_edge_out[...] = jnp.where(core == 0, before, behind)
    stores = []
    for rows in tiles(count):
        unit, inverse = norm_parts(x[rows, :].astype(F32))
        grad = (
            against(gq[rows, :], wq[...])
            + against(gk[rows, :], wk[...])
            + against(gv[rows, :], wv[...])
        )
        result = gr[rows, :] + norm_back(grad * gain[...], unit, inverse)
        ig[rows, :] = result.astype(BF16)
        stores.append(
            pltpu.make_async_copy(
                ig.at[rows, :], ig_out.at[rows, :], sems.at[len(stores)]
            )
        )
        stores[-1].start()
        if rows.start == 0:
            own_edge_out[:EDGE] = result[:EDGE]
        if rows.stop == count:
            own_edge_out[EDGE:] = result[-EDGE:]
    for store in stores:
        store.wait()


def swapped(value, axis, mask):
    count = lax.axis_size(axis)
    return lax.ppermute(value, axis, [(i, i ^ mask) for i in range(count)])


def across(value, first):
    tm, items = lax.axis_size("tm"), lax.axis_size("items")
    pairs = []
    for i in range(tm):
        for j in range(items):
            along_x = (i % 2 == 0) == first
            pairs.append((i * items + j, i * items + (j ^ 1) if along_x else (i ^ 2) * items + j))
    return lax.ppermute(value, ("tm", "items"), pairs)


def cut(value, place, rows):
    return lax.dynamic_slice_in_dim(value, place * rows, rows, 0)


def total_of(parts):
    total = parts[0].astype(F32)
    for part in parts[1:]:
        total = total + part.astype(F32)
    return total.astype(BF16)


def paired(own, got, bit):
    return jnp.where(bit == 0, jnp.concatenate([own, got]), jnp.concatenate([got, own]))


def whole_body(places, where, own, got, *outs):
    blocks, (lane, first) = places
    rows = own.shape[0]
    for place, part in ((where[1], own), (1 - where[1], got)):
        for out, start, row in blocks:
            width = outs[out].shape[1]
            outs[out][pl.ds(pl.multiple_of(row + place * rows, rows), rows), :] = part[
                :, start : start + width
            ].astype(F32)
    if first < len(outs):
        count = sum(out.shape[1] for out in outs[first:]) // 128
        low = jnp.where(where[1] == 0, own[:count, lane:], got[:count, lane:]).astype(F32)
        row = 0
        for out in outs[first:]:
            for at in range(0, out.shape[1], 128):
                out[:, at : at + 128] = low[row : row + 1]
                row += 1


class Place:
    def __init__(self):
        tm = lax.axis_index("tm").astype(jnp.int32)
        x_bit = lax.axis_index("items").astype(jnp.int32) % 2
        y_bit = (tm // 2) % 2
        self.core = tm % 2
        self.steps = [
            (jnp.where(self.core == 0, x_bit, y_bit), lambda value: across(value, True)),
            (jnp.where(self.core == 0, y_bit, x_bit), lambda value: across(value, False)),
            ((tm // 4) % 2, lambda value: swapped(value, "tm", 4)),
            ((tm // 8) % 2, lambda value: swapped(value, "tm", 8)),
        ]


class Sum:
    def __init__(self, place, halved, keep, send):
        self.place = place
        self.parts = [keep, swapped(send, "tm", 1)]
        self.todo = [functools.partial(self.exchange, step, step < halved) for step in range(4)]
        self.todo += [functools.partial(self.spread, step) for step in range(halved - 1, -1, -1)]
        self.todo += [functools.partial(self.spread, -1)]
        self.bit = None

    def held(self):
        return self.parts[0]

    def hold(self, value):
        self.parts[0] = value

    def advance(self):
        self.todo.pop(0)()

    def exchange(self, step, halve):
        bit, exchange = self.place.steps[step]
        if halve:
            rows = self.parts[0].shape[0] // 2
            mine, other = (
                total_of([cut(part, at, rows) for part in self.parts]) for at in (bit, 1 - bit)
            )
        else:
            mine = other = total_of(self.parts)
        self.parts = [mine, exchange(other)]

    def spread(self, step):
        own = total_of(self.parts) if self.bit is None else paired(*self.parts, self.bit)
        if step >= 0:
            self.bit, exchange = self.place.steps[step]
            self.parts = [own, exchange(own)]
        else:
            self.parts = [own, swapped(own, "tm", 1)]

    def whole(self, where, places, outs):
        return call(
            functools.partial(whole_body, places),
            "whole",
            self.parts,
            outs,
            scalars=[where],
            vmem=24,
            moved=6 * MIB,
        )


class PlainSum:
    def __init__(self, place, halved, keep, send):
        self.place = place
        self.todo = []
        self.parts = [keep, send]

    def held(self):
        return self.parts[0]

    def hold(self, value):
        self.parts[0] = value

    def advance(self):
        pass

    def whole(self, where, places, outs):
        keep, send = self.parts
        low = jnp.where(self.place.core == 0, keep, send)
        high = jnp.where(self.place.core == 0, send, keep)
        total = lax.psum(jnp.concatenate([low, high], axis=0), ("tm", "items"))
        blocks, vectors = places
        made = [[] for _, _ in outs]
        for out, lane, _ in blocks:
            made[out].append(total[:, lane : lane + outs[out][0].shape[1]])
        lane, first = vectors
        for out in range(first, len(outs)):
            size = outs[out][0].shape[1]
            start = sum(made_out[0].shape[1] // 128 for _, made_out in enumerate(made[first:out]))
            rows = total[start : start + size // 128, lane : lane + 128]
            made[out].append(rows.reshape(1, size))
        return [jnp.concatenate(parts, axis=0).astype(F32) for parts in made]


def stays(array):
    return pltpu.with_memory_space_constraint(array, pltpu.HBM)


def here(array):
    return pltpu.with_memory_space_constraint(array, pltpu.VMEM)


def ordered(first, second):
    return lax.optimization_barrier((first, second))[1]


def follow(first, second):
    second.hold(ordered(first.held(), second.held()))


def along(value):
    count = lax.axis_size("tm")
    pairs = [(i, i + 1) for i in range(1, count - 1, 2)]
    return lax.ppermute(value, "tm", pairs + [(to, of) for of, to in pairs])


def local(
    fast,
    frames,
    out_grad,
    item_lengths,
    domain_tags,
    domain_weight,
    wq,
    bq,
    wk,
    wv,
    bv,
    wmix,
    bmix,
    again,
    ashift,
    fgain,
    fshift,
    wup,
    bup,
    wdown,
    bdown,
):
    frames = frames[0]
    out_grad = out_grad[0]
    count, width = frames.shape
    ffw = wup.shape[1]
    slots = item_lengths.shape[1]
    stream_len = count * lax.axis_size("tm")
    reach = count + WINDOW - SUB
    unit_flops = 2 * count * width * width
    parts = ffw // width
    bq, bv, bmix, again, ashift, fgain, fshift, bup, bdown = (
        vector[None] for vector in (bq, bv, bmix, again, ashift, fgain, fshift, bup, bdown)
    )
    place = Place()
    where = jnp.stack([lax.axis_index("tm") * count, place.core]).astype(jnp.int32)
    near_end = jnp.where(place.core == 0, count - EDGE, 0)
    near_rows = swapped(lax.dynamic_slice_in_dim(frames, near_end, EDGE, 0), "tm", 1)
    far_rows = along(lax.dynamic_slice_in_dim(frames, count - EDGE - near_end, EDGE, 0))
    kind = Sum if fast else PlainSum
    vector = free(1, width, F32)
    edge_wide = free(2 * EDGE, width, F32)
    edge_half = free(EDGE, width, F32)
    model_low = (count, width, BF16)
    model_wide = (count, width, F32)
    hidden_low = (count, ffw, BF16)
    blocks = (2 * count // SUB, WINDOW, GROUP * SUB, BF16)
    windowed = (reach, width)

    q, k, v = call(
        project_body,
        "project",
        [stays(a) for a in (frames, again, ashift, wq, wk, wv, bq, bv)],
        [near(*model_low)] * 3,
        flops=3 * unit_flops,
        moved=6 * MIB,
    )
    (
        probs,
        q,
        keys,
        values,
        active,
        resid,
        gr,
        gm,
        keep_d,
        send_d,
        keep_u,
        send_u,
        gdb,
        gub,
        gmb,
        gfg,
        gfs,
    ) = call(
        functools.partial(forward_body, stream_len),
        "forward",
        [q, k, v, near_rows, far_rows]
        + [stays(a) for a in (item_lengths, domain_tags, again, ashift, wk, wv)]
        + [stays(a) for a in (bv, bmix, fgain, fshift, bup)],
        [copied(*blocks), copied(*model_low), copied(*windowed, BF16), copied(*windowed, BF16)]
        + [copied(*hidden_low), copied(*model_wide), copied(*model_wide), copied(*model_low)]
        + [near(width // 2, ffw, BF16)] * 2
        + [near(width // 2, ffw + width, BF16)] * 2
        + [vector, free(1, ffw, F32), vector, vector, vector],
        scratch=[
            pltpu.VMEM(windowed, BF16),
            pltpu.VMEM(windowed, BF16),
            pltpu.VMEM((1, slots), F32),
            pltpu.VMEM((slots, 1), F32),
            pltpu.VMEM(blocks[:-1], BF16),
            pltpu.VMEM((count, width), BF16),
            pltpu.VMEM((count, width), F32),
            pltpu.VMEM((count, 128), F32),
            pltpu.VMEM((count, width), BF16),
            pltpu.VMEM((count, width), BF16),
            pltpu.VMEM((count, ffw), BF16),
            pltpu.VMEM((count, width), BF16),
            pltpu.VMEM((count, ffw), BF16),
            pltpu.VMEM((count, width), F32),
            pltpu.VMEM((count, width), BF16),
            pltpu.VMEM((count, width), BF16),
            pltpu.VMEM((width, width), BF16),
            pltpu.VMEM((count, width), BF16),
            pltpu.VMEM((width, ffw), BF16),
            pltpu.VMEM((ffw, width), BF16),
            pltpu.SemaphoreType.DMA((7,)),
            pltpu.SemaphoreType.DMA((parts,)),
            pltpu.SemaphoreType.DMA((5,)),
        ],
        scalars=[where, domain_weight],
        far_ins=[stays(a) for a in (frames, wmix, out_grad, wup, wdown)],
        vmem=40,
        flops=(6 + 5 * parts) * unit_flops,
        moved=24 * MIB,
    )
    down = kind(place, 3, keep_d, send_d)
    up = kind(place, 3, keep_u, send_u)

    (gq, gk, gv, edge, gq_far, gk_far, gv_far) = call(
        attend_back_body,
        "attend_back",
        [stays(a) for a in (q, probs, gm, keys, values)],
        [near(*model_low)] * 3
        + [near(EDGE, 2 * width, BF16)]
        + [copied(*model_low)] * 3,
        scratch=[pltpu.VMEM(windowed, F32)] * 2 + [pltpu.SemaphoreType.DMA((3,))],
        vmem=20,
        flops=8 * unit_flops,
        moved=10 * MIB,
    )
    down.hold(ordered(edge, down.held()))
    down.advance()
    follow(down, up)
    up.advance()
    edge = ordered(up.held(), edge)
    rest_half = near(width // 2, 3 * width + 128, BF16)
    square_low = pltpu.VMEM((width, width), BF16)
    keep_r, send_r = call(
        weights_body,
        "weights",
        [gq, gk, gv, edge, near_rows, far_rows]
        + [stays(a) for a in (again, ashift)]
        + [gdb, gub, gmb, gfg, gfs],
        [rest_half, rest_half],
        scratch=[pltpu.VMEM((count, width), BF16)]
        + [square_low] * 3
        + [pltpu.VMEM((8, width), F32), pltpu.VMEM((width, 128), F32)]
        + [pltpu.SemaphoreType.DMA((4,))],
        scalars=[where],
        far_ins=[stays(a) for a in (frames, wq, wk, wv)],
        vmem=16,
        flops=3 * unit_flops,
        moved=8 * MIB,
    )
    rest = kind(place, 3, keep_r, send_r)
    sums = {"d": down, "u": up, "r": rest}
    latest = keep_r
    for turn in ORDER:
        if turn == "o":
            active = ordered(latest, active)
            (output,) = call(
                output_body,
                "output",
                [stays(bdown)],
                [copied(*model_low)],
                scratch=[
                    pltpu.VMEM((ffw, width), BF16),
                    pltpu.VMEM((count, width), F32),
                    pltpu.VMEM((count, ffw), BF16),
                    pltpu.VMEM((count, width), BF16),
                    pltpu.SemaphoreType.DMA((1 + 3 * (count // TILE),)),
                ],
                far_ins=[stays(a) for a in (wdown, resid, active)],
                vmem=20,
                flops=parts * unit_flops,
                moved=9 * MIB,
            )
            latest = output
        elif turn == "n":
            gr = ordered(latest, gr)
            own_edge, near_edge, far_edge, ig = call(
                input_body,
                "input",
                [stays(a) for a in (frames, gq_far, gk_far, gv_far, gr)]
                + [edge, near_rows, far_rows]
                + [stays(a) for a in (again, wq, wk, wv)],
                [edge_wide, edge_half, edge_half, copied(*model_low)],
                scratch=[
                    pltpu.VMEM((count, width), BF16),
                    pltpu.SemaphoreType.DMA((count // TILE,)),
                ],
                scalars=[where],
                vmem=24,
                flops=3 * unit_flops,
                moved=8 * MIB,
            )
            latest = far_edge
        elif turn == "e":
            far_edge = ordered(latest, far_edge)
            near_got = swapped(near_edge, "tm", 1)
            far_got = along(far_edge)
        elif turn == "i":
            far_got = ordered(latest, far_got)
            low = place.core == 0
            first = (own_edge[:EDGE] + jnp.where(low, far_got, near_got)).astype(BF16)
            last = (own_edge[EDGE:] + jnp.where(low, near_got, far_got)).astype(BF16)
            latest = (first, last)
        else:
            one = sums[turn]
            one.hold(ordered(latest, one.held()))
            if one.todo:
                one.advance()
                latest = one.held()
            elif one is down:
                places = [(0, at, at) for at in range(0, ffw, width)], (0, 1)
                (grad_down,) = one.whole(where, places, [free(ffw, width, F32)])
                latest = grad_down
            elif one is up:
                places = [(0, 0, 0), (1, ffw, 0)], (0, 2)
                outs = [free(width, ffw, F32), free(width, width, F32)]
                grad_up, grad_mix = one.whole(where, places, outs)
                latest = grad_mix
    ig = ig.at[:EDGE].set(first)
    ig = ig.at[count - EDGE :].set(last)
    places = [(i, i * width, 0) for i in range(3)], (3 * width, 3)
    outs = [free(width, width, F32)] * 3 + [vector] * 8 + [free(1, ffw, F32)]
    grad_q, grad_k, grad_v, *vectors = rest.whole(where, places, outs)
    gqb, gvb, gag, gas, gmb, gfg, gfs, gdb, gub = (made[0] for made in vectors)
    return (
        output[None],
        ig[None],
        grad_q,
        gqb,
        grad_k,
        grad_v,
        gvb,
        grad_mix,
        gmb,
        gag,
        gas,
        gfg,
        gfs,
        grad_up,
        gub,
        grad_down,
        gdb,
    )


def solution(mesh):
    rows = P("items", "tm", None)
    in_specs = (rows, rows, P("items", None), P("items", None)) + (P(),) * 16
    out_specs = (rows, rows) + (P(),) * 15
    fast = mesh.shape["tm"] == 16 and mesh.shape["items"] == 2
    return jax.shard_map(
        functools.partial(local, fast),
        mesh=mesh,
        in_specs=in_specs,
        out_specs=out_specs,
        check_vma=False,
    )
```

```python
import functools
import math

import jax
import jax.numpy as jnp
from jax import lax
from jax.experimental import pallas as pl
from jax.experimental.pallas import tpu as pltpu
from jax.sharding import PartitionSpec as P

HEADS = 8
LEFT = 10
RIGHT = 2
EDGE = 16
TILE = 256
SUB = 32
WINDOW = 48
GROUP = 4
MIB = 1 << 20
ORDER = "udrudrurdnurduderudiroudru"
LOG2E = 1.0 / math.log(2.0)
F32 = jnp.float32
BF16 = jnp.bfloat16


def dot(left, right):
    return jnp.dot(left, right, preferred_element_type=F32)


def against(left, right):
    return lax.dot_general(left, right, (((1,), (1,)), ((), ())), preferred_element_type=F32)


def over_rows(left, right):
    return lax.dot_general(left, right, (((0,), (0,)), ((), ())), preferred_element_type=F32)


def norm_parts(values):
    centered = values - jnp.mean(values, axis=-1, keepdims=True)
    variance = jnp.mean(centered * centered, axis=-1, keepdims=True)
    inverse = lax.rsqrt(variance + 1e-05)
    return centered * inverse, inverse


def norm_back(upstream, unit, inverse):
    return inverse * (
        upstream
        - jnp.mean(upstream, axis=-1, keepdims=True)
        - unit * jnp.mean(upstream * unit, axis=-1, keepdims=True)
    )


def row_sum(values):
    return jnp.sum(values, axis=0, keepdims=True)


def scaled_rows(values, weight):
    return values.astype(F32) * jnp.tile(weight, (1, values.shape[1] // 128))


def halves(values, core):
    rows = values.shape[0] // 2
    low, high = values[:rows].astype(BF16), values[rows:].astype(BF16)
    return jnp.where(core == 0, low, high), jnp.where(core == 0, high, low)


def tiles(count, rows=TILE):
    return [slice(start, start + rows) for start in range(0, count, rows)]


def shaped(shape, dtype):
    return jax.ShapeDtypeStruct(shape, dtype)


ANY = pl.BlockSpec(memory_space=pl.ANY)
SCALARS = pl.BlockSpec(memory_space=pltpu.SMEM)
WHOLE = pl.BlockSpec(memory_space=pltpu.VMEM)


def call(body, name, ins, outs, scratch=(), scalars=(), far_ins=(), vmem=10, flops=0, moved=0):
    return pl.pallas_call(
        body,
        in_specs=[SCALARS] * len(scalars) + [WHOLE] * len(ins) + [ANY] * len(far_ins),
        out_specs=[ANY if own_copies else WHOLE for _, own_copies in outs],
        out_shape=[out for out, _ in outs],
        scratch_shapes=list(scratch),
        name=name,
        compiler_params=pltpu.CompilerParams(vmem_limit_bytes=vmem * MIB),
        cost_estimate=pl.CostEstimate(flops=flops, bytes_accessed=moved, transcendentals=0),
    )(*scalars, *ins, *far_ins)


def near(*shape):
    return pltpu.VMEM(shape[:-1], shape[-1]), False


def copied(*shape):
    return pltpu.HBM(shape[:-1], shape[-1]), True


def free(*shape):
    return shaped(shape[:-1], shape[-1]), False


def project_body(x, gain, shift, wq, wk, wv, bq, bv, q_out, k_out, v_out):
    scale = (wq.shape[1] // HEADS) ** (-0.5)
    for rows in tiles(x.shape[0]):
        unit, _ = norm_parts(x[rows, :].astype(F32))
        normed = (unit * gain[...] + shift[...]).astype(BF16)
        q_out[rows, :] = (dot(normed, wq[...]) + bq[...]).astype(BF16) * jnp.asarray(scale, BF16)
        k_out[rows, :] = dot(normed, wk[...]).astype(BF16)
        v_out[rows, :] = (dot(normed, wv[...]) + bv[...]).astype(BF16)


def slot_ends(lengths):
    slots = lengths.shape[1]
    low = lax.broadcasted_iota(jnp.int32, (slots, slots), 0)
    high = lax.broadcasted_iota(jnp.int32, (slots, slots), 1)
    along = jnp.sum(jnp.where(low == high, lengths, 0.0), axis=1, keepdims=True)
    ends_column = jnp.sum(jnp.where(high <= low, lengths, 0.0), axis=1, keepdims=True)
    ends_row = jnp.sum(jnp.where(low <= high, along, 0.0), axis=0, keepdims=True)
    return ends_row, ends_column


def head_lanes(dtype):
    lane = lax.broadcasted_iota(jnp.int32, (1, 128), 1)
    return [(lane < 64).astype(F32).astype(dtype), (lane >= 64).astype(F32).astype(dtype)]


def stacked(values, masks):
    low, high = values[:, :128], values[:, 128:]
    none = jnp.zeros_like(low)
    return jnp.concatenate(
        [
            jnp.concatenate([low * masks[0], none], axis=1),
            jnp.concatenate([low * masks[1], none], axis=1),
            jnp.concatenate([none, high * masks[0]], axis=1),
            jnp.concatenate([none, high * masks[1]], axis=1),
        ],
        axis=0,
    )


def unstacked(values):
    rows = values.shape[0] // GROUP
    first = lax.broadcasted_iota(jnp.int32, (rows, 128), 1) < 64
    low = jnp.where(first, values[:rows, :128], values[rows : 2 * rows, :128])
    high = jnp.where(first, values[2 * rows : 3 * rows, 128:], values[3 * rows :, 128:])
    return jnp.concatenate([low, high], axis=1)


def neighbours(core, near_rows, far_rows):
    one, other = near_rows[...], far_rows[...]
    return jnp.where(core == 0, other, one), jnp.where(core == 0, one, other)


def fill_window(store, edge, own, count):
    store[:LEFT] = edge[EDGE - LEFT : EDGE]
    store[LEFT : LEFT + count] = own
    store[LEFT + count :] = edge[EDGE : EDGE + store.shape[0] - LEFT - count]


def forward_body(
    stream_len,
    where,
    domain,
    q,
    k,
    v,
    near_rows,
    far_rows,
    lengths,
    tags,
    gain,
    shift,
    wk,
    wv,
    bv,
    bmix,
    fgain,
    fshift,
    bup,
    x_in,
    wmix_in,
    out_grad_in,
    wup_in,
    wdown_in,
    probs_out,
    q_out,
    keys_out,
    values_out,
    active_out,
    resid_out,
    gr_out,
    gm_out,
    keep_d_out,
    send_d_out,
    keep_u_out,
    send_u_out,
    gdb_out,
    gub_out,
    gmb_out,
    gfg_out,
    gfs_out,
    keys,
    values,
    ends_row,
    ends_column,
    probs,
    mixed,
    resid,
    weight,
    nffn,
    branch,
    active,
    slope,
    gh,
    gr,
    gm,
    x,
    wmix,
    out_grad,
    wup,
    wdown,
    sems,
    block_sems,
    load_sems,
):
    count, width = q.shape
    ffw = wup.shape[1]
    half = width // 2
    first = where[0]
    core = where[1]
    copies = []
    loads = []
    for source, target in (
        (x_in, x),
        (wmix_in, wmix),
        (out_grad_in, out_grad),
        (wup_in, wup),
        (wdown_in, wdown),
    ):
        loads.append(pltpu.make_async_copy(source, target, load_sems.at[len(loads)]))
        loads[-1].start()

    def carry_out(source, target):
        copies.append(pltpu.make_async_copy(source, target, sems.at[len(copies)]))
        copies[-1].start()

    carry_out(q, q_out)
    edge = jnp.concatenate(neighbours(core, near_rows, far_rows), axis=0).astype(F32)
    unit, _ = norm_parts(edge)
    normed = (unit * gain[...] + shift[...]).astype(BF16)
    fill_window(keys, dot(normed, wk[...]).astype(BF16), k[...], count)
    fill_window(values, (dot(normed, wv[...]) + bv[...]).astype(BF16), v[...], count)
    carry_out(keys, keys_out)
    carry_out(values, values_out)
    row, column = slot_ends(lengths[...].astype(F32))
    ends_row[...] = row
    ends_column[...] = column

    kinds = tags[...]
    slot_weight = jnp.where(kinds == 0, domain[0], 0.0)
    slot_weight = jnp.where(kinds == 1, domain[1], slot_weight)
    slot_weight = jnp.where(kinds == 2, domain[2], slot_weight)
    slots = kinds.shape[1]
    slot = lax.broadcasted_iota(jnp.int32, (TILE, slots), 1).astype(F32)
    masks = head_lanes(BF16)
    lanes_all = GROUP * SUB
    key_at = lax.broadcasted_iota(jnp.int32, (WINDOW, lanes_all), 0)
    query_at = lax.broadcasted_iota(jnp.int32, (WINDOW, lanes_all), 1) % SUB
    near = (key_at >= query_at) & (key_at <= query_at + LEFT + RIGHT)

    def one_tile(step, carried):
        tile_at = pl.multiple_of(step * TILE, TILE)
        places = (first + tile_at + lax.broadcasted_iota(jnp.int32, (TILE, 1), 0)).astype(F32)
        seg = jnp.sum((ends_row[...] <= places).astype(F32), axis=1, keepdims=True)
        weight[pl.ds(tile_at, TILE), :] = jnp.broadcast_to(
            jnp.sum(jnp.where(seg == slot, slot_weight, 0.0), axis=1, keepdims=True),
            (TILE, weight.shape[1]),
        )
        allowed, scores, pieces = [], [], []
        for sub in range(TILE // SUB):
            at = first + tile_at + sub * SUB
            ours = (at + lax.broadcasted_iota(jnp.int32, (1, lanes_all), 1) % SUB).astype(F32)
            others = (at - LEFT + lax.broadcasted_iota(jnp.int32, (WINDOW, 1), 0)).astype(F32)
            seg_ours = jnp.sum((ends_column[...] <= ours).astype(F32), axis=0, keepdims=True)
            seg_others = jnp.sum((ends_row[...] <= others).astype(F32), axis=1, keepdims=True)
            seg_others = jnp.where(others < 0.0, -1.0, seg_others)
            seg_others = jnp.where(others >= float(stream_len), -2.0, seg_others)
            allowed.append(near & (seg_ours == seg_others))
            for group in range(2):
                pieces.append((sub, group))
        for sub, group in pieces:
            start = pl.multiple_of(tile_at + sub * SUB, SUB)
            lanes = slice(group * half, (group + 1) * half)
            queries = stacked(q[pl.ds(start, SUB), lanes], masks)
            scores.append(against(keys[pl.ds(start, WINDOW), lanes], queries))
        lows = []
        for (sub, group), score in zip(pieces, scores):
            score = jnp.where(allowed[sub], score, -1e30)
            grown = jnp.exp(score - jnp.max(score, axis=0, keepdims=True))
            low = (grown * (1.0 / jnp.sum(grown, axis=0, keepdims=True))).astype(BF16)
            probs[2 * (step * (TILE // SUB) + sub) + group] = low
            lows.append(low)
        for (sub, group), low in zip(pieces, lows):
            start = pl.multiple_of(tile_at + sub * SUB, SUB)
            lanes = slice(group * half, (group + 1) * half)
            heads = unstacked(over_rows(low, values[pl.ds(start, WINDOW), lanes]))
            mixed[pl.ds(start, SUB), lanes] = heads.astype(BF16)
        return carried

    lax.fori_loop(0, count // TILE, one_tile, 0)
    carry_out(probs, probs_out)
    for load in loads[:3]:
        load.wait()
    bias = jnp.zeros((1, width), F32)
    for rows in tiles(count):
        summed = x[rows, :].astype(F32) + dot(mixed[rows, :], wmix[...]) + bmix[...]
        resid[rows, :] = summed
        unit, _ = norm_parts(summed)
        nffn[rows, :] = (unit * fgain[...] + fshift[...]).astype(BF16)
        scaled = scaled_rows(out_grad[rows, :], weight[rows, :]).astype(BF16)
        branch[rows, :] = scaled
        bias = bias + row_sum(scaled.astype(F32))
    gdb_out[...] = bias
    carry_out(resid, resid_out)

    def one_block(block, carried):
        at = pl.multiple_of(block * width, width)
        lanes = pl.ds(at, width)
        for rows in tiles(count):
            hidden = dot(nffn[rows, :], wup[:, lanes]) + bup[:, lanes]
            below = 1.0 + lax.erf(hidden * math.sqrt(0.5))
            bell = jnp.exp2(
                hidden * hidden * (-0.5 * LOG2E) + math.log2(2.0 / math.sqrt(2.0 * math.pi))
            )
            active[rows, lanes] = ((hidden * 0.5) * below).astype(BF16)
            slope[rows, :] = (below + hidden * bell).astype(BF16)
        pltpu.make_async_copy(
            active.at[:, lanes], active_out.at[:, lanes], block_sems.at[block]
        ).start()
        keep_d_out[:, lanes], send_d_out[:, lanes] = halves(
            over_rows(active[:, lanes], branch[...]), core
        )
        bias = jnp.zeros((1, width), F32)
        for rows in tiles(count):
            half_branch = branch[rows, :] * jnp.asarray(0.5, BF16)
            grad = against(half_branch, wdown[lanes, :]) * slope[rows, :].astype(F32)
            low = grad.astype(BF16)
            gh[rows, lanes] = low
            bias = bias + row_sum(low.astype(F32))
        gub_out[:, lanes] = bias
        keep_u_out[:, lanes], send_u_out[:, lanes] = halves(
            over_rows(nffn[...], gh[:, lanes]), core
        )
        return carried

    for load in loads[3:]:
        load.wait()
    lax.fori_loop(0, ffw // width, one_block, 0)
    by_bias, by_gain, by_shift = (jnp.zeros((1, width), F32) for _ in range(3))
    for rows in tiles(count):
        grad = against(gh[rows, :], wup[...])
        unit, inverse = norm_parts(resid[rows, :])
        by_gain = by_gain + row_sum(grad * unit)
        by_shift = by_shift + row_sum(grad)
        grad_resid = scaled_rows(out_grad[rows, :], weight[rows, :]) + norm_back(
            grad * fgain[...], unit, inverse
        )
        gr[rows, :] = grad_resid
        low = grad_resid.astype(BF16)
        branch[rows, :] = low
        by_bias = by_bias + row_sum(low.astype(F32))
        gm[rows, :] = against(low, wmix[...]).astype(BF16)
    carry_out(gr, gr_out)
    carry_out(gm, gm_out)
    there = slice(ffw, ffw + width)
    keep_u_out[:, there], send_u_out[:, there] = halves(over_rows(mixed[...], branch[...]), core)
    gmb_out[...] = by_bias
    gfg_out[...] = by_gain
    gfs_out[...] = by_shift
    for block in range(ffw // width):
        lanes = slice(block * width, (block + 1) * width)
        copies.append(
            pltpu.make_async_copy(
                active.at[:, lanes], active_out.at[:, lanes], block_sems.at[block]
            )
        )
    for copy in copies:
        copy.wait()


def output_body(bdown, wdown_in, resid_in, active_in, out, wdown, resid, active, low, sems):
    steps = tiles(resid.shape[0])

    def moved(source, target, place):
        return pltpu.make_async_copy(source, target, sems.at[place])

    loads = [moved(wdown_in, wdown, 0)]
    for i, rows in enumerate(steps):
        loads.append(moved(active_in.at[rows, :], active.at[rows, :], 1 + 2 * i))
        loads.append(moved(resid_in.at[rows, :], resid.at[rows, :], 2 + 2 * i))
    for load in loads:
        load.start()
    loads[0].wait()
    stores = []
    for i, rows in enumerate(steps):
        loads[1 + 2 * i].wait()
        loads[2 + 2 * i].wait()
        low[rows, :] = (
            resid[rows, :] + dot(active[rows, :], wdown[...]) + bdown[...]
        ).astype(BF16)
        stores.append(moved(low.at[rows, :], out.at[rows, :], 1 + 2 * len(steps) + i))
        stores[-1].start()
    for store in stores:
        store.wait()


def attend_back_body(
    gm_in,
    values_in,
    probs_in,
    keys_in,
    q_in,
    gq,
    gk,
    gv,
    edge,
    gq_out,
    gk_out,
    gv_out,
    gm,
    values,
    probs,
    keys,
    q,
    gk_window,
    gv_window,
    sems,
    load_sems,
):
    count, width = q.shape
    half = width // 2
    steps = count // TILE
    spill = keys.shape[0] - count
    blocks = probs.shape[0] // steps

    def loads(step):
        def load(place, source, target, start, size):
            part = pl.ds(start, size)
            return pltpu.make_async_copy(
                source.at[part], target.at[part], load_sems.at[place, step]
            )

        start = step * TILE
        first = start if isinstance(step, int) else pl.multiple_of(start + spill, spill)
        size = TILE + spill if isinstance(step, int) else TILE
        return [
            load(0, gm_in, gm, start, TILE),
            load(1, values_in, values, first, size),
            load(2, probs_in, probs, step * blocks, blocks),
            load(3, keys_in, keys, first, size),
            load(4, q_in, q, start, TILE),
        ]

    def begin(step, carried):
        for load in loads(step):
            load.start()
        return carried

    for load in loads(0):
        load.start()
    lax.fori_loop(1, steps, begin, 0)
    gk_window[...] = jnp.zeros_like(gk_window)
    gv_window[...] = jnp.zeros_like(gv_window)
    scale = (width // HEADS) ** (-0.5)
    masks = head_lanes(BF16)
    pieces = [(sub, group) for sub in range(TILE // SUB) for group in range(2)]

    def one_tile(step, carried):
        tile_at = pl.multiple_of(step * TILE, TILE)

        @pl.when(step == 0)
        def _():
            for load in loads(0):
                load.wait()

        @pl.when(step > 0)
        def _():
            for load in loads(step):
                load.wait()

        def spot(sub, group):
            start = pl.multiple_of(tile_at + sub * SUB, SUB)
            return pl.ds(start, SUB), pl.ds(start, WINDOW), slice(group * half, (group + 1) * half)

        pulls, grads = [], []
        for sub, group in pieces:
            rows, window, lanes = spot(sub, group)
            pulled = stacked(gm[rows, lanes], masks)
            pulls.append(pulled)
            grads.append(against(values[window, lanes], pulled))
        lows = []
        for (sub, group), grad in zip(pieces, grads):
            wide = probs[2 * (step * (TILE // SUB) + sub) + group].astype(F32)
            product = wide * grad
            lows.append((product - wide * jnp.sum(product, axis=0, keepdims=True)).astype(BF16))
        for (sub, group), pulled, low in zip(pieces, pulls, lows):
            rows, window, lanes = spot(sub, group)
            queries = stacked(q[rows, lanes], masks)
            gq[rows, lanes] = (unstacked(over_rows(low, keys[window, lanes])) * scale).astype(BF16)
            gk_window[window, lanes] += dot(low, queries)
            gv_window[window, lanes] += dot(
                probs[2 * (step * (TILE // SUB) + sub) + group], pulled
            )
        return carried

    lax.fori_loop(0, count // TILE, one_tile, 0)
    stores = []

    def store(source, target):
        stores.append(pltpu.make_async_copy(source, target, sems.at[len(stores)]))
        stores[-1].start()

    store(gq, gq_out)
    for place, (window, grad, out) in enumerate(
        ((gk_window, gk, gk_out), (gv_window, gv, gv_out))
    ):
        lanes = slice(place * width, (place + 1) * width)
        grad[...] = window[LEFT : LEFT + count].astype(BF16)
        store(grad, out)
        edge[:LEFT, lanes] = window[:LEFT].astype(BF16)
        edge[LEFT : LEFT + RIGHT, lanes] = window[LEFT + count : LEFT + count + RIGHT].astype(BF16)
    for one in stores:
        one.wait()


def edge_frames(core, near_rows, far_rows):
    before, behind = neighbours(core, near_rows, far_rows)
    return jnp.concatenate([before[EDGE - LEFT :], behind[:RIGHT]], axis=0).astype(F32)


def weights_body(
    where,
    gq,
    gk,
    gv,
    edge,
    near_rows,
    far_rows,
    gain,
    shift,
    gdb,
    gub,
    gmb,
    gfg,
    gfs,
    x_in,
    wq_in,
    wk_in,
    wv_in,
    keep_out,
    send_out,
    x,
    wq,
    wk,
    wv,
    sums,
    vec,
    sems,
):
    width = x.shape[1]
    core = where[1]
    loads = []
    for source, target in ((x_in, x), (wq_in, wq), (wk_in, wk), (wv_in, wv)):
        loads.append(pltpu.make_async_copy(source, target, sems.at[len(loads)]))
        loads[-1].start()
    far_low = norm_parts(edge_frames(core, near_rows, far_rows))[0].astype(BF16)
    gain_column = jnp.transpose(jnp.broadcast_to(gain[...], (128, width)))[:, :1]
    shift_column = jnp.transpose(jnp.broadcast_to(shift[...], (128, width)))[:, :1]
    columns = [row_sum(grad[...].astype(F32)) for grad in (gq, gk, gv)]
    loads[0].wait()
    unit = norm_parts(x[...].astype(F32))[0].astype(BF16)
    by_gain = jnp.zeros((width, 1), F32)
    by_shift = jnp.zeros((width, 1), F32)
    for place, (grad, weight) in enumerate(((gq, wq), (gk, wk), (gv, wv))):
        product = over_rows(unit, grad[...])
        column = columns[place]
        if place > 0:
            there = slice((place - 1) * width, place * width)
            product = product + over_rows(far_low, edge[: LEFT + RIGHT, there])
            column = column + row_sum(edge[: LEFT + RIGHT, there].astype(F32))
        lanes = slice(place * width, (place + 1) * width)
        keep_out[:, lanes], send_out[:, lanes] = halves(
            product * gain_column + shift_column * column, core
        )
        loads[1 + place].wait()
        wide = weight[...].astype(F32)
        by_gain = by_gain + jnp.sum(wide * product, axis=1, keepdims=True)
        by_shift = by_shift + jnp.sum(wide * column, axis=1, keepdims=True)
        if place != 1:
            sums[place // 2 : place // 2 + 1] = column
    sums[2:3] = jnp.transpose(jnp.broadcast_to(by_gain, (width, 128)))[:1]
    sums[3:4] = jnp.transpose(jnp.broadcast_to(by_shift, (width, 128)))[:1]
    vec[...] = jnp.zeros_like(vec)
    row = 0
    for ref in [sums.at[i : i + 1] for i in range(4)] + [gmb, gfg, gfs, gdb, gub]:
        for part in range(0, ref.shape[1], 128):
            vec[row : row + 1] = ref[:, part : part + 128]
            row += 1
    keep_out[:, 3 * width :], send_out[:, 3 * width :] = halves(vec[...], core)


def input_body(
    where,
    x,
    gq,
    gk,
    gv,
    gr,
    edge,
    near_rows,
    far_rows,
    gain,
    wq,
    wk,
    wv,
    own_edge_out,
    near_edge_out,
    far_edge_out,
    ig_out,
    ig,
    sems,
):
    count, width = x.shape
    core = where[1]
    unit, inverse = norm_parts(edge_frames(core, near_rows, far_rows))
    cut = slice(0, LEFT + RIGHT)
    grad = against(edge[cut, :width], wk[...]) + against(edge[cut, width:], wv[...])
    grad = norm_back(grad * gain[...], unit, inverse)
    before = jnp.concatenate([jnp.zeros((EDGE - LEFT, width), F32), grad[:LEFT]], axis=0)
    behind = jnp.concatenate([grad[LEFT:], jnp.zeros((EDGE - RIGHT, width), F32)], axis=0)
    near_edge_out[...] = jnp.where(core == 0, behind, before)
    far_edge_out[...] = jnp.where(core == 0, before, behind)
    stores = []
    for rows in tiles(count):
        unit, inverse = norm_parts(x[rows, :].astype(F32))
        grad = (
            against(gq[rows, :], wq[...])
            + against(gk[rows, :], wk[...])
            + against(gv[rows, :], wv[...])
        )
        result = gr[rows, :] + norm_back(grad * gain[...], unit, inverse)
        ig[rows, :] = result.astype(BF16)
        stores.append(
            pltpu.make_async_copy(
                ig.at[rows, :], ig_out.at[rows, :], sems.at[len(stores)]
            )
        )
        stores[-1].start()
        if rows.start == 0:
            own_edge_out[:EDGE] = result[:EDGE]
        if rows.stop == count:
            own_edge_out[EDGE:] = result[-EDGE:]
    for store in stores:
        store.wait()


def swapped(value, axis, mask):
    count = lax.axis_size(axis)
    return lax.ppermute(value, axis, [(i, i ^ mask) for i in range(count)])


def across(value, first):
    tm, items = lax.axis_size("tm"), lax.axis_size("items")
    pairs = []
    for i in range(tm):
        for j in range(items):
            along_x = (i % 2 == 0) == first
            pairs.append((i * items + j, i * items + (j ^ 1) if along_x else (i ^ 2) * items + j))
    return lax.ppermute(value, ("tm", "items"), pairs)


def cut(value, place, rows):
    return lax.dynamic_slice_in_dim(value, place * rows, rows, 0)


def total_of(parts):
    total = parts[0].astype(F32)
    for part in parts[1:]:
        total = total + part.astype(F32)
    return total.astype(BF16)


def paired(own, got, bit):
    return jnp.where(bit == 0, jnp.concatenate([own, got]), jnp.concatenate([got, own]))


def whole_body(places, where, own, got, *outs):
    blocks, (lane, first) = places
    rows = own.shape[0]
    for place, part in ((where[1], own), (1 - where[1], got)):
        for out, start, row in blocks:
            width = outs[out].shape[1]
            outs[out][pl.ds(pl.multiple_of(row + place * rows, rows), rows), :] = part[
                :, start : start + width
            ].astype(F32)
    if first < len(outs):
        count = sum(out.shape[1] for out in outs[first:]) // 128
        low = jnp.where(where[1] == 0, own[:count, lane:], got[:count, lane:]).astype(F32)
        row = 0
        for out in outs[first:]:
            for at in range(0, out.shape[1], 128):
                out[:, at : at + 128] = low[row : row + 1]
                row += 1


class Place:
    def __init__(self):
        tm = lax.axis_index("tm").astype(jnp.int32)
        x_bit = lax.axis_index("items").astype(jnp.int32) % 2
        y_bit = (tm // 2) % 2
        self.core = tm % 2
        self.steps = [
            (jnp.where(self.core == 0, x_bit, y_bit), lambda value: across(value, True)),
            (jnp.where(self.core == 0, y_bit, x_bit), lambda value: across(value, False)),
            ((tm // 4) % 2, lambda value: swapped(value, "tm", 4)),
            ((tm // 8) % 2, lambda value: swapped(value, "tm", 8)),
        ]


class Sum:
    def __init__(self, place, halved, keep, send):
        self.place = place
        self.parts = [keep, swapped(send, "tm", 1)]
        self.todo = [functools.partial(self.exchange, step, step < halved) for step in range(4)]
        self.todo += [functools.partial(self.spread, step) for step in range(halved - 1, -1, -1)]
        self.todo += [functools.partial(self.spread, -1)]
        self.bit = None

    def held(self):
        return self.parts[0]

    def hold(self, value):
        self.parts[0] = value

    def advance(self):
        self.todo.pop(0)()

    def exchange(self, step, halve):
        bit, exchange = self.place.steps[step]
        if halve:
            rows = self.parts[0].shape[0] // 2
            mine, other = (
                total_of([cut(part, at, rows) for part in self.parts]) for at in (bit, 1 - bit)
            )
        else:
            mine = other = total_of(self.parts)
        self.parts = [mine, exchange(other)]

    def spread(self, step):
        own = total_of(self.parts) if self.bit is None else paired(*self.parts, self.bit)
        if step >= 0:
            self.bit, exchange = self.place.steps[step]
            self.parts = [own, exchange(own)]
        else:
            self.parts = [own, swapped(own, "tm", 1)]

    def whole(self, where, places, outs):
        return call(
            functools.partial(whole_body, places),
            "whole",
            self.parts,
            outs,
            scalars=[where],
            vmem=24,
            moved=6 * MIB,
        )


class PlainSum:
    def __init__(self, place, halved, keep, send):
        self.place = place
        self.todo = []
        self.parts = [keep, send]

    def held(self):
        return self.parts[0]

    def hold(self, value):
        self.parts[0] = value

    def advance(self):
        pass

    def whole(self, where, places, outs):
        keep, send = self.parts
        low = jnp.where(self.place.core == 0, keep, send)
        high = jnp.where(self.place.core == 0, send, keep)
        total = lax.psum(jnp.concatenate([low, high], axis=0), ("tm", "items"))
        blocks, vectors = places
        made = [[] for _, _ in outs]
        for out, lane, _ in blocks:
            made[out].append(total[:, lane : lane + outs[out][0].shape[1]])
        lane, first = vectors
        for out in range(first, len(outs)):
            size = outs[out][0].shape[1]
            start = sum(made_out[0].shape[1] // 128 for _, made_out in enumerate(made[first:out]))
            rows = total[start : start + size // 128, lane : lane + 128]
            made[out].append(rows.reshape(1, size))
        return [jnp.concatenate(parts, axis=0).astype(F32) for parts in made]


def stays(array):
    return pltpu.with_memory_space_constraint(array, pltpu.HBM)


def here(array):
    return pltpu.with_memory_space_constraint(array, pltpu.VMEM)


def ordered(first, second):
    return lax.optimization_barrier((first, second))[1]


def follow(first, second):
    second.hold(ordered(first.held(), second.held()))


def along(value):
    count = lax.axis_size("tm")
    pairs = [(i, i + 1) for i in range(1, count - 1, 2)]
    return lax.ppermute(value, "tm", pairs + [(to, of) for of, to in pairs])


def local(
    fast,
    frames,
    out_grad,
    item_lengths,
    domain_tags,
    domain_weight,
    wq,
    bq,
    wk,
    wv,
    bv,
    wmix,
    bmix,
    again,
    ashift,
    fgain,
    fshift,
    wup,
    bup,
    wdown,
    bdown,
):
    frames = frames[0]
    out_grad = out_grad[0]
    count, width = frames.shape
    ffw = wup.shape[1]
    slots = item_lengths.shape[1]
    stream_len = count * lax.axis_size("tm")
    reach = count + WINDOW - SUB
    unit_flops = 2 * count * width * width
    parts = ffw // width
    bq, bv, bmix, again, ashift, fgain, fshift, bup, bdown = (
        vector[None] for vector in (bq, bv, bmix, again, ashift, fgain, fshift, bup, bdown)
    )
    place = Place()
    where = jnp.stack([lax.axis_index("tm") * count, place.core]).astype(jnp.int32)
    near_end = jnp.where(place.core == 0, count - EDGE, 0)
    near_rows = swapped(lax.dynamic_slice_in_dim(frames, near_end, EDGE, 0), "tm", 1)
    far_rows = along(lax.dynamic_slice_in_dim(frames, count - EDGE - near_end, EDGE, 0))
    kind = Sum if fast else PlainSum
    vector = free(1, width, F32)
    edge_wide = free(2 * EDGE, width, F32)
    edge_half = free(EDGE, width, F32)
    model_low = (count, width, BF16)
    model_wide = (count, width, F32)
    hidden_low = (count, ffw, BF16)
    blocks = (2 * count // SUB, WINDOW, GROUP * SUB, BF16)
    windowed = (reach, width)
    low_scratch = pltpu.VMEM((count, width), BF16)

    q, k, v = call(
        project_body,
        "project",
        [stays(a) for a in (frames, again, ashift, wq, wk, wv, bq, bv)],
        [near(*model_low)] * 3,
        flops=3 * unit_flops,
        moved=6 * MIB,
    )
    (
        probs,
        q,
        keys,
        values,
        active,
        resid,
        gr,
        gm,
        keep_d,
        send_d,
        keep_u,
        send_u,
        gdb,
        gub,
        gmb,
        gfg,
        gfs,
    ) = call(
        functools.partial(forward_body, stream_len),
        "forward",
        [q, k, v, near_rows, far_rows]
        + [stays(a) for a in (item_lengths, domain_tags, again, ashift, wk, wv)]
        + [stays(a) for a in (bv, bmix, fgain, fshift, bup)],
        [copied(*blocks), copied(*model_low), copied(*windowed, BF16), copied(*windowed, BF16)]
        + [copied(*hidden_low), copied(*model_wide), copied(*model_wide), copied(*model_low)]
        + [near(width // 2, ffw, BF16)] * 2
        + [near(width // 2, ffw + width, BF16)] * 2
        + [vector, free(1, ffw, F32), vector, vector, vector],
        scratch=[
            pltpu.VMEM(windowed, BF16),
            pltpu.VMEM(windowed, BF16),
            pltpu.VMEM((1, slots), F32),
            pltpu.VMEM((slots, 1), F32),
            pltpu.VMEM(blocks[:-1], BF16),
            pltpu.VMEM((count, width), BF16),
            pltpu.VMEM((count, width), F32),
            pltpu.VMEM((count, 128), F32),
            pltpu.VMEM((count, width), BF16),
            pltpu.VMEM((count, width), BF16),
            pltpu.VMEM((count, ffw), BF16),
            pltpu.VMEM((count, width), BF16),
            pltpu.VMEM((count, ffw), BF16),
            pltpu.VMEM((count, width), F32),
            pltpu.VMEM((count, width), BF16),
            pltpu.VMEM((count, width), BF16),
            pltpu.VMEM((width, width), BF16),
            pltpu.VMEM((count, width), BF16),
            pltpu.VMEM((width, ffw), BF16),
            pltpu.VMEM((ffw, width), BF16),
            pltpu.SemaphoreType.DMA((7,)),
            pltpu.SemaphoreType.DMA((parts,)),
            pltpu.SemaphoreType.DMA((5,)),
        ],
        scalars=[where, domain_weight],
        far_ins=[stays(a) for a in (frames, wmix, out_grad, wup, wdown)],
        vmem=40,
        flops=(6 + 5 * parts) * unit_flops,
        moved=24 * MIB,
    )
    down = kind(place, 3, keep_d, send_d)
    up = kind(place, 3, keep_u, send_u)

    down.advance()
    follow(down, up)
    up.advance()
    gm = ordered(up.held(), gm)
    (gq, gk, gv, edge, gq_far, gk_far, gv_far) = call(
        attend_back_body,
        "attend_back",
        [],
        [near(*model_low)] * 3
        + [near(EDGE, 2 * width, BF16)]
        + [copied(*model_low)] * 3,
        scratch=[
            low_scratch,
            pltpu.VMEM(windowed, BF16),
            pltpu.VMEM(blocks[:-1], BF16),
            pltpu.VMEM(windowed, BF16),
            low_scratch,
            pltpu.VMEM(windowed, F32),
            pltpu.VMEM(windowed, F32),
            pltpu.SemaphoreType.DMA((3,)),
            pltpu.SemaphoreType.DMA((5, count // TILE)),
        ],
        far_ins=[stays(a) for a in (gm, values, probs, keys, q)],
        vmem=20,
        flops=8 * unit_flops,
        moved=10 * MIB,
    )
    down.hold(ordered(edge, down.held()))
    down.advance()
    edge = ordered(down.held(), edge)
    rest_half = near(width // 2, 3 * width + 128, BF16)
    square_low = pltpu.VMEM((width, width), BF16)
    keep_r, send_r = call(
        weights_body,
        "weights",
        [gq, gk, gv, edge, near_rows, far_rows]
        + [stays(a) for a in (again, ashift)]
        + [gdb, gub, gmb, gfg, gfs],
        [rest_half, rest_half],
        scratch=[pltpu.VMEM((count, width), BF16)]
        + [square_low] * 3
        + [pltpu.VMEM((8, width), F32), pltpu.VMEM((width, 128), F32)]
        + [pltpu.SemaphoreType.DMA((4,))],
        scalars=[where],
        far_ins=[stays(a) for a in (frames, wq, wk, wv)],
        vmem=16,
        flops=3 * unit_flops,
        moved=8 * MIB,
    )
    rest = kind(place, 2, keep_r, send_r)
    sums = {"d": down, "u": up, "r": rest}
    latest = keep_r
    for turn in ORDER:
        if turn == "o":
            active = ordered(latest, active)
            (output,) = call(
                output_body,
                "output",
                [stays(bdown)],
                [copied(*model_low)],
                scratch=[
                    pltpu.VMEM((ffw, width), BF16),
                    pltpu.VMEM((count, width), F32),
                    pltpu.VMEM((count, ffw), BF16),
                    pltpu.VMEM((count, width), BF16),
                    pltpu.SemaphoreType.DMA((1 + 3 * (count // TILE),)),
                ],
                far_ins=[stays(a) for a in (wdown, resid, active)],
                vmem=20,
                flops=parts * unit_flops,
                moved=9 * MIB,
            )
            latest = output
        elif turn == "n":
            gr = ordered(latest, gr)
            own_edge, near_edge, far_edge, ig = call(
                input_body,
                "input",
                [stays(a) for a in (frames, gq_far, gk_far, gv_far, gr)]
                + [edge, near_rows, far_rows]
                + [stays(a) for a in (again, wq, wk, wv)],
                [edge_wide, edge_half, edge_half, copied(*model_low)],
                scratch=[
                    pltpu.VMEM((count, width), BF16),
                    pltpu.SemaphoreType.DMA((count // TILE,)),
                ],
                scalars=[where],
                vmem=24,
                flops=3 * unit_flops,
                moved=8 * MIB,
            )
            latest = far_edge
        elif turn == "e":
            far_edge = ordered(latest, far_edge)
            near_got = swapped(near_edge, "tm", 1)
            far_got = along(far_edge)
        elif turn == "i":
            far_got = ordered(latest, far_got)
            low = place.core == 0
            first = (own_edge[:EDGE] + jnp.where(low, far_got, near_got)).astype(BF16)
            last = (own_edge[EDGE:] + jnp.where(low, near_got, far_got)).astype(BF16)
            latest = (first, last)
        else:
            one = sums[turn]
            one.hold(ordered(latest, one.held()))
            if one.todo:
                one.advance()
                latest = one.held()
            elif one is down:
                places = [(0, at, at) for at in range(0, ffw, width)], (0, 1)
                (grad_down,) = one.whole(where, places, [free(ffw, width, F32)])
                latest = grad_down
            elif one is up:
                places = [(0, 0, 0), (1, ffw, 0)], (0, 2)
                outs = [free(width, ffw, F32), free(width, width, F32)]
                grad_up, grad_mix = one.whole(where, places, outs)
                latest = grad_mix
    ig = ig.at[:EDGE].set(first)
    ig = ig.at[count - EDGE :].set(last)
    places = [(i, i * width, 0) for i in range(3)], (3 * width, 3)
    outs = [free(width, width, F32)] * 3 + [vector] * 8 + [free(1, ffw, F32)]
    grad_q, grad_k, grad_v, *vectors = rest.whole(where, places, outs)
    gqb, gvb, gag, gas, gmb, gfg, gfs, gdb, gub = (made[0] for made in vectors)
    return (
        output[None],
        ig[None],
        grad_q,
        gqb,
        grad_k,
        grad_v,
        gvb,
        grad_mix,
        gmb,
        gag,
        gas,
        gfg,
        gfs,
        grad_up,
        gub,
        grad_down,
        gdb,
    )


def solution(mesh):
    rows = P("items", "tm", None)
    in_specs = (rows, rows, P("items", None), P("items", None)) + (P(),) * 16
    out_specs = (rows, rows) + (P(),) * 15
    fast = mesh.shape["tm"] == 16 and mesh.shape["items"] == 2
    return jax.shard_map(
        functools.partial(local, fast),
        mesh=mesh,
        in_specs=in_specs,
        out_specs=out_specs,
        check_vma=False,
    )
```

```python
import functools
import math

import jax
import jax.numpy as jnp
from jax import lax
from jax.experimental import pallas as pl
from jax.experimental.pallas import tpu as pltpu
from jax.sharding import PartitionSpec as P

HEADS = 8
LEFT = 10
RIGHT = 2
EDGE = 16
TILE = 256
SUB = 32
WINDOW = 48
GROUP = 4
MIB = 1 << 20
ORDER = "udrudrurdnurduderudiroudru"
LOG2E = 1.0 / math.log(2.0)
F32 = jnp.float32
BF16 = jnp.bfloat16


def dot(left, right):
    return jnp.dot(left, right, preferred_element_type=F32)


def against(left, right):
    return lax.dot_general(left, right, (((1,), (1,)), ((), ())), preferred_element_type=F32)


def over_rows(left, right):
    return lax.dot_general(left, right, (((0,), (0,)), ((), ())), preferred_element_type=F32)


def norm_parts(values):
    centered = values - jnp.mean(values, axis=-1, keepdims=True)
    variance = jnp.mean(centered * centered, axis=-1, keepdims=True)
    inverse = lax.rsqrt(variance + 1e-05)
    return centered * inverse, inverse


def norm_back(upstream, unit, inverse):
    return inverse * (
        upstream
        - jnp.mean(upstream, axis=-1, keepdims=True)
        - unit * jnp.mean(upstream * unit, axis=-1, keepdims=True)
    )


def row_sum(values):
    return jnp.sum(values, axis=0, keepdims=True)


def scaled_rows(values, weight):
    return values.astype(F32) * jnp.tile(weight, (1, values.shape[1] // 128))


def halves(values, core):
    rows = values.shape[0] // 2
    low, high = values[:rows].astype(BF16), values[rows:].astype(BF16)
    return jnp.where(core == 0, low, high), jnp.where(core == 0, high, low)


def tiles(count, rows=TILE):
    return [slice(start, start + rows) for start in range(0, count, rows)]


def shaped(shape, dtype):
    return jax.ShapeDtypeStruct(shape, dtype)


ANY = pl.BlockSpec(memory_space=pl.ANY)
SCALARS = pl.BlockSpec(memory_space=pltpu.SMEM)
WHOLE = pl.BlockSpec(memory_space=pltpu.VMEM)


def call(body, name, ins, outs, scratch=(), scalars=(), far_ins=(), vmem=10, flops=0, moved=0):
    return pl.pallas_call(
        body,
        in_specs=[SCALARS] * len(scalars) + [WHOLE] * len(ins) + [ANY] * len(far_ins),
        out_specs=[ANY if own_copies else WHOLE for _, own_copies in outs],
        out_shape=[out for out, _ in outs],
        scratch_shapes=list(scratch),
        name=name,
        compiler_params=pltpu.CompilerParams(vmem_limit_bytes=vmem * MIB),
        cost_estimate=pl.CostEstimate(flops=flops, bytes_accessed=moved, transcendentals=0),
    )(*scalars, *ins, *far_ins)


def near(*shape):
    return pltpu.VMEM(shape[:-1], shape[-1]), False


def copied(*shape):
    return pltpu.HBM(shape[:-1], shape[-1]), True


def free(*shape):
    return shaped(shape[:-1], shape[-1]), False


def project_body(x, gain, shift, wq, wk, wv, bq, bv, q_out, k_out, v_out):
    scale = (wq.shape[1] // HEADS) ** (-0.5)
    for rows in tiles(x.shape[0]):
        unit, _ = norm_parts(x[rows, :].astype(F32))
        normed = (unit * gain[...] + shift[...]).astype(BF16)
        q_out[rows, :] = (dot(normed, wq[...]) + bq[...]).astype(BF16) * jnp.asarray(scale, BF16)
        k_out[rows, :] = dot(normed, wk[...]).astype(BF16)
        v_out[rows, :] = (dot(normed, wv[...]) + bv[...]).astype(BF16)


def slot_ends(lengths):
    slots = lengths.shape[1]
    low = lax.broadcasted_iota(jnp.int32, (slots, slots), 0)
    high = lax.broadcasted_iota(jnp.int32, (slots, slots), 1)
    along = jnp.sum(jnp.where(low == high, lengths, 0.0), axis=1, keepdims=True)
    ends_column = jnp.sum(jnp.where(high <= low, lengths, 0.0), axis=1, keepdims=True)
    ends_row = jnp.sum(jnp.where(low <= high, along, 0.0), axis=0, keepdims=True)
    return ends_row, ends_column


def head_lanes(dtype):
    lane = lax.broadcasted_iota(jnp.int32, (1, 128), 1)
    return [(lane < 64).astype(F32).astype(dtype), (lane >= 64).astype(F32).astype(dtype)]


def stacked(values, masks):
    low, high = values[:, :128], values[:, 128:]
    none = jnp.zeros_like(low)
    return jnp.concatenate(
        [
            jnp.concatenate([low * masks[0], none], axis=1),
            jnp.concatenate([low * masks[1], none], axis=1),
            jnp.concatenate([none, high * masks[0]], axis=1),
            jnp.concatenate([none, high * masks[1]], axis=1),
        ],
        axis=0,
    )


def unstacked(values):
    rows = values.shape[0] // GROUP
    first = lax.broadcasted_iota(jnp.int32, (rows, 128), 1) < 64
    low = jnp.where(first, values[:rows, :128], values[rows : 2 * rows, :128])
    high = jnp.where(first, values[2 * rows : 3 * rows, 128:], values[3 * rows :, 128:])
    return jnp.concatenate([low, high], axis=1)


def neighbours(core, near_rows, far_rows):
    one, other = near_rows[...], far_rows[...]
    return jnp.where(core == 0, other, one), jnp.where(core == 0, one, other)


def fill_window(store, edge, own, count):
    store[:LEFT] = edge[EDGE - LEFT : EDGE]
    store[LEFT : LEFT + count] = own
    store[LEFT + count :] = edge[EDGE : EDGE + store.shape[0] - LEFT - count]


def forward_body(
    stream_len,
    where,
    domain,
    q,
    k,
    v,
    near_rows,
    far_rows,
    lengths,
    tags,
    gain,
    shift,
    wk,
    wv,
    bv,
    bmix,
    fgain,
    fshift,
    bup,
    x_in,
    wmix_in,
    out_grad_in,
    wup_in,
    wdown_in,
    probs_out,
    q_out,
    keys_out,
    values_out,
    active_out,
    resid_out,
    gr_out,
    gm_out,
    keep_d_out,
    send_d_out,
    keep_u_out,
    send_u_out,
    gdb_out,
    gub_out,
    gmb_out,
    gfg_out,
    gfs_out,
    keys,
    values,
    ends_row,
    ends_column,
    probs,
    mixed,
    resid,
    weight,
    nffn,
    branch,
    active,
    slope,
    gh,
    gr,
    gm,
    x,
    wmix,
    out_grad,
    wup,
    wdown,
    sems,
    block_sems,
    load_sems,
):
    count, width = q.shape
    ffw = wup.shape[1]
    half = width // 2
    first = where[0]
    core = where[1]
    copies = []
    loads = []
    for source, target in (
        (x_in, x),
        (wmix_in, wmix),
        (out_grad_in, out_grad),
        (wup_in, wup),
        (wdown_in, wdown),
    ):
        loads.append(pltpu.make_async_copy(source, target, load_sems.at[len(loads)]))
        loads[-1].start()

    def carry_out(source, target):
        copies.append(pltpu.make_async_copy(source, target, sems.at[len(copies)]))
        copies[-1].start()

    carry_out(q, q_out)
    edge = jnp.concatenate(neighbours(core, near_rows, far_rows), axis=0).astype(F32)
    unit, _ = norm_parts(edge)
    normed = (unit * gain[...] + shift[...]).astype(BF16)
    fill_window(keys, dot(normed, wk[...]).astype(BF16), k[...], count)
    fill_window(values, (dot(normed, wv[...]) + bv[...]).astype(BF16), v[...], count)
    carry_out(keys, keys_out)
    carry_out(values, values_out)
    row, column = slot_ends(lengths[...].astype(F32))
    ends_row[...] = row
    ends_column[...] = column

    kinds = tags[...]
    slot_weight = jnp.where(kinds == 0, domain[0], 0.0)
    slot_weight = jnp.where(kinds == 1, domain[1], slot_weight)
    slot_weight = jnp.where(kinds == 2, domain[2], slot_weight)
    slots = kinds.shape[1]
    slot = lax.broadcasted_iota(jnp.int32, (TILE, slots), 1).astype(F32)
    masks = head_lanes(BF16)
    lanes_all = GROUP * SUB
    key_at = lax.broadcasted_iota(jnp.int32, (WINDOW, lanes_all), 0)
    query_at = lax.broadcasted_iota(jnp.int32, (WINDOW, lanes_all), 1) % SUB
    near = (key_at >= query_at) & (key_at <= query_at + LEFT + RIGHT)

    def one_tile(step, carried):
        tile_at = pl.multiple_of(step * TILE, TILE)
        places = (first + tile_at + lax.broadcasted_iota(jnp.int32, (TILE, 1), 0)).astype(F32)
        seg = jnp.sum((ends_row[...] <= places).astype(F32), axis=1, keepdims=True)
        weight[pl.ds(tile_at, TILE), :] = jnp.broadcast_to(
            jnp.sum(jnp.where(seg == slot, slot_weight, 0.0), axis=1, keepdims=True),
            (TILE, weight.shape[1]),
        )
        allowed, scores, pieces = [], [], []
        for sub in range(TILE // SUB):
            at = first + tile_at + sub * SUB
            ours = (at + lax.broadcasted_iota(jnp.int32, (1, lanes_all), 1) % SUB).astype(F32)
            others = (at - LEFT + lax.broadcasted_iota(jnp.int32, (WINDOW, 1), 0)).astype(F32)
            seg_ours = jnp.sum((ends_column[...] <= ours).astype(F32), axis=0, keepdims=True)
            seg_others = jnp.sum((ends_row[...] <= others).astype(F32), axis=1, keepdims=True)
            seg_others = jnp.where(others < 0.0, -1.0, seg_others)
            seg_others = jnp.where(others >= float(stream_len), -2.0, seg_others)
            allowed.append(near & (seg_ours == seg_others))
            for group in range(2):
                pieces.append((sub, group))
        for sub, group in pieces:
            start = pl.multiple_of(tile_at + sub * SUB, SUB)
            lanes = slice(group * half, (group + 1) * half)
            queries = stacked(q[pl.ds(start, SUB), lanes], masks)
            scores.append(against(keys[pl.ds(start, WINDOW), lanes], queries))
        lows = []
        for (sub, group), score in zip(pieces, scores):
            score = jnp.where(allowed[sub], score, -1e30)
            grown = jnp.exp(score - jnp.max(score, axis=0, keepdims=True))
            low = (grown * (1.0 / jnp.sum(grown, axis=0, keepdims=True))).astype(BF16)
            probs[2 * (step * (TILE // SUB) + sub) + group] = low
            lows.append(low)
        for (sub, group), low in zip(pieces, lows):
            start = pl.multiple_of(tile_at + sub * SUB, SUB)
            lanes = slice(group * half, (group + 1) * half)
            heads = unstacked(over_rows(low, values[pl.ds(start, WINDOW), lanes]))
            mixed[pl.ds(start, SUB), lanes] = heads.astype(BF16)
        return carried

    lax.fori_loop(0, count // TILE, one_tile, 0)
    carry_out(probs, probs_out)
    for load in loads[:3]:
        load.wait()
    bias = jnp.zeros((1, width), F32)
    for rows in tiles(count):
        summed = x[rows, :].astype(F32) + dot(mixed[rows, :], wmix[...]) + bmix[...]
        resid[rows, :] = summed
        unit, _ = norm_parts(summed)
        nffn[rows, :] = (unit * fgain[...] + fshift[...]).astype(BF16)
        scaled = scaled_rows(out_grad[rows, :], weight[rows, :]).astype(BF16)
        branch[rows, :] = scaled
        bias = bias + row_sum(scaled.astype(F32))
    gdb_out[...] = bias
    carry_out(resid, resid_out)

    def one_block(block, carried):
        at = pl.multiple_of(block * width, width)
        lanes = pl.ds(at, width)
        for rows in tiles(count):
            hidden = dot(nffn[rows, :], wup[:, lanes]) + bup[:, lanes]
            below = 1.0 + lax.erf(hidden * math.sqrt(0.5))
            bell = jnp.exp2(
                hidden * hidden * (-0.5 * LOG2E) + math.log2(2.0 / math.sqrt(2.0 * math.pi))
            )
            active[rows, lanes] = ((hidden * 0.5) * below).astype(BF16)
            slope[rows, :] = (below + hidden * bell).astype(BF16)
        pltpu.make_async_copy(
            active.at[:, lanes], active_out.at[:, lanes], block_sems.at[block]
        ).start()
        keep_d_out[:, lanes], send_d_out[:, lanes] = halves(
            over_rows(active[:, lanes], branch[...]), core
        )
        bias = jnp.zeros((1, width), F32)
        for rows in tiles(count):
            half_branch = branch[rows, :] * jnp.asarray(0.5, BF16)
            grad = against(half_branch, wdown[lanes, :]) * slope[rows, :].astype(F32)
            low = grad.astype(BF16)
            gh[rows, lanes] = low
            bias = bias + row_sum(low.astype(F32))
        gub_out[:, lanes] = bias
        keep_u_out[:, lanes], send_u_out[:, lanes] = halves(
            over_rows(nffn[...], gh[:, lanes]), core
        )
        return carried

    for load in loads[3:]:
        load.wait()
    lax.fori_loop(0, ffw // width, one_block, 0)
    by_bias, by_gain, by_shift = (jnp.zeros((1, width), F32) for _ in range(3))
    for rows in tiles(count):
        grad = against(gh[rows, :], wup[...])
        unit, inverse = norm_parts(resid[rows, :])
        by_gain = by_gain + row_sum(grad * unit)
        by_shift = by_shift + row_sum(grad)
        grad_resid = scaled_rows(out_grad[rows, :], weight[rows, :]) + norm_back(
            grad * fgain[...], unit, inverse
        )
        gr[rows, :] = grad_resid
        low = grad_resid.astype(BF16)
        branch[rows, :] = low
        by_bias = by_bias + row_sum(low.astype(F32))
        gm[rows, :] = against(low, wmix[...]).astype(BF16)
    carry_out(gr, gr_out)
    carry_out(gm, gm_out)
    there = slice(ffw, ffw + width)
    keep_u_out[:, there], send_u_out[:, there] = halves(over_rows(mixed[...], branch[...]), core)
    gmb_out[...] = by_bias
    gfg_out[...] = by_gain
    gfs_out[...] = by_shift
    for block in range(ffw // width):
        lanes = slice(block * width, (block + 1) * width)
        copies.append(
            pltpu.make_async_copy(
                active.at[:, lanes], active_out.at[:, lanes], block_sems.at[block]
            )
        )
    for copy in copies:
        copy.wait()


def output_body(bdown, wdown_in, resid_in, active_in, out, wdown, resid, active, low, sems):
    steps = tiles(resid.shape[0])

    def moved(source, target, place):
        return pltpu.make_async_copy(source, target, sems.at[place])

    loads = [moved(wdown_in, wdown, 0)]
    for i, rows in enumerate(steps):
        loads.append(moved(active_in.at[rows, :], active.at[rows, :], 1 + 2 * i))
        loads.append(moved(resid_in.at[rows, :], resid.at[rows, :], 2 + 2 * i))
    for load in loads:
        load.start()
    loads[0].wait()
    stores = []
    for i, rows in enumerate(steps):
        loads[1 + 2 * i].wait()
        loads[2 + 2 * i].wait()
        low[rows, :] = (
            resid[rows, :] + dot(active[rows, :], wdown[...]) + bdown[...]
        ).astype(BF16)
        stores.append(moved(low.at[rows, :], out.at[rows, :], 1 + 2 * len(steps) + i))
        stores[-1].start()
    for store in stores:
        store.wait()


def attend_back_body(
    gm_in,
    values_in,
    probs_in,
    keys_in,
    q_in,
    x_in,
    unit,
    gq,
    gk,
    gv,
    edge,
    gq_out,
    gk_out,
    gv_out,
    gm,
    values,
    probs,
    keys,
    q,
    x,
    gk_window,
    gv_window,
    sems,
    load_sems,
):
    count, width = q.shape
    half = width // 2
    steps = count // TILE
    spill = keys.shape[0] - count
    blocks = probs.shape[0] // steps

    def loads(step):
        def load(place, source, target, start, size):
            part = pl.ds(start, size)
            return pltpu.make_async_copy(
                source.at[part], target.at[part], load_sems.at[place, step]
            )

        start = step * TILE
        first = start if isinstance(step, int) else pl.multiple_of(start + spill, spill)
        size = TILE + spill if isinstance(step, int) else TILE
        return [
            load(0, gm_in, gm, start, TILE),
            load(1, values_in, values, first, size),
            load(2, probs_in, probs, step * blocks, blocks),
            load(3, keys_in, keys, first, size),
            load(4, q_in, q, start, TILE),
            load(5, x_in, x, start, TILE),
        ]

    def begin(step, carried):
        for load in loads(step):
            load.start()
        return carried

    for load in loads(0):
        load.start()
    lax.fori_loop(1, steps, begin, 0)
    gk_window[...] = jnp.zeros_like(gk_window)
    gv_window[...] = jnp.zeros_like(gv_window)
    scale = (width // HEADS) ** (-0.5)
    masks = head_lanes(BF16)
    pieces = [(sub, group) for sub in range(TILE // SUB) for group in range(2)]

    def one_tile(step, carried):
        tile_at = pl.multiple_of(step * TILE, TILE)

        @pl.when(step == 0)
        def _():
            for load in loads(0):
                load.wait()

        @pl.when(step > 0)
        def _():
            for load in loads(step):
                load.wait()

        def spot(sub, group):
            start = pl.multiple_of(tile_at + sub * SUB, SUB)
            return pl.ds(start, SUB), pl.ds(start, WINDOW), slice(group * half, (group + 1) * half)

        tile_rows = pl.ds(tile_at, TILE)
        unit[tile_rows, :] = norm_parts(x[tile_rows, :].astype(F32))[0].astype(BF16)
        pulls, grads = [], []
        for sub, group in pieces:
            rows, window, lanes = spot(sub, group)
            pulled = stacked(gm[rows, lanes], masks)
            pulls.append(pulled)
            grads.append(against(values[window, lanes], pulled))
        lows = []
        for (sub, group), grad in zip(pieces, grads):
            wide = probs[2 * (step * (TILE // SUB) + sub) + group].astype(F32)
            product = wide * grad
            lows.append((product - wide * jnp.sum(product, axis=0, keepdims=True)).astype(BF16))
        for (sub, group), pulled, low in zip(pieces, pulls, lows):
            rows, window, lanes = spot(sub, group)
            queries = stacked(q[rows, lanes], masks)
            gq[rows, lanes] = (unstacked(over_rows(low, keys[window, lanes])) * scale).astype(BF16)
            gk_window[window, lanes] += dot(low, queries)
            gv_window[window, lanes] += dot(
                probs[2 * (step * (TILE // SUB) + sub) + group], pulled
            )
        return carried

    lax.fori_loop(0, count // TILE, one_tile, 0)
    stores = []

    def store(source, target):
        stores.append(pltpu.make_async_copy(source, target, sems.at[len(stores)]))
        stores[-1].start()

    store(gq, gq_out)
    for place, (window, grad, out) in enumerate(
        ((gk_window, gk, gk_out), (gv_window, gv, gv_out))
    ):
        lanes = slice(place * width, (place + 1) * width)
        grad[...] = window[LEFT : LEFT + count].astype(BF16)
        store(grad, out)
        edge[:LEFT, lanes] = window[:LEFT].astype(BF16)
        edge[LEFT : LEFT + RIGHT, lanes] = window[LEFT + count : LEFT + count + RIGHT].astype(BF16)
    for one in stores:
        one.wait()


def edge_frames(core, near_rows, far_rows):
    before, behind = neighbours(core, near_rows, far_rows)
    return jnp.concatenate([before[EDGE - LEFT :], behind[:RIGHT]], axis=0).astype(F32)


def weights_body(
    where,
    unit,
    gq,
    gk,
    gv,
    edge,
    near_rows,
    far_rows,
    gain,
    shift,
    gdb,
    gub,
    gmb,
    gfg,
    gfs,
    wq_in,
    wk_in,
    wv_in,
    keep_out,
    send_out,
    wq,
    wk,
    wv,
    sums,
    vec,
    sems,
):
    width = unit.shape[1]
    core = where[1]
    loads = []
    for source, target in ((wq_in, wq), (wk_in, wk), (wv_in, wv)):
        loads.append(pltpu.make_async_copy(source, target, sems.at[len(loads)]))
        loads[-1].start()
    far_low = norm_parts(edge_frames(core, near_rows, far_rows))[0].astype(BF16)
    gain_column = jnp.transpose(jnp.broadcast_to(gain[...], (128, width)))[:, :1]
    shift_column = jnp.transpose(jnp.broadcast_to(shift[...], (128, width)))[:, :1]
    columns = [row_sum(grad[...].astype(F32)) for grad in (gq, gk, gv)]
    by_gain = jnp.zeros((width, 1), F32)
    by_shift = jnp.zeros((width, 1), F32)
    for place, (grad, weight) in enumerate(((gq, wq), (gk, wk), (gv, wv))):
        product = over_rows(unit[...], grad[...])
        column = columns[place]
        if place > 0:
            there = slice((place - 1) * width, place * width)
            product = product + over_rows(far_low, edge[: LEFT + RIGHT, there])
            column = column + row_sum(edge[: LEFT + RIGHT, there].astype(F32))
        lanes = slice(place * width, (place + 1) * width)
        keep_out[:, lanes], send_out[:, lanes] = halves(
            product * gain_column + shift_column * column, core
        )
        loads[place].wait()
        wide = weight[...].astype(F32)
        by_gain = by_gain + jnp.sum(wide * product, axis=1, keepdims=True)
        by_shift = by_shift + jnp.sum(wide * column, axis=1, keepdims=True)
        if place != 1:
            sums[place // 2 : place // 2 + 1] = column
    sums[2:3] = jnp.transpose(jnp.broadcast_to(by_gain, (width, 128)))[:1]
    sums[3:4] = jnp.transpose(jnp.broadcast_to(by_shift, (width, 128)))[:1]
    vec[...] = jnp.zeros_like(vec)
    row = 0
    for ref in [sums.at[i : i + 1] for i in range(4)] + [gmb, gfg, gfs, gdb, gub]:
        for part in range(0, ref.shape[1], 128):
            vec[row : row + 1] = ref[:, part : part + 128]
            row += 1
    keep_out[:, 3 * width :], send_out[:, 3 * width :] = halves(vec[...], core)


def input_body(
    where,
    x,
    gq,
    gk,
    gv,
    gr,
    edge,
    near_rows,
    far_rows,
    gain,
    wq,
    wk,
    wv,
    own_edge_out,
    near_edge_out,
    far_edge_out,
    ig_out,
    ig,
    sems,
):
    count, width = x.shape
    core = where[1]
    unit, inverse = norm_parts(edge_frames(core, near_rows, far_rows))
    cut = slice(0, LEFT + RIGHT)
    grad = against(edge[cut, :width], wk[...]) + against(edge[cut, width:], wv[...])
    grad = norm_back(grad * gain[...], unit, inverse)
    before = jnp.concatenate([jnp.zeros((EDGE - LEFT, width), F32), grad[:LEFT]], axis=0)
    behind = jnp.concatenate([grad[LEFT:], jnp.zeros((EDGE - RIGHT, width), F32)], axis=0)
    near_edge_out[...] = jnp.where(core == 0, behind, before)
    far_edge_out[...] = jnp.where(core == 0, before, behind)
    stores = []
    for rows in tiles(count):
        unit, inverse = norm_parts(x[rows, :].astype(F32))
        grad = (
            against(gq[rows, :], wq[...])
            + against(gk[rows, :], wk[...])
            + against(gv[rows, :], wv[...])
        )
        result = gr[rows, :] + norm_back(grad * gain[...], unit, inverse)
        ig[rows, :] = result.astype(BF16)
        stores.append(
            pltpu.make_async_copy(
                ig.at[rows, :], ig_out.at[rows, :], sems.at[len(stores)]
            )
        )
        stores[-1].start()
        if rows.start == 0:
            own_edge_out[:EDGE] = result[:EDGE]
        if rows.stop == count:
            own_edge_out[EDGE:] = result[-EDGE:]
    for store in stores:
        store.wait()


def swapped(value, axis, mask):
    count = lax.axis_size(axis)
    return lax.ppermute(value, axis, [(i, i ^ mask) for i in range(count)])


def across(value, first):
    tm, items = lax.axis_size("tm"), lax.axis_size("items")
    pairs = []
    for i in range(tm):
        for j in range(items):
            along_x = (i % 2 == 0) == first
            pairs.append((i * items + j, i * items + (j ^ 1) if along_x else (i ^ 2) * items + j))
    return lax.ppermute(value, ("tm", "items"), pairs)


def cut(value, place, rows):
    return lax.dynamic_slice_in_dim(value, place * rows, rows, 0)


def total_of(parts):
    total = parts[0].astype(F32)
    for part in parts[1:]:
        total = total + part.astype(F32)
    return total.astype(BF16)


def paired(own, got, bit):
    return jnp.where(bit == 0, jnp.concatenate([own, got]), jnp.concatenate([got, own]))


def whole_body(places, where, own, got, *outs):
    blocks, (lane, first) = places
    rows = own.shape[0]
    for place, part in ((where[1], own), (1 - where[1], got)):
        for out, start, row in blocks:
            width = outs[out].shape[1]
            outs[out][pl.ds(pl.multiple_of(row + place * rows, rows), rows), :] = part[
                :, start : start + width
            ].astype(F32)
    if first < len(outs):
        count = sum(out.shape[1] for out in outs[first:]) // 128
        low = jnp.where(where[1] == 0, own[:count, lane:], got[:count, lane:]).astype(F32)
        row = 0
        for out in outs[first:]:
            for at in range(0, out.shape[1], 128):
                out[:, at : at + 128] = low[row : row + 1]
                row += 1


class Place:
    def __init__(self):
        tm = lax.axis_index("tm").astype(jnp.int32)
        x_bit = lax.axis_index("items").astype(jnp.int32) % 2
        y_bit = (tm // 2) % 2
        self.core = tm % 2
        self.steps = [
            (jnp.where(self.core == 0, x_bit, y_bit), lambda value: across(value, True)),
            (jnp.where(self.core == 0, y_bit, x_bit), lambda value: across(value, False)),
            ((tm // 4) % 2, lambda value: swapped(value, "tm", 4)),
            ((tm // 8) % 2, lambda value: swapped(value, "tm", 8)),
        ]


def fold_body(step, where, keep, got, mine_out, other_out):
    rows = keep.shape[0] // 2
    bit = where[2 + step]
    for place, out in ((bit, mine_out), (1 - bit, other_out)):
        at = pl.ds(pl.multiple_of(place * rows, rows), rows)
        out[...] = total_of([keep[at, :], got[at, :]])


class Sum:
    def __init__(self, place, halved, folds, keep, send):
        self.place = place
        self.folds = folds
        self.parts = [keep, swapped(send, "tm", 1)]
        self.todo = [functools.partial(self.exchange, step, step < halved) for step in range(4)]
        self.todo += [functools.partial(self.spread, step) for step in range(halved - 1, -1, -1)]
        self.todo += [functools.partial(self.spread, -1)]
        self.bit = None

    def held(self):
        return self.parts[0]

    def hold(self, value):
        self.parts[0] = value

    def advance(self):
        self.todo.pop(0)()

    def exchange(self, step, halve):
        bit, exchange = self.place.steps[step]
        if halve and step < self.folds:
            rows, width = self.parts[0].shape
            mine, other = call(
                functools.partial(fold_body, step),
                "fold",
                self.parts,
                [near(rows // 2, width, BF16)] * 2,
                scalars=[self.place.where],
                vmem=8,
                moved=4 * MIB,
            )
        elif halve:
            rows = self.parts[0].shape[0] // 2
            mine, other = (
                total_of([cut(part, at, rows) for part in self.parts]) for at in (bit, 1 - bit)
            )
        else:
            mine = other = total_of(self.parts)
        self.parts = [mine, exchange(other)]

    def spread(self, step):
        own = total_of(self.parts) if self.bit is None else paired(*self.parts, self.bit)
        if step >= 0:
            self.bit, exchange = self.place.steps[step]
            self.parts = [own, exchange(own)]
        else:
            self.parts = [own, swapped(own, "tm", 1)]

    def whole(self, where, places, outs):
        return call(
            functools.partial(whole_body, places),
            "whole",
            self.parts,
            outs,
            scalars=[where],
            vmem=24,
            moved=6 * MIB,
        )


class PlainSum:
    def __init__(self, place, halved, folds, keep, send):
        self.place = place
        self.todo = []
        self.parts = [keep, send]

    def held(self):
        return self.parts[0]

    def hold(self, value):
        self.parts[0] = value

    def advance(self):
        pass

    def whole(self, where, places, outs):
        keep, send = self.parts
        low = jnp.where(self.place.core == 0, keep, send)
        high = jnp.where(self.place.core == 0, send, keep)
        total = lax.psum(jnp.concatenate([low, high], axis=0), ("tm", "items"))
        blocks, vectors = places
        made = [[] for _, _ in outs]
        for out, lane, _ in blocks:
            made[out].append(total[:, lane : lane + outs[out][0].shape[1]])
        lane, first = vectors
        for out in range(first, len(outs)):
            size = outs[out][0].shape[1]
            start = sum(made_out[0].shape[1] // 128 for _, made_out in enumerate(made[first:out]))
            rows = total[start : start + size // 128, lane : lane + 128]
            made[out].append(rows.reshape(1, size))
        return [jnp.concatenate(parts, axis=0).astype(F32) for parts in made]


def stays(array):
    return pltpu.with_memory_space_constraint(array, pltpu.HBM)


def here(array):
    return pltpu.with_memory_space_constraint(array, pltpu.VMEM)


def ordered(first, second):
    return lax.optimization_barrier((first, second))[1]


def follow(first, second):
    second.hold(ordered(first.held(), second.held()))


def along(value):
    count = lax.axis_size("tm")
    pairs = [(i, i + 1) for i in range(1, count - 1, 2)]
    return lax.ppermute(value, "tm", pairs + [(to, of) for of, to in pairs])


def local(
    fast,
    frames,
    out_grad,
    item_lengths,
    domain_tags,
    domain_weight,
    wq,
    bq,
    wk,
    wv,
    bv,
    wmix,
    bmix,
    again,
    ashift,
    fgain,
    fshift,
    wup,
    bup,
    wdown,
    bdown,
):
    frames = frames[0]
    out_grad = out_grad[0]
    count, width = frames.shape
    ffw = wup.shape[1]
    slots = item_lengths.shape[1]
    stream_len = count * lax.axis_size("tm")
    reach = count + WINDOW - SUB
    unit_flops = 2 * count * width * width
    parts = ffw // width
    bq, bv, bmix, again, ashift, fgain, fshift, bup, bdown = (
        vector[None] for vector in (bq, bv, bmix, again, ashift, fgain, fshift, bup, bdown)
    )
    place = Place()
    bits = [bit for bit, _ in place.steps]
    where = jnp.stack([lax.axis_index("tm") * count, place.core] + bits).astype(jnp.int32)
    place.where = where
    near_end = jnp.where(place.core == 0, count - EDGE, 0)
    near_rows = swapped(lax.dynamic_slice_in_dim(frames, near_end, EDGE, 0), "tm", 1)
    far_rows = along(lax.dynamic_slice_in_dim(frames, count - EDGE - near_end, EDGE, 0))
    kind = Sum if fast else PlainSum
    vector = free(1, width, F32)
    edge_wide = free(2 * EDGE, width, F32)
    edge_half = free(EDGE, width, F32)
    model_low = (count, width, BF16)
    model_wide = (count, width, F32)
    hidden_low = (count, ffw, BF16)
    blocks = (2 * count // SUB, WINDOW, GROUP * SUB, BF16)
    windowed = (reach, width)
    low_scratch = pltpu.VMEM((count, width), BF16)

    q, k, v = call(
        project_body,
        "project",
        [stays(a) for a in (frames, again, ashift, wq, wk, wv, bq, bv)],
        [near(*model_low)] * 3,
        flops=3 * unit_flops,
        moved=6 * MIB,
    )
    (
        probs,
        q,
        keys,
        values,
        active,
        resid,
        gr,
        gm,
        keep_d,
        send_d,
        keep_u,
        send_u,
        gdb,
        gub,
        gmb,
        gfg,
        gfs,
    ) = call(
        functools.partial(forward_body, stream_len),
        "forward",
        [q, k, v, near_rows, far_rows]
        + [stays(a) for a in (item_lengths, domain_tags, again, ashift, wk, wv)]
        + [stays(a) for a in (bv, bmix, fgain, fshift, bup)],
        [copied(*blocks), copied(*model_low), copied(*windowed, BF16), copied(*windowed, BF16)]
        + [copied(*hidden_low), copied(*model_wide), copied(*model_wide), copied(*model_low)]
        + [near(width // 2, ffw, BF16)] * 2
        + [near(width // 2, ffw + width, BF16)] * 2
        + [vector, free(1, ffw, F32), vector, vector, vector],
        scratch=[
            pltpu.VMEM(windowed, BF16),
            pltpu.VMEM(windowed, BF16),
            pltpu.VMEM((1, slots), F32),
            pltpu.VMEM((slots, 1), F32),
            pltpu.VMEM(blocks[:-1], BF16),
            pltpu.VMEM((count, width), BF16),
            pltpu.VMEM((count, width), F32),
            pltpu.VMEM((count, 128), F32),
            pltpu.VMEM((count, width), BF16),
            pltpu.VMEM((count, width), BF16),
            pltpu.VMEM((count, ffw), BF16),
            pltpu.VMEM((count, width), BF16),
            pltpu.VMEM((count, ffw), BF16),
            pltpu.VMEM((count, width), F32),
            pltpu.VMEM((count, width), BF16),
            pltpu.VMEM((count, width), BF16),
            pltpu.VMEM((width, width), BF16),
            pltpu.VMEM((count, width), BF16),
            pltpu.VMEM((width, ffw), BF16),
            pltpu.VMEM((ffw, width), BF16),
            pltpu.SemaphoreType.DMA((7,)),
            pltpu.SemaphoreType.DMA((parts,)),
            pltpu.SemaphoreType.DMA((5,)),
        ],
        scalars=[where, domain_weight],
        far_ins=[stays(a) for a in (frames, wmix, out_grad, wup, wdown)],
        vmem=40,
        flops=(6 + 5 * parts) * unit_flops,
        moved=24 * MIB,
    )
    down = kind(place, 3, 2, keep_d, send_d)
    up = kind(place, 3, 1, keep_u, send_u)

    down.advance()
    follow(down, up)
    up.advance()
    gm = ordered(up.held(), gm)
    (unit, gq, gk, gv, edge, gq_far, gk_far, gv_far) = call(
        attend_back_body,
        "attend_back",
        [],
        [near(*model_low)] * 4
        + [near(EDGE, 2 * width, BF16)]
        + [copied(*model_low)] * 3,
        scratch=[
            low_scratch,
            pltpu.VMEM(windowed, BF16),
            pltpu.VMEM(blocks[:-1], BF16),
            pltpu.VMEM(windowed, BF16),
            low_scratch,
            low_scratch,
            pltpu.VMEM(windowed, F32),
            pltpu.VMEM(windowed, F32),
            pltpu.SemaphoreType.DMA((3,)),
            pltpu.SemaphoreType.DMA((6, count // TILE)),
        ],
        far_ins=[stays(a) for a in (gm, values, probs, keys, q, frames)],
        vmem=20,
        flops=8 * unit_flops,
        moved=10 * MIB,
    )
    down.hold(ordered(edge, down.held()))
    down.advance()
    edge = ordered(down.held(), edge)
    rest_half = near(width // 2, 3 * width + 128, BF16)
    square_low = pltpu.VMEM((width, width), BF16)
    keep_r, send_r = call(
        weights_body,
        "weights",
        [unit, gq, gk, gv, edge, near_rows, far_rows]
        + [stays(a) for a in (again, ashift)]
        + [gdb, gub, gmb, gfg, gfs],
        [rest_half, rest_half],
        scratch=[square_low] * 3
        + [pltpu.VMEM((8, width), F32), pltpu.VMEM((width, 128), F32)]
        + [pltpu.SemaphoreType.DMA((3,))],
        scalars=[where],
        far_ins=[stays(a) for a in (wq, wk, wv)],
        vmem=16,
        flops=3 * unit_flops,
        moved=8 * MIB,
    )
    rest = kind(place, 2, 0, keep_r, send_r)
    sums = {"d": down, "u": up, "r": rest}
    latest = keep_r
    for turn in ORDER:
        if turn == "o":
            active = ordered(latest, active)
            (output,) = call(
                output_body,
                "output",
                [stays(bdown)],
                [copied(*model_low)],
                scratch=[
                    pltpu.VMEM((ffw, width), BF16),
                    pltpu.VMEM((count, width), F32),
                    pltpu.VMEM((count, ffw), BF16),
                    pltpu.VMEM((count, width), BF16),
                    pltpu.SemaphoreType.DMA((1 + 3 * (count // TILE),)),
                ],
                far_ins=[stays(a) for a in (wdown, resid, active)],
                vmem=20,
                flops=parts * unit_flops,
                moved=9 * MIB,
            )
            latest = output
        elif turn == "n":
            gr = ordered(latest, gr)
            own_edge, near_edge, far_edge, ig = call(
                input_body,
                "input",
                [stays(a) for a in (frames, gq_far, gk_far, gv_far, gr)]
                + [edge, near_rows, far_rows]
                + [stays(a) for a in (again, wq, wk, wv)],
                [edge_wide, edge_half, edge_half, copied(*model_low)],
                scratch=[
                    pltpu.VMEM((count, width), BF16),
                    pltpu.SemaphoreType.DMA((count // TILE,)),
                ],
                scalars=[where],
                vmem=24,
                flops=3 * unit_flops,
                moved=8 * MIB,
            )
            latest = far_edge
        elif turn == "e":
            far_edge = ordered(latest, far_edge)
            near_got = swapped(near_edge, "tm", 1)
            far_got = along(far_edge)
        elif turn == "i":
            far_got = ordered(latest, far_got)
            low = place.core == 0
            first = (own_edge[:EDGE] + jnp.where(low, far_got, near_got)).astype(BF16)
            last = (own_edge[EDGE:] + jnp.where(low, near_got, far_got)).astype(BF16)
            latest = (first, last)
        else:
            one = sums[turn]
            one.hold(ordered(latest, one.held()))
            if one.todo:
                one.advance()
                latest = one.held()
            elif one is down:
                places = [(0, at, at) for at in range(0, ffw, width)], (0, 1)
                (grad_down,) = one.whole(where, places, [free(ffw, width, F32)])
                latest = grad_down
            elif one is up:
                places = [(0, 0, 0), (1, ffw, 0)], (0, 2)
                outs = [free(width, ffw, F32), free(width, width, F32)]
                grad_up, grad_mix = one.whole(where, places, outs)
                latest = grad_mix
    ig = ig.at[:EDGE].set(first)
    ig = ig.at[count - EDGE :].set(last)
    places = [(i, i * width, 0) for i in range(3)], (3 * width, 3)
    outs = [free(width, width, F32)] * 3 + [vector] * 8 + [free(1, ffw, F32)]
    grad_q, grad_k, grad_v, *vectors = rest.whole(where, places, outs)
    gqb, gvb, gag, gas, gmb, gfg, gfs, gdb, gub = (made[0] for made in vectors)
    return (
        output[None],
        ig[None],
        grad_q,
        gqb,
        grad_k,
        grad_v,
        gvb,
        grad_mix,
        gmb,
        gag,
        gas,
        gfg,
        gfs,
        grad_up,
        gub,
        grad_down,
        gdb,
    )


def solution(mesh):
    rows = P("items", "tm", None)
    in_specs = (rows, rows, P("items", None), P("items", None)) + (P(),) * 16
    out_specs = (rows, rows) + (P(),) * 15
    fast = mesh.shape["tm"] == 16 and mesh.shape["items"] == 2
    return jax.shard_map(
        functools.partial(local, fast),
        mesh=mesh,
        in_specs=in_specs,
        out_specs=out_specs,
        check_vma=False,
    )
```

```python
import functools
import math

import jax
import jax.numpy as jnp
from jax import lax
from jax.experimental import pallas as pl
from jax.experimental.pallas import tpu as pltpu
from jax.sharding import PartitionSpec as P

HEADS = 8
LEFT = 10
RIGHT = 2
EDGE = 16
TILE = 256
SUB = 32
WINDOW = 48
GROUP = 4
MIB = 1 << 20
ORDER = "udrudrurdnurdudreudiroudru"
LOG2E = 1.0 / math.log(2.0)
F32 = jnp.float32
BF16 = jnp.bfloat16


def dot(left, right):
    return jnp.dot(left, right, preferred_element_type=F32)


def against(left, right):
    return lax.dot_general(left, right, (((1,), (1,)), ((), ())), preferred_element_type=F32)


def over_rows(left, right):
    return lax.dot_general(left, right, (((0,), (0,)), ((), ())), preferred_element_type=F32)


def norm_parts(values):
    centered = values - jnp.mean(values, axis=-1, keepdims=True)
    variance = jnp.mean(centered * centered, axis=-1, keepdims=True)
    inverse = lax.rsqrt(variance + 1e-05)
    return centered * inverse, inverse


def norm_back(upstream, unit, inverse):
    return inverse * (
        upstream
        - jnp.mean(upstream, axis=-1, keepdims=True)
        - unit * jnp.mean(upstream * unit, axis=-1, keepdims=True)
    )


def row_sum(values):
    return jnp.sum(values, axis=0, keepdims=True)


def scaled_rows(values, weight):
    return values.astype(F32) * jnp.tile(weight, (1, values.shape[1] // 128))


def halves(values, core):
    rows = values.shape[0] // 2
    low, high = values[:rows].astype(BF16), values[rows:].astype(BF16)
    return jnp.where(core == 0, low, high), jnp.where(core == 0, high, low)


def tiles(count, rows=TILE):
    return [slice(start, start + rows) for start in range(0, count, rows)]


def shaped(shape, dtype):
    return jax.ShapeDtypeStruct(shape, dtype)


ANY = pl.BlockSpec(memory_space=pl.ANY)
SCALARS = pl.BlockSpec(memory_space=pltpu.SMEM)
WHOLE = pl.BlockSpec(memory_space=pltpu.VMEM)


def call(body, name, ins, outs, scratch=(), scalars=(), far_ins=(), vmem=10, flops=0, moved=0):
    return pl.pallas_call(
        body,
        in_specs=[SCALARS] * len(scalars) + [WHOLE] * len(ins) + [ANY] * len(far_ins),
        out_specs=[ANY if own_copies else WHOLE for _, own_copies in outs],
        out_shape=[out for out, _ in outs],
        scratch_shapes=list(scratch),
        name=name,
        compiler_params=pltpu.CompilerParams(vmem_limit_bytes=vmem * MIB),
        cost_estimate=pl.CostEstimate(flops=flops, bytes_accessed=moved, transcendentals=0),
    )(*scalars, *ins, *far_ins)


def near(*shape):
    return pltpu.VMEM(shape[:-1], shape[-1]), False


def copied(*shape):
    return pltpu.HBM(shape[:-1], shape[-1]), True


def free(*shape):
    return shaped(shape[:-1], shape[-1]), False


def project_body(x, gain, shift, wq, wk, wv, bq, bv, q_out, k_out, v_out):
    scale = (wq.shape[1] // HEADS) ** (-0.5)
    for rows in tiles(x.shape[0]):
        unit, _ = norm_parts(x[rows, :].astype(F32))
        normed = (unit * gain[...] + shift[...]).astype(BF16)
        q_out[rows, :] = (dot(normed, wq[...]) + bq[...]).astype(BF16) * jnp.asarray(scale, BF16)
        k_out[rows, :] = dot(normed, wk[...]).astype(BF16)
        v_out[rows, :] = (dot(normed, wv[...]) + bv[...]).astype(BF16)


def slot_ends(lengths):
    slots = lengths.shape[1]
    low = lax.broadcasted_iota(jnp.int32, (slots, slots), 0)
    high = lax.broadcasted_iota(jnp.int32, (slots, slots), 1)
    along = jnp.sum(jnp.where(low == high, lengths, 0.0), axis=1, keepdims=True)
    ends_column = jnp.sum(jnp.where(high <= low, lengths, 0.0), axis=1, keepdims=True)
    ends_row = jnp.sum(jnp.where(low <= high, along, 0.0), axis=0, keepdims=True)
    return ends_row, ends_column


def head_lanes(dtype):
    lane = lax.broadcasted_iota(jnp.int32, (1, 128), 1)
    return [(lane < 64).astype(F32).astype(dtype), (lane >= 64).astype(F32).astype(dtype)]


def stacked(values, masks):
    low, high = values[:, :128], values[:, 128:]
    none = jnp.zeros_like(low)
    return jnp.concatenate(
        [
            jnp.concatenate([low * masks[0], none], axis=1),
            jnp.concatenate([low * masks[1], none], axis=1),
            jnp.concatenate([none, high * masks[0]], axis=1),
            jnp.concatenate([none, high * masks[1]], axis=1),
        ],
        axis=0,
    )


def unstacked(values):
    rows = values.shape[0] // GROUP
    first = lax.broadcasted_iota(jnp.int32, (rows, 128), 1) < 64
    low = jnp.where(first, values[:rows, :128], values[rows : 2 * rows, :128])
    high = jnp.where(first, values[2 * rows : 3 * rows, 128:], values[3 * rows :, 128:])
    return jnp.concatenate([low, high], axis=1)


def neighbours(core, near_rows, far_rows):
    one, other = near_rows[...], far_rows[...]
    return jnp.where(core == 0, other, one), jnp.where(core == 0, one, other)


def fill_window(store, edge, own, count):
    store[:LEFT] = edge[EDGE - LEFT : EDGE]
    store[LEFT : LEFT + count] = own
    store[LEFT + count :] = edge[EDGE : EDGE + store.shape[0] - LEFT - count]


def forward_body(
    stream_len,
    where,
    domain,
    q,
    k,
    v,
    near_rows,
    far_rows,
    lengths,
    tags,
    gain,
    shift,
    wk,
    wv,
    bv,
    bmix,
    fgain,
    fshift,
    bup,
    x_in,
    wmix_in,
    out_grad_in,
    wup_in,
    wdown_in,
    probs_out,
    q_out,
    keys_out,
    values_out,
    active_out,
    resid_out,
    gr_out,
    gm_out,
    keep_d_out,
    send_d_out,
    keep_u_out,
    send_u_out,
    gdb_out,
    gub_out,
    gmb_out,
    gfg_out,
    gfs_out,
    keys,
    values,
    ends_row,
    ends_column,
    probs,
    mixed,
    resid,
    weight,
    nffn,
    branch,
    active,
    slope,
    gh,
    gr,
    gm,
    x,
    wmix,
    out_grad,
    wup,
    wdown,
    sems,
    block_sems,
    load_sems,
):
    count, width = q.shape
    ffw = wup.shape[1]
    half = width // 2
    first = where[0]
    core = where[1]
    copies = []
    loads = []
    for source, target in (
        (x_in, x),
        (wmix_in, wmix),
        (out_grad_in, out_grad),
        (wup_in, wup),
        (wdown_in, wdown),
    ):
        loads.append(pltpu.make_async_copy(source, target, load_sems.at[len(loads)]))
        loads[-1].start()

    def carry_out(source, target):
        copies.append(pltpu.make_async_copy(source, target, sems.at[len(copies)]))
        copies[-1].start()

    carry_out(q, q_out)
    edge = jnp.concatenate(neighbours(core, near_rows, far_rows), axis=0).astype(F32)
    unit, _ = norm_parts(edge)
    normed = (unit * gain[...] + shift[...]).astype(BF16)
    fill_window(keys, dot(normed, wk[...]).astype(BF16), k[...], count)
    fill_window(values, (dot(normed, wv[...]) + bv[...]).astype(BF16), v[...], count)
    carry_out(keys, keys_out)
    carry_out(values, values_out)
    row, column = slot_ends(lengths[...].astype(F32))
    ends_row[...] = row
    ends_column[...] = column

    kinds = tags[...]
    slot_weight = jnp.where(kinds == 0, domain[0], 0.0)
    slot_weight = jnp.where(kinds == 1, domain[1], slot_weight)
    slot_weight = jnp.where(kinds == 2, domain[2], slot_weight)
    slots = kinds.shape[1]
    slot = lax.broadcasted_iota(jnp.int32, (TILE, slots), 1).astype(F32)
    masks = head_lanes(BF16)
    lanes_all = GROUP * SUB
    key_at = lax.broadcasted_iota(jnp.int32, (WINDOW, lanes_all), 0)
    query_at = lax.broadcasted_iota(jnp.int32, (WINDOW, lanes_all), 1) % SUB
    near = (key_at >= query_at) & (key_at <= query_at + LEFT + RIGHT)

    def one_tile(step, carried):
        tile_at = pl.multiple_of(step * TILE, TILE)
        places = (first + tile_at + lax.broadcasted_iota(jnp.int32, (TILE, 1), 0)).astype(F32)
        seg = jnp.sum((ends_row[...] <= places).astype(F32), axis=1, keepdims=True)
        weight[pl.ds(tile_at, TILE), :] = jnp.broadcast_to(
            jnp.sum(jnp.where(seg == slot, slot_weight, 0.0), axis=1, keepdims=True),
            (TILE, weight.shape[1]),
        )
        allowed, scores, pieces = [], [], []
        for sub in range(TILE // SUB):
            at = first + tile_at + sub * SUB
            ours = (at + lax.broadcasted_iota(jnp.int32, (1, lanes_all), 1) % SUB).astype(F32)
            others = (at - LEFT + lax.broadcasted_iota(jnp.int32, (WINDOW, 1), 0)).astype(F32)
            seg_ours = jnp.sum((ends_column[...] <= ours).astype(F32), axis=0, keepdims=True)
            seg_others = jnp.sum((ends_row[...] <= others).astype(F32), axis=1, keepdims=True)
            seg_others = jnp.where(others < 0.0, -1.0, seg_others)
            seg_others = jnp.where(others >= float(stream_len), -2.0, seg_others)
            allowed.append(near & (seg_ours == seg_others))
            for group in range(2):
                pieces.append((sub, group))
        for sub, group in pieces:
            start = pl.multiple_of(tile_at + sub * SUB, SUB)
            lanes = slice(group * half, (group + 1) * half)
            queries = stacked(q[pl.ds(start, SUB), lanes], masks)
            scores.append(against(keys[pl.ds(start, WINDOW), lanes], queries))
        lows = []
        for (sub, group), score in zip(pieces, scores):
            score = jnp.where(allowed[sub], score, -1e30)
            grown = jnp.exp(score - jnp.max(score, axis=0, keepdims=True))
            low = (grown * (1.0 / jnp.sum(grown, axis=0, keepdims=True))).astype(BF16)
            probs[2 * (step * (TILE // SUB) + sub) + group] = low
            lows.append(low)
        for (sub, group), low in zip(pieces, lows):
            start = pl.multiple_of(tile_at + sub * SUB, SUB)
            lanes = slice(group * half, (group + 1) * half)
            heads = unstacked(over_rows(low, values[pl.ds(start, WINDOW), lanes]))
            mixed[pl.ds(start, SUB), lanes] = heads.astype(BF16)
        return carried

    lax.fori_loop(0, count // TILE, one_tile, 0)
    carry_out(probs, probs_out)
    for load in loads[:3]:
        load.wait()
    bias = jnp.zeros((1, width), F32)
    for rows in tiles(count):
        summed = x[rows, :].astype(F32) + dot(mixed[rows, :], wmix[...]) + bmix[...]
        resid[rows, :] = summed
        unit, _ = norm_parts(summed)
        nffn[rows, :] = (unit * fgain[...] + fshift[...]).astype(BF16)
        scaled = scaled_rows(out_grad[rows, :], weight[rows, :]).astype(BF16)
        branch[rows, :] = scaled
        bias = bias + row_sum(scaled.astype(F32))
    gdb_out[...] = bias
    carry_out(resid, resid_out)

    def one_block(block, carried):
        at = pl.multiple_of(block * width, width)
        lanes = pl.ds(at, width)
        for rows in tiles(count):
            hidden = dot(nffn[rows, :], wup[:, lanes]) + bup[:, lanes]
            below = 1.0 + lax.erf(hidden * math.sqrt(0.5))
            bell = jnp.exp2(
                hidden * hidden * (-0.5 * LOG2E) + math.log2(2.0 / math.sqrt(2.0 * math.pi))
            )
            active[rows, lanes] = ((hidden * 0.5) * below).astype(BF16)
            slope[rows, :] = (below + hidden * bell).astype(BF16)
        pltpu.make_async_copy(
            active.at[:, lanes], active_out.at[:, lanes], block_sems.at[block]
        ).start()
        keep_d_out[:, lanes], send_d_out[:, lanes] = halves(
            over_rows(active[:, lanes], branch[...]), core
        )
        bias = jnp.zeros((1, width), F32)
        for rows in tiles(count):
            half_branch = branch[rows, :] * jnp.asarray(0.5, BF16)
            grad = against(half_branch, wdown[lanes, :]) * slope[rows, :].astype(F32)
            low = grad.astype(BF16)
            gh[rows, lanes] = low
            bias = bias + row_sum(low.astype(F32))
        gub_out[:, lanes] = bias
        keep_u_out[:, lanes], send_u_out[:, lanes] = halves(
            over_rows(nffn[...], gh[:, lanes]), core
        )
        return carried

    for load in loads[3:]:
        load.wait()
    lax.fori_loop(0, ffw // width, one_block, 0)
    by_bias, by_gain, by_shift = (jnp.zeros((1, width), F32) for _ in range(3))
    for rows in tiles(count):
        grad = against(gh[rows, :], wup[...])
        unit, inverse = norm_parts(resid[rows, :])
        by_gain = by_gain + row_sum(grad * unit)
        by_shift = by_shift + row_sum(grad)
        grad_resid = scaled_rows(out_grad[rows, :], weight[rows, :]) + norm_back(
            grad * fgain[...], unit, inverse
        )
        gr[rows, :] = grad_resid
        low = grad_resid.astype(BF16)
        branch[rows, :] = low
        by_bias = by_bias + row_sum(low.astype(F32))
        gm[rows, :] = against(low, wmix[...]).astype(BF16)
    carry_out(gr, gr_out)
    carry_out(gm, gm_out)
    there = slice(ffw, ffw + width)
    keep_u_out[:, there], send_u_out[:, there] = halves(over_rows(mixed[...], branch[...]), core)
    gmb_out[...] = by_bias
    gfg_out[...] = by_gain
    gfs_out[...] = by_shift
    for block in range(ffw // width):
        lanes = slice(block * width, (block + 1) * width)
        copies.append(
            pltpu.make_async_copy(
                active.at[:, lanes], active_out.at[:, lanes], block_sems.at[block]
            )
        )
    for copy in copies:
        copy.wait()


def output_body(bdown, wdown_in, resid_in, active_in, out, wdown, resid, active, low, sems):
    steps = tiles(resid.shape[0])

    def moved(source, target, place):
        return pltpu.make_async_copy(source, target, sems.at[place])

    loads = [moved(wdown_in, wdown, 0)]
    for i, rows in enumerate(steps):
        loads.append(moved(active_in.at[rows, :], active.at[rows, :], 1 + 2 * i))
        loads.append(moved(resid_in.at[rows, :], resid.at[rows, :], 2 + 2 * i))
    for load in loads:
        load.start()
    loads[0].wait()
    stores = []
    for i, rows in enumerate(steps):
        loads[1 + 2 * i].wait()
        loads[2 + 2 * i].wait()
        low[rows, :] = (
            resid[rows, :] + dot(active[rows, :], wdown[...]) + bdown[...]
        ).astype(BF16)
        stores.append(moved(low.at[rows, :], out.at[rows, :], 1 + 2 * len(steps) + i))
        stores[-1].start()
    for store in stores:
        store.wait()


def attend_back_body(
    gm_in,
    values_in,
    probs_in,
    keys_in,
    q_in,
    x_in,
    unit,
    gq,
    gk,
    gv,
    edge,
    gq_out,
    gk_out,
    gv_out,
    gm,
    values,
    probs,
    keys,
    q,
    x,
    gk_window,
    gv_window,
    sems,
    load_sems,
):
    count, width = q.shape
    half = width // 2
    steps = count // TILE
    spill = keys.shape[0] - count
    blocks = probs.shape[0] // steps

    def loads(step):
        def load(place, source, target, start, size):
            part = pl.ds(start, size)
            return pltpu.make_async_copy(
                source.at[part], target.at[part], load_sems.at[place, step]
            )

        start = step * TILE
        first = start if isinstance(step, int) else pl.multiple_of(start + spill, spill)
        size = TILE + spill if isinstance(step, int) else TILE
        return [
            load(0, gm_in, gm, start, TILE),
            load(1, values_in, values, first, size),
            load(2, probs_in, probs, step * blocks, blocks),
            load(3, keys_in, keys, first, size),
            load(4, q_in, q, start, TILE),
            load(5, x_in, x, start, TILE),
        ]

    def begin(step, carried):
        for load in loads(step):
            load.start()
        return carried

    for load in loads(0):
        load.start()
    lax.fori_loop(1, steps, begin, 0)
    gk_window[...] = jnp.zeros_like(gk_window)
    gv_window[...] = jnp.zeros_like(gv_window)
    scale = (width // HEADS) ** (-0.5)
    masks = head_lanes(BF16)
    pieces = [(sub, group) for sub in range(TILE // SUB) for group in range(2)]

    def one_tile(step, carried):
        tile_at = pl.multiple_of(step * TILE, TILE)

        @pl.when(step == 0)
        def _():
            for load in loads(0):
                load.wait()

        @pl.when(step > 0)
        def _():
            for load in loads(step):
                load.wait()

        def spot(sub, group):
            start = pl.multiple_of(tile_at + sub * SUB, SUB)
            return pl.ds(start, SUB), pl.ds(start, WINDOW), slice(group * half, (group + 1) * half)

        tile_rows = pl.ds(tile_at, TILE)
        unit[tile_rows, :] = norm_parts(x[tile_rows, :].astype(F32))[0].astype(BF16)
        pulls, grads = [], []
        for sub, group in pieces:
            rows, window, lanes = spot(sub, group)
            pulled = stacked(gm[rows, lanes], masks)
            pulls.append(pulled)
            grads.append(against(values[window, lanes], pulled))
        lows = []
        for (sub, group), grad in zip(pieces, grads):
            wide = probs[2 * (step * (TILE // SUB) + sub) + group].astype(F32)
            product = wide * grad
            lows.append((product - wide * jnp.sum(product, axis=0, keepdims=True)).astype(BF16))
        for (sub, group), pulled, low in zip(pieces, pulls, lows):
            rows, window, lanes = spot(sub, group)
            queries = stacked(q[rows, lanes], masks)
            gq[rows, lanes] = (unstacked(over_rows(low, keys[window, lanes])) * scale).astype(BF16)
            gk_window[window, lanes] += dot(low, queries)
            gv_window[window, lanes] += dot(
                probs[2 * (step * (TILE // SUB) + sub) + group], pulled
            )
        return carried

    lax.fori_loop(0, count // TILE, one_tile, 0, unroll=2)
    stores = []

    def store(source, target):
        stores.append(pltpu.make_async_copy(source, target, sems.at[len(stores)]))
        stores[-1].start()

    store(gq, gq_out)
    for place, (window, grad, out) in enumerate(
        ((gk_window, gk, gk_out), (gv_window, gv, gv_out))
    ):
        lanes = slice(place * width, (place + 1) * width)
        grad[...] = window[LEFT : LEFT + count].astype(BF16)
        store(grad, out)
        edge[:LEFT, lanes] = window[:LEFT].astype(BF16)
        edge[LEFT : LEFT + RIGHT, lanes] = window[LEFT + count : LEFT + count + RIGHT].astype(BF16)
    for one in stores:
        one.wait()


def edge_frames(core, near_rows, far_rows):
    before, behind = neighbours(core, near_rows, far_rows)
    return jnp.concatenate([before[EDGE - LEFT :], behind[:RIGHT]], axis=0).astype(F32)


def weights_body(
    where,
    unit,
    gq,
    gk,
    gv,
    edge,
    near_rows,
    far_rows,
    gain,
    shift,
    gdb,
    gub,
    gmb,
    gfg,
    gfs,
    wq_in,
    wk_in,
    wv_in,
    keep_out,
    send_out,
    wq,
    wk,
    wv,
    sums,
    vec,
    sems,
):
    width = unit.shape[1]
    core = where[1]
    loads = []
    for source, target in ((wq_in, wq), (wk_in, wk), (wv_in, wv)):
        loads.append(pltpu.make_async_copy(source, target, sems.at[len(loads)]))
        loads[-1].start()
    far_low = norm_parts(edge_frames(core, near_rows, far_rows))[0].astype(BF16)
    gain_column = jnp.transpose(jnp.broadcast_to(gain[...], (128, width)))[:, :1]
    shift_column = jnp.transpose(jnp.broadcast_to(shift[...], (128, width)))[:, :1]
    columns = [row_sum(grad[...].astype(F32)) for grad in (gq, gk, gv)]
    by_gain = jnp.zeros((width, 1), F32)
    by_shift = jnp.zeros((width, 1), F32)
    for place, (grad, weight) in enumerate(((gq, wq), (gk, wk), (gv, wv))):
        product = over_rows(unit[...], grad[...])
        column = columns[place]
        if place > 0:
            there = slice((place - 1) * width, place * width)
            product = product + over_rows(far_low, edge[: LEFT + RIGHT, there])
            column = column + row_sum(edge[: LEFT + RIGHT, there].astype(F32))
        lanes = slice(place * width, (place + 1) * width)
        keep_out[:, lanes], send_out[:, lanes] = halves(
            product * gain_column + shift_column * column, core
        )
        loads[place].wait()
        wide = weight[...].astype(F32)
        by_gain = by_gain + jnp.sum(wide * product, axis=1, keepdims=True)
        by_shift = by_shift + jnp.sum(wide * column, axis=1, keepdims=True)
        if place != 1:
            sums[place // 2 : place // 2 + 1] = column
    sums[2:3] = jnp.transpose(jnp.broadcast_to(by_gain, (width, 128)))[:1]
    sums[3:4] = jnp.transpose(jnp.broadcast_to(by_shift, (width, 128)))[:1]
    vec[...] = jnp.zeros_like(vec)
    row = 0
    for ref in [sums.at[i : i + 1] for i in range(4)] + [gmb, gfg, gfs, gdb, gub]:
        for part in range(0, ref.shape[1], 128):
            vec[row : row + 1] = ref[:, part : part + 128]
            row += 1
    keep_out[:, 3 * width :], send_out[:, 3 * width :] = halves(vec[...], core)


def input_body(
    where,
    x,
    gq,
    gk,
    gv,
    gr,
    edge,
    near_rows,
    far_rows,
    gain,
    wq,
    wk,
    wv,
    own_edge_out,
    near_edge_out,
    far_edge_out,
    ig_out,
    ig,
    sems,
):
    count, width = x.shape
    core = where[1]
    unit, inverse = norm_parts(edge_frames(core, near_rows, far_rows))
    cut = slice(0, LEFT + RIGHT)
    grad = against(edge[cut, :width], wk[...]) + against(edge[cut, width:], wv[...])
    grad = norm_back(grad * gain[...], unit, inverse)
    before = jnp.concatenate([jnp.zeros((EDGE - LEFT, width), F32), grad[:LEFT]], axis=0)
    behind = jnp.concatenate([grad[LEFT:], jnp.zeros((EDGE - RIGHT, width), F32)], axis=0)
    near_edge_out[...] = jnp.where(core == 0, behind, before)
    far_edge_out[...] = jnp.where(core == 0, before, behind)
    stores = []
    for rows in tiles(count):
        unit, inverse = norm_parts(x[rows, :].astype(F32))
        grad = (
            against(gq[rows, :], wq[...])
            + against(gk[rows, :], wk[...])
            + against(gv[rows, :], wv[...])
        )
        result = gr[rows, :] + norm_back(grad * gain[...], unit, inverse)
        ig[rows, :] = result.astype(BF16)
        stores.append(
            pltpu.make_async_copy(
                ig.at[rows, :], ig_out.at[rows, :], sems.at[len(stores)]
            )
        )
        stores[-1].start()
        if rows.start == 0:
            own_edge_out[:EDGE] = result[:EDGE]
        if rows.stop == count:
            own_edge_out[EDGE:] = result[-EDGE:]
    for store in stores:
        store.wait()


def swapped(value, axis, mask):
    count = lax.axis_size(axis)
    return lax.ppermute(value, axis, [(i, i ^ mask) for i in range(count)])


def across(value, first):
    tm, items = lax.axis_size("tm"), lax.axis_size("items")
    pairs = []
    for i in range(tm):
        for j in range(items):
            along_x = (i % 2 == 0) == first
            pairs.append((i * items + j, i * items + (j ^ 1) if along_x else (i ^ 2) * items + j))
    return lax.ppermute(value, ("tm", "items"), pairs)


def cut(value, place, rows):
    return lax.dynamic_slice_in_dim(value, place * rows, rows, 0)


def total_of(parts):
    total = parts[0].astype(F32)
    for part in parts[1:]:
        total = total + part.astype(F32)
    return total.astype(BF16)


def paired(own, got, bit):
    return jnp.where(bit == 0, jnp.concatenate([own, got]), jnp.concatenate([got, own]))


def whole_body(places, where, own, got, *outs):
    blocks, (lane, first) = places
    rows = own.shape[0]
    for place, part in ((where[1], own), (1 - where[1], got)):
        for out, start, row in blocks:
            width = outs[out].shape[1]
            outs[out][pl.ds(pl.multiple_of(row + place * rows, rows), rows), :] = part[
                :, start : start + width
            ].astype(F32)
    if first < len(outs):
        count = sum(out.shape[1] for out in outs[first:]) // 128
        low = jnp.where(where[1] == 0, own[:count, lane:], got[:count, lane:]).astype(F32)
        row = 0
        for out in outs[first:]:
            for at in range(0, out.shape[1], 128):
                out[:, at : at + 128] = low[row : row + 1]
                row += 1


class Place:
    def __init__(self):
        tm = lax.axis_index("tm").astype(jnp.int32)
        x_bit = lax.axis_index("items").astype(jnp.int32) % 2
        y_bit = (tm // 2) % 2
        self.core = tm % 2
        self.steps = [
            (jnp.where(self.core == 0, x_bit, y_bit), lambda value: across(value, True)),
            (jnp.where(self.core == 0, y_bit, x_bit), lambda value: across(value, False)),
            ((tm // 4) % 2, lambda value: swapped(value, "tm", 4)),
            ((tm // 8) % 2, lambda value: swapped(value, "tm", 8)),
        ]


def fold_body(step, where, keep, got, mine_out, other_out):
    rows = keep.shape[0] // 2
    bit = where[2 + step]
    for place, out in ((bit, mine_out), (1 - bit, other_out)):
        at = pl.ds(pl.multiple_of(place * rows, rows), rows)
        out[...] = total_of([keep[at, :], got[at, :]])


class Sum:
    def __init__(self, place, halved, folds, keep, send):
        self.place = place
        self.folds = folds
        self.parts = [keep, swapped(send, "tm", 1)]
        self.todo = [functools.partial(self.exchange, step, step < halved) for step in range(4)]
        self.todo += [functools.partial(self.spread, step) for step in range(halved - 1, -1, -1)]
        self.todo += [functools.partial(self.spread, -1)]
        self.bit = None

    def held(self):
        return self.parts[0]

    def hold(self, value):
        self.parts[0] = value

    def advance(self):
        self.todo.pop(0)()

    def exchange(self, step, halve):
        bit, exchange = self.place.steps[step]
        if halve and step < self.folds:
            rows, width = self.parts[0].shape
            mine, other = call(
                functools.partial(fold_body, step),
                "fold",
                self.parts,
                [near(rows // 2, width, BF16)] * 2,
                scalars=[self.place.where],
                vmem=8,
                moved=4 * MIB,
            )
        elif halve:
            rows = self.parts[0].shape[0] // 2
            mine, other = (
                total_of([cut(part, at, rows) for part in self.parts]) for at in (bit, 1 - bit)
            )
        else:
            mine = other = total_of(self.parts)
        self.parts = [mine, exchange(other)]

    def spread(self, step):
        own = total_of(self.parts) if self.bit is None else paired(*self.parts, self.bit)
        if step >= 0:
            self.bit, exchange = self.place.steps[step]
            self.parts = [own, exchange(own)]
        else:
            self.parts = [own, swapped(own, "tm", 1)]

    def whole(self, where, places, outs):
        return call(
            functools.partial(whole_body, places),
            "whole",
            self.parts,
            outs,
            scalars=[where],
            vmem=24,
            moved=6 * MIB,
        )


class PlainSum:
    def __init__(self, place, halved, folds, keep, send):
        self.place = place
        self.todo = []
        self.parts = [keep, send]

    def held(self):
        return self.parts[0]

    def hold(self, value):
        self.parts[0] = value

    def advance(self):
        pass

    def whole(self, where, places, outs):
        keep, send = self.parts
        low = jnp.where(self.place.core == 0, keep, send)
        high = jnp.where(self.place.core == 0, send, keep)
        total = lax.psum(jnp.concatenate([low, high], axis=0), ("tm", "items"))
        blocks, vectors = places
        made = [[] for _, _ in outs]
        for out, lane, _ in blocks:
            made[out].append(total[:, lane : lane + outs[out][0].shape[1]])
        lane, first = vectors
        for out in range(first, len(outs)):
            size = outs[out][0].shape[1]
            start = sum(made_out[0].shape[1] // 128 for _, made_out in enumerate(made[first:out]))
            rows = total[start : start + size // 128, lane : lane + 128]
            made[out].append(rows.reshape(1, size))
        return [jnp.concatenate(parts, axis=0).astype(F32) for parts in made]


def stays(array):
    return pltpu.with_memory_space_constraint(array, pltpu.HBM)


def here(array):
    return pltpu.with_memory_space_constraint(array, pltpu.VMEM)


def ordered(first, second):
    return lax.optimization_barrier((first, second))[1]


def follow(first, second):
    second.hold(ordered(first.held(), second.held()))


def along(value):
    count = lax.axis_size("tm")
    pairs = [(i, i + 1) for i in range(1, count - 1, 2)]
    return lax.ppermute(value, "tm", pairs + [(to, of) for of, to in pairs])


def local(
    fast,
    frames,
    out_grad,
    item_lengths,
    domain_tags,
    domain_weight,
    wq,
    bq,
    wk,
    wv,
    bv,
    wmix,
    bmix,
    again,
    ashift,
    fgain,
    fshift,
    wup,
    bup,
    wdown,
    bdown,
):
    frames = frames[0]
    out_grad = out_grad[0]
    count, width = frames.shape
    ffw = wup.shape[1]
    slots = item_lengths.shape[1]
    stream_len = count * lax.axis_size("tm")
    reach = count + WINDOW - SUB
    unit_flops = 2 * count * width * width
    parts = ffw // width
    bq, bv, bmix, again, ashift, fgain, fshift, bup, bdown = (
        vector[None] for vector in (bq, bv, bmix, again, ashift, fgain, fshift, bup, bdown)
    )
    place = Place()
    bits = [bit for bit, _ in place.steps]
    where = jnp.stack([lax.axis_index("tm") * count, place.core] + bits).astype(jnp.int32)
    place.where = where
    near_end = jnp.where(place.core == 0, count - EDGE, 0)
    near_rows = swapped(lax.dynamic_slice_in_dim(frames, near_end, EDGE, 0), "tm", 1)
    far_rows = along(lax.dynamic_slice_in_dim(frames, count - EDGE - near_end, EDGE, 0))
    kind = Sum if fast else PlainSum
    vector = free(1, width, F32)
    edge_wide = free(2 * EDGE, width, F32)
    edge_half = free(EDGE, width, F32)
    model_low = (count, width, BF16)
    model_wide = (count, width, F32)
    hidden_low = (count, ffw, BF16)
    blocks = (2 * count // SUB, WINDOW, GROUP * SUB, BF16)
    windowed = (reach, width)
    low_scratch = pltpu.VMEM((count, width), BF16)

    q, k, v = call(
        project_body,
        "project",
        [stays(a) for a in (frames, again, ashift, wq, wk, wv, bq, bv)],
        [near(*model_low)] * 3,
        flops=3 * unit_flops,
        moved=6 * MIB,
    )
    (
        probs,
        q,
        keys,
        values,
        active,
        resid,
        gr,
        gm,
        keep_d,
        send_d,
        keep_u,
        send_u,
        gdb,
        gub,
        gmb,
        gfg,
        gfs,
    ) = call(
        functools.partial(forward_body, stream_len),
        "forward",
        [q, k, v, near_rows, far_rows]
        + [stays(a) for a in (item_lengths, domain_tags, again, ashift, wk, wv)]
        + [stays(a) for a in (bv, bmix, fgain, fshift, bup)],
        [copied(*blocks), copied(*model_low), copied(*windowed, BF16), copied(*windowed, BF16)]
        + [copied(*hidden_low), copied(*model_wide), copied(*model_wide), copied(*model_low)]
        + [near(width // 2, ffw, BF16)] * 2
        + [near(width // 2, ffw + width, BF16)] * 2
        + [vector, free(1, ffw, F32), vector, vector, vector],
        scratch=[
            pltpu.VMEM(windowed, BF16),
            pltpu.VMEM(windowed, BF16),
            pltpu.VMEM((1, slots), F32),
            pltpu.VMEM((slots, 1), F32),
            pltpu.VMEM(blocks[:-1], BF16),
            pltpu.VMEM((count, width), BF16),
            pltpu.VMEM((count, width), F32),
            pltpu.VMEM((count, 128), F32),
            pltpu.VMEM((count, width), BF16),
            pltpu.VMEM((count, width), BF16),
            pltpu.VMEM((count, ffw), BF16),
            pltpu.VMEM((count, width), BF16),
            pltpu.VMEM((count, ffw), BF16),
            pltpu.VMEM((count, width), F32),
            pltpu.VMEM((count, width), BF16),
            pltpu.VMEM((count, width), BF16),
            pltpu.VMEM((width, width), BF16),
            pltpu.VMEM((count, width), BF16),
            pltpu.VMEM((width, ffw), BF16),
            pltpu.VMEM((ffw, width), BF16),
            pltpu.SemaphoreType.DMA((7,)),
            pltpu.SemaphoreType.DMA((parts,)),
            pltpu.SemaphoreType.DMA((5,)),
        ],
        scalars=[where, domain_weight],
        far_ins=[stays(a) for a in (frames, wmix, out_grad, wup, wdown)],
        vmem=36,
        flops=(6 + 5 * parts) * unit_flops,
        moved=24 * MIB,
    )
    down = kind(place, 3, 2, keep_d, send_d)
    up = kind(place, 3, 1, keep_u, send_u)

    down.advance()
    follow(down, up)
    up.advance()
    gm = ordered(up.held(), gm)
    (unit, gq, gk, gv, edge, gq_far, gk_far, gv_far) = call(
        attend_back_body,
        "attend_back",
        [],
        [near(*model_low)] * 4
        + [near(EDGE, 2 * width, BF16)]
        + [copied(*model_low)] * 3,
        scratch=[
            low_scratch,
            pltpu.VMEM(windowed, BF16),
            pltpu.VMEM(blocks[:-1], BF16),
            pltpu.VMEM(windowed, BF16),
            low_scratch,
            low_scratch,
            pltpu.VMEM(windowed, F32),
            pltpu.VMEM(windowed, F32),
            pltpu.SemaphoreType.DMA((3,)),
            pltpu.SemaphoreType.DMA((6, count // TILE)),
        ],
        far_ins=[stays(a) for a in (gm, values, probs, keys, q, frames)],
        vmem=20,
        flops=8 * unit_flops,
        moved=10 * MIB,
    )
    down.hold(ordered(edge, down.held()))
    down.advance()
    edge = ordered(down.held(), edge)
    rest_half = near(width // 2, 3 * width + 128, BF16)
    square_low = pltpu.VMEM((width, width), BF16)
    keep_r, send_r = call(
        weights_body,
        "weights",
        [unit, gq, gk, gv, edge, near_rows, far_rows]
        + [stays(a) for a in (again, ashift)]
        + [gdb, gub, gmb, gfg, gfs],
        [rest_half, rest_half],
        scratch=[square_low] * 3
        + [pltpu.VMEM((8, width), F32), pltpu.VMEM((width, 128), F32)]
        + [pltpu.SemaphoreType.DMA((3,))],
        scalars=[where],
        far_ins=[stays(a) for a in (wq, wk, wv)],
        vmem=16,
        flops=3 * unit_flops,
        moved=8 * MIB,
    )
    rest = kind(place, 2, 0, keep_r, send_r)
    sums = {"d": down, "u": up, "r": rest}
    latest = keep_r
    for turn in ORDER:
        if turn == "o":
            active = ordered(latest, active)
            (output,) = call(
                output_body,
                "output",
                [stays(bdown)],
                [copied(*model_low)],
                scratch=[
                    pltpu.VMEM((ffw, width), BF16),
                    pltpu.VMEM((count, width), F32),
                    pltpu.VMEM((count, ffw), BF16),
                    pltpu.VMEM((count, width), BF16),
                    pltpu.SemaphoreType.DMA((1 + 3 * (count // TILE),)),
                ],
                far_ins=[stays(a) for a in (wdown, resid, active)],
                vmem=20,
                flops=parts * unit_flops,
                moved=9 * MIB,
            )
            latest = output
        elif turn == "n":
            gr = ordered(latest, gr)
            own_edge, near_edge, far_edge, ig = call(
                input_body,
                "input",
                [stays(a) for a in (frames, gq_far, gk_far, gv_far, gr)]
                + [edge, near_rows, far_rows]
                + [stays(a) for a in (again, wq, wk, wv)],
                [edge_wide, edge_half, edge_half, copied(*model_low)],
                scratch=[
                    pltpu.VMEM((count, width), BF16),
                    pltpu.SemaphoreType.DMA((count // TILE,)),
                ],
                scalars=[where],
                vmem=24,
                flops=3 * unit_flops,
                moved=8 * MIB,
            )
            latest = far_edge
        elif turn == "e":
            far_edge = ordered(latest, far_edge)
            near_got = swapped(near_edge, "tm", 1)
            far_got = along(far_edge)
        elif turn == "i":
            far_got = ordered(latest, far_got)
            low = place.core == 0
            first = (own_edge[:EDGE] + jnp.where(low, far_got, near_got)).astype(BF16)
            last = (own_edge[EDGE:] + jnp.where(low, near_got, far_got)).astype(BF16)
            latest = (first, last)
        else:
            one = sums[turn]
            one.hold(ordered(latest, one.held()))
            if one.todo:
                one.advance()
                latest = one.held()
            elif one is down:
                places = [(0, at, at) for at in range(0, ffw, width)], (0, 1)
                (grad_down,) = one.whole(where, places, [free(ffw, width, F32)])
                latest = grad_down
            elif one is up:
                places = [(0, 0, 0), (1, ffw, 0)], (0, 2)
                outs = [free(width, ffw, F32), free(width, width, F32)]
                grad_up, grad_mix = one.whole(where, places, outs)
                latest = grad_mix
    ig = ig.at[:EDGE].set(first)
    ig = ig.at[count - EDGE :].set(last)
    places = [(i, i * width, 0) for i in range(3)], (3 * width, 3)
    outs = [free(width, width, F32)] * 3 + [vector] * 8 + [free(1, ffw, F32)]
    grad_q, grad_k, grad_v, *vectors = rest.whole(where, places, outs)
    gqb, gvb, gag, gas, gmb, gfg, gfs, gdb, gub = (made[0] for made in vectors)
    return (
        output[None],
        ig[None],
        grad_q,
        gqb,
        grad_k,
        grad_v,
        gvb,
        grad_mix,
        gmb,
        gag,
        gas,
        gfg,
        gfs,
        grad_up,
        gub,
        grad_down,
        gdb,
    )


def solution(mesh):
    rows = P("items", "tm", None)
    in_specs = (rows, rows, P("items", None), P("items", None)) + (P(),) * 16
    out_specs = (rows, rows) + (P(),) * 15
    fast = mesh.shape["tm"] == 16 and mesh.shape["items"] == 2
    return jax.shard_map(
        functools.partial(local, fast),
        mesh=mesh,
        in_specs=in_specs,
        out_specs=out_specs,
        check_vma=False,
    )
```
